128 devices in a mesh: dp: 16 (over x, y_hi, core), context: 8 (over z, y_lo).
Axes of the slice: x: 4, y: 4 (y_hi: 2, y_lo: 2; y = y_hi * 2 + y_lo), z: 4, core: 2. Of those that a mesh axis runs over, the one named last changes fastest.
Arguments:
- image_tokens: bfloat16 [16, 896, 3072], P('dp', 'context'), may hold values from -6 to 6
- text_tokens: bfloat16 [16, 128, 3072], P('dp', 'context'), may hold values from -6 to 6
- image_mod: bfloat16 [16, 3, 3072], P('dp'), may hold values from -4 to 4
- text_mod: bfloat16 [16, 3, 3072], P('dp'), may hold values from -4 to 4
- image_qkv_weight: bfloat16 [3072, 3, 16, 128], P('dp', None, 'context'), may hold values from -0.109375 to 0.109375
- text_qkv_weight: bfloat16 [3072, 3, 16, 128], P('dp', None, 'context'), may hold values from -0.109375 to 0.109375
- image_out_weight: bfloat16 [3072, 16, 128], P('dp', 'context'), may hold values from -1 to 1
- text_out_weight: bfloat16 [3072, 16, 128], P('dp', 'context'), may hold values from -1 to 1
- image_slope: bfloat16 [16, 896, 3072], P('dp', 'context'), may hold values from -0.119628906 to 0.119628906
- text_slope: bfloat16 [16, 128, 3072], P('dp', 'context'), may hold values from -0.119628906 to 0.119628906
Outputs:
- image_update: bfloat16 [16, 896, 3072], P('dp', 'context')
- text_update: bfloat16 [16, 128, 3072], P('dp', 'context')
- image_qkv_grad: float32 [3072, 3, 16, 128], P('dp', None, 'context')
- text_qkv_grad: float32 [3072, 3, 16, 128], P('dp', None, 'context')
- image_out_grad: float32 [3072, 16, 128], P('dp', 'context')
- text_out_grad: float32 [3072, 16, 128], P('dp', 'context')
- image_mod_grad: float32 [16, 3, 3072], P('dp')
- text_mod_grad: float32 [16, 3, 3072], P('dp')
The draws below stay inside these ranges and needn't reach their ends.
All inputs are finite; a program needn't handle non-finite values.
Results may differ from the reference program's by a relative error of at most 0.015.
Values may be sent and summed in bfloat16 or wider, within the bound.
A program may use at most 128 MiB of HBM per device.

```python
import jax
import jax.numpy as jnp
from jax import lax

D = 3072
H = 16
HD = 128
IMG = 896
TXT = 128
SEQ = 1024
IMAGES = 16
N_CONTEXT = 8


def block_levels(own_key, dims, split, least, high):
    gain = 1.0
    for axis_at, blocks in split:
        draws = jax.random.uniform(jax.random.fold_in(jax.random.fold_in(own_key, 6), axis_at), (blocks,), jnp.float32, least / len(split), high / len(split))
        gain = gain * jnp.repeat(jnp.exp(draws), dims[axis_at] // blocks).reshape((-1,) + (1,) * (len(dims) - 1 - axis_at))
    return gain


def bell_draw(rng, shape, width, reach, cuts=(), dtype=jnp.bfloat16):
    level = block_levels(rng, shape, cuts, -0.22, 0.18) if cuts else 1.0
    values = jax.random.normal(rng, shape, jnp.float32) * width * level
    return jnp.minimum(jnp.maximum(values, -reach), reach).astype(dtype)


def setup_inputs(seed: int = 0) -> dict:
    key_list = jax.random.split(jax.random.key(seed), 11)
    return {
        "image_tokens": bell_draw(key_list[0], (IMAGES, IMG, D), 1.0, 6.0, ((0, 16), (1, 8))),
        "text_tokens": bell_draw(key_list[1], (IMAGES, TXT, D), 1.0, 6.0, ((0, 16), (1, 8))),
        "image_mod": bell_draw(key_list[2], (IMAGES, 3, D), 0.8, 4.0, ((0, 16),)),
        "text_mod": bell_draw(key_list[3], (IMAGES, 3, D), 0.8, 4.0, ((0, 16),)),
        "image_qkv_weight": bell_draw(key_list[4], (D, 3, H, HD), D ** -0.5, 0.109375, ((0, 16), (2, 8))),
        "text_qkv_weight": bell_draw(key_list[5], (D, 3, H, HD), D ** -0.5, 0.109375, ((0, 16), (2, 8))),
        "image_out_weight": bell_draw(key_list[6], (D, H, HD), (HD // 4) ** -0.5, 1.0, ((0, 16), (1, 8))),
        "text_out_weight": bell_draw(key_list[7], (D, H, HD), (HD // 4) ** -0.5, 1.0, ((0, 16), (1, 8))),
        "image_slope": bell_draw(key_list[8], (IMAGES, IMG, D), 0.02, 0.119628906, ((0, 16), (1, 8))),
        "text_slope": bell_draw(key_list[9], (IMAGES, TXT, D), 0.02, 0.119628906, ((0, 16), (1, 8))),
    }


norm_eps = 1e-06

def layer_normal(values):
    average = lax.optimization_barrier(jnp.mean(values, axis=-1, keepdims=True))
    centred = values - average
    return centred * lax.rsqrt(lax.optimization_barrier(jnp.mean(centred * centred, axis=-1, keepdims=True)) + norm_eps)

def rms_normal(values):
    factor = lax.rsqrt(lax.optimization_barrier(jnp.mean(values * values, axis=-1, keepdims=True)) + norm_eps)
    return (values * factor, factor)

def rms_back(normed, factor, slopes):
    return factor * (slopes - normed * lax.optimization_barrier(jnp.mean(slopes * normed, axis=-1, keepdims=True)))

def to_bf(values):
    return lax.optimization_barrier(values.astype(jnp.bfloat16))

def modulate(tokens, modulation):
    normal = layer_normal(tokens.astype(jnp.float32))
    factors = modulation.astype(jnp.float32)
    return (normal, ((1.0 + factors[1]) * normal + factors[0]).astype(jnp.bfloat16))

def grouped_sum(attended_rows, out_flat):
    row_total = attended_rows.shape[0]
    group_width = H // N_CONTEXT * HD
    left_side = attended_rows.astype(jnp.float32).reshape(row_total, N_CONTEXT, group_width)
    right_side = out_flat.astype(jnp.float32).reshape(D, N_CONTEXT, group_width)
    partial_value = jnp.einsum('tcx,dcx->ctd', left_side, right_side)
    return lax.optimization_barrier(jnp.sum(to_bf(partial_value).astype(jnp.float32), axis=0))

def reference(image_tokens, text_tokens, image_mod, text_mod, image_qkv_weight, text_qkv_weight, image_out_weight, text_out_weight, image_slope, text_slope):
    triple = 3 * H * HD
    inner_width = H * HD
    score_scale = HD ** (-0.5)
    wq_image = image_qkv_weight.reshape(D, triple)
    wq_text = text_qkv_weight.reshape(D, triple)
    wo_image = image_out_weight.reshape(D, inner_width)
    wo_text = text_out_weight.reshape(D, inner_width)

    def one_image(totals, inputs):
        tokens_image, tokens_text, mod_image, mod_text, slope_image, slope_text = inputs
        normal_image, input_image = modulate(tokens_image, mod_image)
        normal_text, input_text = modulate(tokens_text, mod_text)
        projected = jnp.concatenate([jnp.dot(input_text, wq_text, preferred_element_type=jnp.float32), jnp.dot(input_image, wq_image, preferred_element_type=jnp.float32)], axis=0).reshape(SEQ, 3, H, HD)
        query_normal, query_factor = rms_normal(projected[:, 0])
        key_normal, key_factor = rms_normal(projected[:, 1])
        query_b = to_bf(query_normal).astype(jnp.float32)
        key_b = to_bf(key_normal).astype(jnp.float32)
        value_b = to_bf(projected[:, 2]).astype(jnp.float32)
        scores = jnp.einsum('ihe,jhe->hij', query_b, key_b) * score_scale
        raised = jnp.exp(scores)
        attn_probs = raised / lax.optimization_barrier(jnp.sum(raised, axis=-1, keepdims=True))
        probs_b = to_bf(attn_probs)
        probs_f = probs_b.astype(jnp.float32)
        attended = to_bf(jnp.einsum('hij,jhe->ihe', probs_f, value_b)).reshape(SEQ, inner_width)
        att_text = attended[:TXT]
        att_image = attended[TXT:]
        mixed_text = grouped_sum(att_text, wo_text)
        mixed_image = grouped_sum(att_image, wo_image)
        factors_image = mod_image.astype(jnp.float32)
        factors_text = mod_text.astype(jnp.float32)
        update_image = (factors_image[2] * mixed_image).astype(jnp.bfloat16)
        update_text = (factors_text[2] * mixed_text).astype(jnp.bfloat16)
        slope_image_f = slope_image.astype(jnp.float32)
        slope_text_f = slope_text.astype(jnp.float32)
        gated_image = (factors_image[2] * slope_image_f).astype(jnp.bfloat16)
        gated_text = (factors_text[2] * slope_text_f).astype(jnp.bfloat16)
        back_att = to_bf(jnp.concatenate([jnp.dot(gated_text, wo_text, preferred_element_type=jnp.float32), jnp.dot(gated_image, wo_image, preferred_element_type=jnp.float32)], axis=0))
        back_att_f = back_att.astype(jnp.float32).reshape(SEQ, H, HD)
        back_probs = jnp.einsum('ihe,jhe->hij', back_att_f, value_b)
        back_value = jnp.einsum('hij,ihe->jhe', probs_f, back_att_f)
        back_scores = to_bf(attn_probs * (back_probs - lax.optimization_barrier(jnp.sum(attn_probs * back_probs, axis=-1, keepdims=True))) * score_scale).astype(jnp.float32)
        back_query = jnp.einsum('hij,jhe->ihe', back_scores, key_b)
        back_key = jnp.einsum('hij,ihe->jhe', back_scores, query_b)
        back_qkv = jnp.stack([rms_back(query_normal, query_factor, back_query), rms_back(key_normal, key_factor, back_key), back_value], axis=1).reshape(SEQ, triple).astype(jnp.bfloat16)
        back_text = back_qkv[:TXT]
        back_image = back_qkv[TXT:]
        grad_q_image = to_bf(jnp.dot(input_image.T, back_image, preferred_element_type=jnp.float32)).astype(jnp.float32)
        grad_q_text = to_bf(jnp.dot(input_text.T, back_text, preferred_element_type=jnp.float32)).astype(jnp.float32)
        grad_o_image = to_bf(jnp.dot(gated_image.T, att_image, preferred_element_type=jnp.float32)).astype(jnp.float32)
        grad_o_text = to_bf(jnp.dot(gated_text.T, att_text, preferred_element_type=jnp.float32)).astype(jnp.float32)
        spread_image = jnp.dot(back_image, wq_image.T, preferred_element_type=jnp.float32)
        spread_text = jnp.dot(back_text, wq_text.T, preferred_element_type=jnp.float32)
        modgrad_image = jnp.stack([lax.optimization_barrier(jnp.sum(spread_image, axis=0)), lax.optimization_barrier(jnp.sum(spread_image * normal_image, axis=0)), lax.optimization_barrier(jnp.sum(slope_image_f * mixed_image, axis=0))])
        modgrad_text = jnp.stack([lax.optimization_barrier(jnp.sum(spread_text, axis=0)), lax.optimization_barrier(jnp.sum(spread_text * normal_text, axis=0)), lax.optimization_barrier(jnp.sum(slope_text_f * mixed_text, axis=0))])
        totals = (totals[0] + grad_q_image, totals[1] + grad_q_text, totals[2] + grad_o_image, totals[3] + grad_o_text)
        return (totals, (update_image, update_text, modgrad_image, modgrad_text))
    start_totals = (jnp.zeros((D, triple), jnp.float32), jnp.zeros((D, triple), jnp.float32), jnp.zeros((D, inner_width), jnp.float32), jnp.zeros((D, inner_width), jnp.float32))
    totals, stacked = lax.scan(one_image, start_totals, (image_tokens, text_tokens, image_mod, text_mod, image_slope, text_slope))
    return (stacked[0], stacked[1], totals[0].reshape(D, 3, H, HD), totals[1].reshape(D, 3, H, HD), totals[2].reshape(D, H, HD), totals[3].reshape(D, H, HD), stacked[2], stacked[3])
```

```python
import jax
import jax.numpy as jnp
from jax import lax
from jax.experimental import pallas as pl
from jax.experimental.pallas import tpu as pltpu
from jax.sharding import PartitionSpec as P

EPS = 1e-06
BF = jnp.bfloat16
F32 = jnp.float32
D = 3072
TXT = 128
SEQ = 1024
TB = 16
IB = 112
WR = 192
HALF = 96
SCALE = 128 ** (-0.5)
QI, QT, OI, OT, WC = 0, 768, 1536, 1792, 2048
GROUPS = ((OI, 512), (QI, 768), (QT, 768))


def dot(a, b):
    return jnp.dot(a, b, preferred_element_type=F32)


def dot_last(a, b):
    return lax.dot_general(a, b, (((1,), (1,)), ((), ())), preferred_element_type=F32)


def dot_rows(a, b):
    return lax.dot_general(a, b, (((0,), (0,)), ((), ())), preferred_element_type=F32)


def m16(v):
    return pl.multiple_of(v, 16)


def kernel(
    tok,
    slo,
    wl,
    modr,
    modc,
    upd,
    gout,
    modsum,
    xn,
    g,
    w,
    st,
    pq,
    qb,
    kb,
    vb,
    att,
    batt,
    bq,
    dk,
    dv,
    mland,
    mzl,
    sland,
    so,
    ha,
    hb,
    xl,
    yhl,
    ms,
    ml,
    xs,
    xr,
    gs,
    gr,
    ws,
    wr,
    mys,
    myr,
    mzs,
    mzr,
    ss,
    sr,
    rs,
    rr,
    mss,
    msr,
    loc,
):
    d = lax.axis_index("dp")
    c = lax.axis_index("context")
    core = lax.rem(d, 2)
    yh = lax.rem(d // 2, 2)
    xpos = d // 4
    c_zp, c_zm, c_z2 = lax.rem(c + 2, 8), lax.rem(c + 6, 8), lax.rem(c + 4, 8)
    ylflip = 1 - 2 * lax.rem(c, 2)
    d_xp, d_xm, d_x2 = lax.rem(d + 4, 16), lax.rem(d + 12, 16), lax.rem(d + 8, 16)
    yhflip = 2 - 4 * yh
    zp, zm, z2, yl = (d, c_zp), (d, c_zm), (d, c_z2), (d, c + ylflip)
    xp, xm, yhp, sib = (d_xp, c), (d_xm, c), (d + yhflip, c), (d + 1 - 2 * core, c)

    def rcopy(src, dst, ssem, rsem, dev):
        return pltpu.make_async_remote_copy(
            src_ref=src,
            dst_ref=dst,
            send_sem=ssem,
            recv_sem=rsem,
            device_id=dev,
            device_id_type=pl.DeviceIdType.MESH,
        )

    def trow(cc):
        return pl.ds(m16(cc * TB), TB)

    def irow(cc, off=0, n=IB):
        return pl.ds(m16(TXT + cc * IB + off), n)

    sent = []
    sent_g = []

    def go(cp, kept=sent):
        cp.start()
        kept.append(cp)

    locs = [
        pltpu.make_async_copy(tok.at[pl.ds(0, TB)], xn.at[trow(c)], loc.at[0]),
        pltpu.make_async_copy(tok.at[pl.ds(TB, IB)], xn.at[irow(c)], loc.at[1]),
        pltpu.make_async_copy(slo.at[pl.ds(0, TB)], g.at[trow(c)], loc.at[2]),
        pltpu.make_async_copy(slo.at[pl.ds(TB, IB)], g.at[irow(c)], loc.at[3]),
        pltpu.make_async_copy(wl, w.at[pl.ds(m16(d * WR), WR)], loc.at[4]),
    ]
    for cp in locs:
        cp.start()
    bar = pltpu.get_barrier_semaphore()
    peers = (zp, zm, z2, yl, xp, xm, yhp, sib)
    for dev in peers:
        pl.semaphore_signal(bar, inc=1, device_id=dev, device_id_type=pl.DeviceIdType.MESH)
    for cp in locs:
        cp.wait()

    def own_row(i):
        return pl.ds(m16(jnp.where(i == 0, c * TB, TXT + c * IB + (i - 1) * 16)), 16)

    def norm_rows(i, _):
        rows = own_row(i)
        v = xn[rows, :].astype(F32)
        v = v - jnp.mean(v, axis=-1, keepdims=True)
        v = v * lax.rsqrt(jnp.mean(v * v, axis=-1, keepdims=True) + EPS)
        xn[rows, :] = v.astype(BF)
        return 0

    lax.fori_loop(0, 8, norm_rows, 0)
    pl.semaphore_wait(bar, len(peers))

    def full(cc):
        return (trow(cc), irow(cc))

    def half_a(cc):
        return (irow(cc, 0, 64),)

    def half_b(cc):
        return (irow(cc, 64, 48), trow(cc))

    yc = c + ylflip
    plan = (
        (0, yl, full(c), full(yc)),
        (2, zp, full(c), full(c_zm)),
        (4, zm, full(c), full(c_zp)),
        (6, zp, full(yc), full(c_zm + ylflip)),
        (8, zm, full(yc), full(c_zp + ylflip)),
        (10, zp, half_a(c_zm), half_a(c_z2)),
        (11, zm, half_b(c_zp), half_b(c_z2)),
        (13, zp, half_a(c_zm + ylflip), half_a(c_z2 + ylflip)),
        (14, zm, half_b(c_zp + ylflip), half_b(c_z2 + ylflip)),
    )

    def ctx_send(buf, s, r, n):
        first, dev, rows, _ = plan[n]
        for i, rw in enumerate(rows):
            cp = rcopy(buf.at[rw], buf.at[rw], s.at[first + i], r.at[first + i], dev)
            go(cp, sent_g if buf is g else sent)

    def ctx_recv(buf, s, r, n):
        first, dev, _, rows = plan[n]
        for i, rw in enumerate(rows):
            rcopy(buf.at[rw], buf.at[rw], s.at[first + i], r.at[first + i], dev).wait_recv()

    def wrow(dd, off=0, n=WR):
        return pl.ds(m16(dd * WR + off), n)

    wplan = (
        (yhp, wrow(d), wrow(d + yhflip)),
        (xp, wrow(d), wrow(d_xm)),
        (xm, wrow(d), wrow(d_xp)),
        (xp, wrow(d + yhflip), wrow(d_xm + yhflip)),
        (xm, wrow(d + yhflip), wrow(d_xp + yhflip)),
        (xp, wrow(d_xm, 0, HALF), wrow(d_x2, 0, HALF)),
        (xm, wrow(d_xp, HALF, HALF), wrow(d_x2, HALF, HALF)),
        (xp, wrow(d_xm + yhflip, 0, HALF), wrow(d_x2 + yhflip, 0, HALF)),
        (xm, wrow(d_xp + yhflip, HALF, HALF), wrow(d_x2 + yhflip, HALF, HALF)),
    ) + tuple(
        (sib, wrow(b), wrow(b + 1 - 2 * core))
        for b in (
            d,
            d + yhflip,
            d_xm,
            d_xp,
            d_xm + yhflip,
            d_xp + yhflip,
            d_x2,
            d_x2 + yhflip,
        )
    )

    def w_send(*ns):
        for n in ns:
            dev, rows, _ = wplan[n]
            go(rcopy(w.at[rows], w.at[rows], ws.at[n], wr.at[n], dev))

    def w_recv(*ns):
        for n in ns:
            dev, _, rows = wplan[n]
            rcopy(w.at[rows], w.at[rows], ws.at[n], wr.at[n], dev).wait_recv()

    ctx_send(xn, xs, xr, 0)
    ctx_send(xn, xs, xr, 1)
    ctx_send(xn, xs, xr, 2)
    w_send(0, 1, 2, 9)

    def gate_rows(i, _):
        rows = own_row(i)
        gate = jnp.where(i == 0, modr[5:6, :], modr[2:3, :])
        g[rows, :] = (gate * g[rows, :].astype(F32)).astype(BF)
        return 0

    lax.fori_loop(0, 8, gate_rows, 0)

    def modulate(start, count, text):
        def step(i, _):
            rows = pl.ds(m16(start + i * 16), 16)
            base = 3 if text else 0
            v = xn[rows, :].astype(F32)
            st[rows, :] = (modr[base + 1 : base + 2, :] * v + modr[base : base + 1, :]).astype(BF)
            return 0

        lax.fori_loop(0, count // 16, step, 0)

    def modulate_block(cc):
        modulate(cc * TB, TB, True)
        modulate(TXT + cc * IB, IB, False)

    modulate_block(c)
    ctx_recv(xn, xs, xr, 0)
    ctx_send(xn, xs, xr, 3)
    ctx_send(xn, xs, xr, 4)
    w_recv(0)
    w_send(3, 4, 10)
    modulate_block(yc)
    ctx_recv(xn, xs, xr, 1)
    ctx_send(xn, xs, xr, 5)
    ctx_recv(xn, xs, xr, 2)
    ctx_send(xn, xs, xr, 6)
    w_recv(1)
    w_send(5, 11)
    w_recv(2)
    w_send(6, 12)
    modulate_block(c_zm)
    modulate_block(c_zp)
    ctx_recv(xn, xs, xr, 3)
    ctx_send(xn, xs, xr, 7)
    ctx_recv(xn, xs, xr, 4)
    ctx_send(xn, xs, xr, 8)
    w_recv(3)
    w_send(7, 13)
    w_recv(4)
    w_send(8, 14)
    modulate_block(c_zm + ylflip)
    modulate_block(c_zp + ylflip)
    ctx_recv(xn, xs, xr, 5)
    ctx_recv(xn, xs, xr, 6)
    w_recv(5, 6)
    w_send(15)
    modulate_block(c_z2)
    ctx_recv(xn, xs, xr, 7)
    ctx_recv(xn, xs, xr, 8)
    ctx_send(g, gs, gr, 0)
    ctx_send(g, gs, gr, 1)
    ctx_send(g, gs, gr, 2)
    w_recv(7, 8)
    w_send(16)
    modulate_block(c_z2 + ylflip)
    w_recv(9, 10, 11, 12, 13, 14, 15, 16)

    def project(rows, col):
        left = st[rows, :]
        for j, out in enumerate((qb, kb, vb)):
            acc = dot(left, w[:, col + j * 256 : col + (j + 1) * 256])
            if j == 2:
                out[rows, :] = acc.astype(BF)
                continue
            pq[rows, j * 256 : (j + 1) * 256] = acc
            for h in range(2):
                a = acc[:, h * 128 : (h + 1) * 128]
                f = lax.rsqrt(jnp.mean(a * a, axis=-1, keepdims=True) + EPS)
                out[rows, h * 128 : (h + 1) * 128] = (a * f).astype(BF)

    def project_image(i, _):
        project(pl.ds(m16(TXT + i * 448), 448), QI)
        return 0

    lax.fori_loop(0, 2, project_image, 0)
    project(pl.ds(0, TXT), QT)

    for h in range(2):
        cols = slice(h * 128, (h + 1) * 128)

        def forward(i, _, cols=cols):
            rows = pl.ds(m16(i * 256), 256)
            e = jnp.exp(dot_last(qb[rows, cols], kb[:, cols]) * SCALE)
            p = e / jnp.sum(e, axis=-1, keepdims=True)
            att[rows, cols] = dot(p.astype(BF), vb[:, cols]).astype(BF)
            return 0

        lax.fori_loop(0, 4, forward, 0)

    def mix(i, _):
        n = pl.ds(pl.multiple_of(i * 512, 512), 512)
        st[0:TXT, n] = dot_last(att[0:TXT, :], w[n, OT : OT + 256]).astype(BF)
        st[TXT:576, n] = dot_last(att[TXT:576, :], w[n, OI : OI + 256]).astype(BF)
        st[576:SEQ, n] = dot_last(att[576:SEQ, :], w[n, OI : OI + 256]).astype(BF)
        return 0

    lax.fori_loop(0, 6, mix, 0)

    zs = (c_z2, c_zp, c_zm, c)
    for n, cc in enumerate(zs):
        dst = cc + ylflip
        go(rcopy(st.at[trow(dst)], mland.at[n, pl.ds(0, TB)], mys.at[2 * n], myr.at[2 * n], yl))
        go(
            rcopy(
                st.at[irow(dst)],
                mland.at[n, pl.ds(TB, IB)],
                mys.at[2 * n + 1],
                myr.at[2 * n + 1],
                yl,
            )
        )

    ctx_recv(g, gs, gr, 0)
    ctx_send(g, gs, gr, 3)
    ctx_send(g, gs, gr, 4)
    ctx_recv(g, gs, gr, 1)
    ctx_send(g, gs, gr, 5)
    ctx_recv(g, gs, gr, 2)
    ctx_send(g, gs, gr, 6)

    def mixed_stage(n):
        cc = zs[n]
        for i, (rw, off, size) in enumerate(((trow(cc), 0, TB), (irow(cc), TB, IB))):
            rcopy(
                st.at[rw],
                mland.at[n, pl.ds(off, size)],
                mys.at[2 * n + i],
                myr.at[2 * n + i],
                yl,
            ).wait_recv()

        def step(i, _):
            rows = pl.ds(m16(jnp.where(i == 0, cc * TB, TXT + cc * IB + (i - 1) * 16)), 16)
            land = mland[n, pl.ds(m16(i * 16), 16), :].astype(F32)
            st[rows, :] = (st[rows, :].astype(F32) + land).astype(BF)
            return 0

        lax.fori_loop(0, 8, step, 0)
        dev = (z2, zp, zm)[n]
        go(rcopy(st.at[trow(cc)], mzl.at[n, pl.ds(0, TB)], mzs.at[2 * n], mzr.at[2 * n], dev))
        go(
            rcopy(
                st.at[irow(cc)],
                mzl.at[n, pl.ds(TB, IB)],
                mzs.at[2 * n + 1],
                mzr.at[2 * n + 1],
                dev,
            )
        )

    ctx_recv(g, gs, gr, 3)
    ctx_send(g, gs, gr, 7)
    ctx_recv(g, gs, gr, 4)
    ctx_send(g, gs, gr, 8)
    ctx_recv(g, gs, gr, 5)
    ctx_recv(g, gs, gr, 6)
    ctx_recv(g, gs, gr, 7)
    ctx_recv(g, gs, gr, 8)

    def chip(k):
        j = k // 2
        dx = jnp.where(j == 0, 2, jnp.where(j == 1, 1, jnp.where(j == 2, 3, 0)))
        yy = jnp.where(lax.rem(k, 2) == 0, 1 - yh, yh)
        return lax.rem(xpos + dx, 4) * 2 + yy

    def out_tile(k):
        cols = pl.ds(pl.multiple_of(chip(k) * 384, 128), 384)
        so[k, :, 0:256] = dot_rows(g[TXT:SEQ, cols], att[TXT:SEQ, :]).astype(BF)
        so[k, :, 256:512] = dot_rows(g[0:TXT, cols], att[0:TXT, :]).astype(BF)

    def stage_cols(k):
        return pl.ds(pl.multiple_of(lax.rem(k, 4) * 768, 256), 768)

    def qkv_tile(k, text):
        p = chip(k)
        cols = pl.ds(pl.multiple_of(p * 384, 128), 384)
        rows = slice(0, TXT) if text else slice(TXT, SEQ)
        base = 3 if text else 0
        wcol = QT if text else QI
        back = bq[rows, :]
        grad = dot_rows(xn[rows, cols], back)
        total = jnp.sum(back.astype(F32), axis=0, keepdims=True)
        own = w[pl.ds(m16(p * 384), 384), wcol : wcol + 768].astype(F32)
        shift_part = jnp.sum(own * total, axis=-1, keepdims=True)
        scale_part = jnp.sum(own * grad, axis=-1, keepdims=True)
        lane = lax.broadcasted_iota(jnp.int32, (384, 128), 1)
        vals = jnp.where(lane == base, shift_part, jnp.where(lane == base + 1, scale_part, 0.0))
        mrow = pl.ds(m16(lax.rem(p, 2) * 384), 384)
        mcol = pl.ds(pl.multiple_of(p // 2 * 128, 128), 128)
        if text:
            vals = vals + pq[mrow, mcol]
        pq[mrow, mcol] = vals
        mod = modc[pl.ds(m16(p * 384), 384), :].astype(F32)
        full_grad = (1.0 + mod[:, base + 1 : base + 2]) * grad + mod[:, base : base + 1] * total
        g[pl.ds(m16(k // 4 * 384), 384), stage_cols(k)] = full_grad.astype(BF)

    def stage(gi, k, half):
        rows = half * WR
        if gi == 0:
            return so.at[k, pl.ds(m16(rows), WR)]
        return g.at[pl.ds(m16(k // 4 * 384 + rows), WR), stage_cols(k)]

    def to_sib(gi, k):
        c0, n = GROUPS[gi]
        return rcopy(
            stage(gi, k, 1 - core),
            sland.at[k, :, c0 : c0 + n],
            ss.at[gi * 8 + k],
            sr.at[gi * 8 + k],
            sib,
        )

    def grad_range(gi, k0, k1):
        c0, n = GROUPS[gi]

        def compute(k, _):
            if gi == 0:
                out_tile(k)
            else:
                qkv_tile(k, gi == 2)
            to_sib(gi, k).start()
            return 0

        lax.fori_loop(k0, k1, compute, 0)

        def combine(k, _):
            to_sib(gi, k).wait()

            def step(i, _):
                r = pl.ds(m16(i * 32), 32)
                if gi == 0:
                    mine = so[k, pl.ds(m16(core * WR + i * 32), 32), :]
                else:
                    mine = g[pl.ds(m16(k // 4 * 384 + core * WR + i * 32), 32), stage_cols(k)]
                land = sland[k, r, c0 : c0 + n].astype(F32)
                sland[k, r, c0 : c0 + n] = (mine.astype(F32) + land).astype(BF)
                return 0

            lax.fori_loop(0, 6, step, 0)
            return 0

        lax.fori_loop(k0, k1, combine, 0)

    def gcopy(gi, n, src, dst, dev):
        return rcopy(src, dst, rs.at[gi * 9 + n], rr.at[gi * 9 + n], dev)

    def far_copy(gi, v, side):
        c0, n = GROUPS[gi]
        cs = slice(c0, c0 + n)
        src = sland.at[v, pl.ds(side * HALF, HALF), cs]
        dst = (ha, hb)[side].at[v, :, cs]
        return gcopy(gi, 2 * v + side, src, dst, (xp, xm)[side])

    def near_copy(gi, v, side):
        c0, n = GROUPS[gi]
        cs = slice(c0, c0 + n)
        src = sland.at[2 + 2 * side + v, :, cs]
        return gcopy(gi, 4 + 2 * v + side, src, xl.at[side, v, :, cs], (xp, xm)[side])

    def yh_copy(gi):
        c0, n = GROUPS[gi]
        cs = slice(c0, c0 + n)
        return gcopy(gi, 8, sland.at[6, :, cs], yhl.at[:, cs], yhp)

    def grad_far(gi):
        for v in range(2):
            for side in range(2):
                go(far_copy(gi, v, side))

    def grad_near(gi):
        c0, n = GROUPS[gi]
        cs = slice(c0, c0 + n)
        for v in range(2):
            for side, land in ((0, ha), (1, hb)):
                far_copy(gi, v, side).wait_recv()
                k = 2 + 2 * side + v

                def step(i, _, land=land, k=k, side=side, v=v):
                    r = pl.ds(m16(side * HALF + i * 32), 32)
                    q = pl.ds(m16(i * 32), 32)
                    sland[k, r, cs] = (
                        sland[k, r, cs].astype(F32) + land[v, q, cs].astype(F32)
                    ).astype(BF)
                    return 0

                lax.fori_loop(0, 3, step, 0)
                go(near_copy(gi, v, side))

    def grad_yh(gi):
        c0, n = GROUPS[gi]
        cs = slice(c0, c0 + n)
        near_copy(gi, 0, 0).wait_recv()
        near_copy(gi, 0, 1).wait_recv()

        def step(i, _):
            r = pl.ds(m16(i * 32), 32)
            total = sland[6, r, cs].astype(F32) + xl[0, 0, r, cs].astype(F32)
            sland[6, r, cs] = (total + xl[1, 0, r, cs].astype(F32)).astype(BF)
            return 0

        lax.fori_loop(0, 6, step, 0)
        go(yh_copy(gi))

    def grad_last(gi):
        c0, n = GROUPS[gi]
        near_copy(gi, 1, 0).wait_recv()
        near_copy(gi, 1, 1).wait_recv()
        yh_copy(gi).wait_recv()
        for b in range(c0 // 256, (c0 + n) // 256):
            cs = slice(b * 256, (b + 1) * 256)

            def step(i, _, cs=cs, b=b):
                r = pl.ds(m16(i * 32), 32)
                total = sland[7, r, cs].astype(F32) + xl[0, 1, r, cs].astype(F32)
                total = total + xl[1, 1, r, cs].astype(F32) + yhl[r, cs].astype(F32)
                orow = pl.ds(m16(b // 2 * WR + i * 32), 32)
                pq[orow, b % 2 * 256 : b % 2 * 256 + 256] = total
                return 0

            lax.fori_loop(0, 6, step, 0)

    grad_range(0, 0, 2)
    grad_far(0)

    def back_image(i, _):
        rows = pl.ds(m16(TXT + i * 448), 448)
        batt[rows, :] = dot(g[rows, :], w[:, OI : OI + 256]).astype(BF)
        return 0

    lax.fori_loop(0, 2, back_image, 0)
    batt[0:TXT, :] = dot(g[0:TXT, :], w[:, OT : OT + 256]).astype(BF)
    grad_range(0, 2, 8)
    grad_near(0)

    for cp in sent_g:
        cp.wait_send()
    slopes = pltpu.make_async_copy(slo, g.at[pl.ds(768, 128)], loc.at[5])
    slopes.start()

    def rms_back(a, slope):
        f = lax.rsqrt(jnp.mean(a * a, axis=-1, keepdims=True) + EPS)
        normal = a * f
        return f * (slope - normal * jnp.mean(slope * normal, axis=-1, keepdims=True))

    for h in range(2):
        cols = slice(h * 128, (h + 1) * 128)
        dk[...] = jnp.zeros_like(dk)
        dv[...] = jnp.zeros_like(dv)

        def backward(i, _, cols=cols):
            rows = pl.ds(m16(i * 256), 256)
            qt = qb[rows, cols]
            bt = batt[rows, cols]
            e = jnp.exp(dot_last(kb[:, cols], qt) * SCALE)
            p = e / jnp.sum(e, axis=0, keepdims=True)
            dv[...] += dot(p.astype(BF), bt)
            dp = dot_last(vb[:, cols], bt)
            ds = p * (dp - jnp.sum(p * dp, axis=0, keepdims=True)) * SCALE
            ds = ds.astype(BF)
            dk[...] += dot(ds, qt)
            dq = dot_rows(ds, kb[:, cols])
            bq[rows, cols] = rms_back(pq[rows, cols], dq).astype(BF)
            return 0

        lax.fori_loop(0, 4, backward, 0)

        def finish(i, _, h=h, cols=cols):
            rows = pl.ds(m16(i * 256), 256)
            kcols = slice(256 + h * 128, 384 + h * 128)
            bq[rows, kcols] = rms_back(pq[rows, kcols], dk[rows, :]).astype(BF)
            bq[rows, 512 + h * 128 : 640 + h * 128] = dv[rows, :].astype(BF)
            return 0

        lax.fori_loop(0, 4, finish, 0)

    for gi in (1, 2):
        grad_range(gi, 0, 2)
        grad_far(gi)
        grad_range(gi, 2, 8)
        if gi == 1:
            mixed_stage(0)
    grad_near(1)
    mixed_stage(1)
    mixed_stage(2)
    grad_near(2)
    grad_yh(0)

    def turn(p, _):
        mrow = pl.ds(m16(lax.rem(p, 2) * 384), 384)
        mcol = pl.ds(pl.multiple_of(p // 2 * 128, 128), 128)
        flat = jnp.transpose(pq[mrow, mcol])
        ms[0, :, pl.ds(pl.multiple_of(p * 384, 128), 384)] = flat[0:8, :]
        return 0

    lax.fori_loop(0, 8, turn, 0)
    grad_yh(1)

    for i, (off, size) in enumerate(((0, TB), (TB, IB))):
        rcopy(
            st.at[pl.ds(0, size)], mland.at[3, pl.ds(off, size)], mys.at[6 + i], myr.at[6 + i], yl
        ).wait_recv()
        for n in range(3):
            rcopy(
                st.at[pl.ds(0, size)],
                mzl.at[n, pl.ds(off, size)],
                mzs.at[2 * n + i],
                mzr.at[2 * n + i],
                zp,
            ).wait_recv()
    slopes.wait()

    def own_mixed(i, gate, acc):
        rows = own_row(i)
        q = pl.ds(m16(i * 16), 16)
        total = st[rows, :].astype(F32) + mland[3, q, :].astype(F32)
        for n in range(3):
            total = total + mzl[n, q, :].astype(F32)
        st[rows, :] = (gate * total).astype(BF)
        slope = g[pl.ds(m16(768 + i * 16), 16), :].astype(F32)
        return acc + jnp.sum(slope * total, axis=0, keepdims=True)

    zero = jnp.zeros((1, D), F32)
    ms[0, 5:6, :] = own_mixed(0, modr[5:6, :], zero)
    ms[0, 2:3, :] = zero

    def image_mixed(i, _):
        ms[0, 2:3, :] = own_mixed(i, modr[2:3, :], ms[0, 2:3, :])
        return 0

    lax.fori_loop(1, 8, image_mixed, 0)
    outs = [
        pltpu.make_async_copy(st.at[trow(c)], upd.at[pl.ds(0, TB)], loc.at[6]),
        pltpu.make_async_copy(st.at[irow(c)], upd.at[pl.ds(TB, IB)], loc.at[7]),
    ]
    for cp in outs:
        cp.start()

    first = rcopy(ms.at[0], ml.at[0], mss.at[0], msr.at[0], yl)
    go(first)
    first.wait_recv()
    ms[1] = ms[0] + ml[0]
    more = [
        rcopy(ms.at[1], ml.at[1 + n], mss.at[1 + n], msr.at[1 + n], dev)
        for n, dev in enumerate((zp, zm, z2))
    ]
    for cp in more:
        go(cp)
    grad_yh(2)
    for cp in more:
        cp.wait_recv()
    modsum[...] = ms[1] + ml[1] + ml[2] + ml[3]

    for gi in range(3):
        grad_last(gi)
    for b in range(4):
        cp = pltpu.make_async_copy(
            pq.at[pl.ds(b * WR, WR)], gout.at[:, b * 512 : (b + 1) * 512], loc.at[8 + b]
        )
        cp.start()
        outs.append(cp)
    for cp in outs:
        cp.wait()
    for cp in sent:
        cp.wait_send()


def body(
    image_tokens,
    text_tokens,
    image_mod,
    text_mod,
    image_qkv_weight,
    text_qkv_weight,
    image_out_weight,
    text_out_weight,
    image_slope,
    text_slope,
):
    tok = jnp.concatenate([text_tokens[0], image_tokens[0]], axis=0)
    slo = jnp.concatenate([text_slope[0], image_slope[0]], axis=0)
    wl = jnp.concatenate(
        [
            image_qkv_weight.reshape(WR, 768),
            text_qkv_weight.reshape(WR, 768),
            image_out_weight.reshape(WR, 256),
            text_out_weight.reshape(WR, 256),
        ],
        axis=1,
    )
    mods = jnp.concatenate([image_mod[0], text_mod[0], jnp.zeros((2, D), BF)], axis=0)
    bump = jnp.array([0, 1, 0, 0, 1, 0, 0, 0], F32)[:, None]
    modr = mods.astype(F32) + bump
    modc = mods.T
    hbm = pl.BlockSpec(memory_space=pl.ANY)
    vmem = pl.BlockSpec(memory_space=pltpu.VMEM)
    dma = pltpu.SemaphoreType.DMA
    upd, gout, modsum = pl.pallas_call(
        kernel,
        out_shape=(
            jax.ShapeDtypeStruct((TB + IB, D), BF),
            jax.ShapeDtypeStruct((WR, WC), F32),
            jax.ShapeDtypeStruct((8, D), F32),
        ),
        in_specs=[hbm, hbm, hbm, vmem, vmem],
        out_specs=(hbm, hbm, vmem),
        scratch_shapes=[
            pltpu.VMEM((SEQ, D), BF),
            pltpu.VMEM((SEQ, D), BF),
            pltpu.VMEM((D, WC), BF),
            pltpu.VMEM((SEQ, D), BF),
            pltpu.VMEM((SEQ, 512), F32),
            pltpu.VMEM((SEQ, 256), BF),
            pltpu.VMEM((SEQ, 256), BF),
            pltpu.VMEM((SEQ, 256), BF),
            pltpu.VMEM((SEQ, 256), BF),
            pltpu.VMEM((SEQ, 256), BF),
            pltpu.VMEM((SEQ, 768), BF),
            pltpu.VMEM((SEQ, 128), F32),
            pltpu.VMEM((SEQ, 128), F32),
            pltpu.VMEM((4, 128, D), BF),
            pltpu.VMEM((3, 128, D), BF),
            pltpu.VMEM((8, WR, WC), BF),
            pltpu.VMEM((8, 384, 512), BF),
            pltpu.VMEM((2, HALF, WC), BF),
            pltpu.VMEM((2, HALF, WC), BF),
            pltpu.VMEM((2, 2, WR, WC), BF),
            pltpu.VMEM((WR, WC), BF),
            pltpu.VMEM((2, 8, D), F32),
            pltpu.VMEM((4, 8, D), F32),
            dma((16,)),
            dma((16,)),
            dma((16,)),
            dma((16,)),
            dma((17,)),
            dma((17,)),
            dma((8,)),
            dma((8,)),
            dma((6,)),
            dma((6,)),
            dma((24,)),
            dma((24,)),
            dma((27,)),
            dma((27,)),
            dma((4,)),
            dma((4,)),
            dma((12,)),
        ],
        compiler_params=pltpu.CompilerParams(
            collective_id=0, has_side_effects=True, vmem_limit_bytes=63 * 2**20
        ),
    )(tok, slo, wl, modr, modc)
    return (
        upd[TB:][None],
        upd[:TB][None],
        gout[:, QI:QT].reshape(WR, 3, 2, 128),
        gout[:, QT:OI].reshape(WR, 3, 2, 128),
        gout[:, OI:OT].reshape(WR, 2, 128),
        gout[:, OT:WC].reshape(WR, 2, 128),
        modsum[0:3][None],
        modsum[3:6][None],
    )


def solution(mesh):
    tokens = P("dp", "context", None)
    mods = P("dp", None, None)
    qkv = P("dp", None, "context", None)
    return jax.shard_map(
        body,
        mesh=mesh,
        in_specs=(tokens, tokens, mods, mods, qkv, qkv, tokens, tokens, tokens, tokens),
        out_specs=(tokens, tokens, qkv, qkv, tokens, tokens, mods, mods),
        check_vma=False,
    )
```

```python
import jax
import jax.numpy as jnp
from jax import lax
from jax.experimental import pallas as pl
from jax.experimental.pallas import tpu as pltpu
from jax.sharding import PartitionSpec as P

EPS = 1e-06
BF = jnp.bfloat16
F32 = jnp.float32
D = 3072
TXT = 128
SEQ = 1024
TB = 16
IB = 112
WR = 192
HALF = 96
SCALE = 128 ** (-0.5)
QI, QT, OI, OT, WC = 0, 768, 1536, 1792, 2048
GROUPS = ((OI, 512), (QI, 768), (QT, 768))


def dot(a, b):
    return jnp.dot(a, b, preferred_element_type=F32)


def dot_last(a, b):
    return lax.dot_general(a, b, (((1,), (1,)), ((), ())), preferred_element_type=F32)


def dot_rows(a, b):
    return lax.dot_general(a, b, (((0,), (0,)), ((), ())), preferred_element_type=F32)


def each(low, high, step):
    lax.fori_loop(low, high, lambda i, _: (step(i), 0)[1], 0)


each_io = each


def m16(v):
    return pl.multiple_of(v, 16)


def kernel(
    tok_i,
    tok_t,
    slo_i,
    slo_t,
    wq_i,
    wq_t,
    wo_i,
    wo_t,
    mod_i,
    mod_t,
    upd_i,
    upd_t,
    gq_i,
    gq_t,
    go_i,
    go_t,
    ms_i,
    ms_t,
    xn,
    g,
    w,
    st,
    pq,
    qb,
    kb,
    vb,
    att,
    batt,
    bq,
    dk,
    dv,
    modr,
    mland,
    mzl,
    sland,
    so,
    ha,
    hb,
    xl,
    yhl,
    ms,
    ml,
    xs,
    xr,
    gs,
    gr,
    ws,
    wr,
    mys,
    myr,
    mzs,
    mzr,
    ss,
    sr,
    rs,
    rr,
    mss,
    msr,
    loc,
):
    d = lax.axis_index("dp")
    c = lax.axis_index("context")
    core = lax.rem(d, 2)
    yh = lax.rem(d // 2, 2)
    xpos = d // 4
    c_zp, c_zm, c_z2 = lax.rem(c + 2, 8), lax.rem(c + 6, 8), lax.rem(c + 4, 8)
    ylflip = 1 - 2 * lax.rem(c, 2)
    d_xp, d_xm, d_x2 = lax.rem(d + 4, 16), lax.rem(d + 12, 16), lax.rem(d + 8, 16)
    yhflip = 2 - 4 * yh
    zp, zm, z2, yl = (d, c_zp), (d, c_zm), (d, c_z2), (d, c + ylflip)
    xp, xm, yhp, sib = (d_xp, c), (d_xm, c), (d + yhflip, c), (d + 1 - 2 * core, c)

    def rcopy(src, dst, ssem, rsem, dev):
        return pltpu.make_async_remote_copy(
            src_ref=src,
            dst_ref=dst,
            send_sem=ssem,
            recv_sem=rsem,
            device_id=dev,
            device_id_type=pl.DeviceIdType.MESH,
        )

    def trow(cc):
        return pl.ds(m16(cc * TB), TB)

    def irow(cc, off=0, n=IB):
        return pl.ds(m16(TXT + cc * IB + off), n)

    sent = []
    sent_g = []

    def go(cp, kept=sent):
        cp.start()
        kept.append(cp)

    wown = pl.ds(m16(d * WR), WR)
    locs = [
        pltpu.make_async_copy(src, dst, loc.at[n])
        for n, (src, dst) in enumerate(
            (
                (tok_t.at[0], xn.at[trow(c)]),
                (tok_i.at[0], xn.at[irow(c)]),
                (slo_t.at[0], g.at[trow(c)]),
                (slo_i.at[0], g.at[irow(c)]),
                (wq_i, w.at[wown, QI : QI + 768]),
                (wq_t, w.at[wown, QT : QT + 768]),
                (wo_i, w.at[wown, OI : OI + 256]),
                (wo_t, w.at[wown, OT : OT + 256]),
            )
        )
    ]
    for cp in locs:
        cp.start()
    bar = pltpu.get_barrier_semaphore()
    peers = (zp, zm, z2, yl, xp, xm, yhp, sib)
    for dev in peers:
        pl.semaphore_signal(bar, inc=1, device_id=dev, device_id_type=pl.DeviceIdType.MESH)
    modr[...] = jnp.zeros_like(modr)
    modr[0:3, :] = mod_i[0].astype(F32)
    modr[3:6, :] = mod_t[0].astype(F32)
    modr[1:2, :] = modr[1:2, :] + 1.0
    modr[4:5, :] = modr[4:5, :] + 1.0
    for cp in locs:
        cp.wait()

    def own_row(i):
        return pl.ds(m16(jnp.where(i == 0, c * TB, TXT + c * IB + (i - 1) * 16)), 16)

    def norm_rows(i):
        rows = own_row(i)
        v = xn[rows, :].astype(F32)
        v = v - jnp.mean(v, axis=-1, keepdims=True)
        v = v * lax.rsqrt(jnp.mean(v * v, axis=-1, keepdims=True) + EPS)
        xn[rows, :] = v.astype(BF)

    each(0, 8, norm_rows)
    pl.semaphore_wait(bar, len(peers))

    def full(cc):
        return (trow(cc), irow(cc))

    def half_a(cc):
        return (irow(cc, 0, 64),)

    def half_b(cc):
        return (irow(cc, 64, 48), trow(cc))

    def main(cc):
        return (trow(cc), irow(cc, 0, 80))

    def main_a(cc):
        return (irow(cc, 0, 48),)

    def main_b(cc):
        return (irow(cc, 48, 32), trow(cc))

    def edge(cc):
        return (irow(cc, 80, 32),)

    yc = c + ylflip
    y_zp, y_zm, y_z2 = c_zp + ylflip, c_zm + ylflip, c_z2 + ylflip
    plan = (
        (0, yl, full(c), full(yc)),
        (2, zp, full(c), full(c_zm)),
        (4, zm, full(c), full(c_zp)),
        (6, zp, main(yc), main(y_zm)),
        (8, zm, main(yc), main(y_zp)),
        (10, zp, half_a(c_zm), half_a(c_z2)),
        (11, zm, half_b(c_zp), half_b(c_z2)),
        (13, zp, main_a(y_zm), main_a(y_z2)),
        (14, zm, main_b(y_zp), main_b(y_z2)),
        (16, yl, edge(c_zm), edge(y_zm)),
        (17, yl, edge(c_zp), edge(y_zp)),
        (18, yl, edge(c_z2), edge(y_z2)),
    )

    def ctx_send(buf, s, r, n):
        first, dev, rows, _ = plan[n]
        for i, rw in enumerate(rows):
            cp = rcopy(buf.at[rw], buf.at[rw], s.at[first + i], r.at[first + i], dev)
            go(cp, sent_g if buf is g else sent)

    def ctx_recv(buf, s, r, n):
        first, dev, _, rows = plan[n]
        for i, rw in enumerate(rows):
            rcopy(buf.at[rw], buf.at[rw], s.at[first + i], r.at[first + i], dev).wait_recv()

    def wrow(dd, off=0, n=WR):
        return pl.ds(m16(dd * WR + off), n)

    wplan = (
        (yhp, wrow(d), wrow(d + yhflip)),
        (xp, wrow(d), wrow(d_xm)),
        (xm, wrow(d), wrow(d_xp)),
        (xp, wrow(d + yhflip), wrow(d_xm + yhflip)),
        (xm, wrow(d + yhflip), wrow(d_xp + yhflip)),
        (xp, wrow(d_xm, 0, HALF), wrow(d_x2, 0, HALF)),
        (xm, wrow(d_xp, HALF, HALF), wrow(d_x2, HALF, HALF)),
        (xp, wrow(d_xm + yhflip, 0, HALF), wrow(d_x2 + yhflip, 0, HALF)),
        (xm, wrow(d_xp + yhflip, HALF, HALF), wrow(d_x2 + yhflip, HALF, HALF)),
    ) + tuple(
        (sib, wrow(b), wrow(b + 1 - 2 * core))
        for b in (
            d,
            d + yhflip,
            d_xm,
            d_xp,
            d_xm + yhflip,
            d_xp + yhflip,
            d_x2,
            d_x2 + yhflip,
        )
    )

    def w_send(*ns):
        for n in ns:
            dev, rows, _ = wplan[n]
            go(rcopy(w.at[rows], w.at[rows], ws.at[n], wr.at[n], dev))

    def w_recv(*ns):
        for n in ns:
            dev, _, rows = wplan[n]
            rcopy(w.at[rows], w.at[rows], ws.at[n], wr.at[n], dev).wait_recv()

    def x_send(*ns):
        for n in ns:
            ctx_send(xn, xs, xr, n)

    def x_recv(*ns):
        for n in ns:
            ctx_recv(xn, xs, xr, n)

    def g_send(*ns):
        for n in ns:
            ctx_send(g, gs, gr, n)

    def g_recv(*ns):
        for n in ns:
            ctx_recv(g, gs, gr, n)

    x_send(0, 1, 2)
    w_send(0, 1, 2, 9)

    def gate_rows(i):
        rows = own_row(i)
        gate = jnp.where(i == 0, modr[5:6, :], modr[2:3, :])
        g[rows, :] = (gate * g[rows, :].astype(F32)).astype(BF)

    each(0, 8, gate_rows)

    def modulate(start, count, text):
        def step(i):
            rows = pl.ds(m16(start + i * 16), 16)
            base = 3 if text else 0
            v = xn[rows, :].astype(F32)
            st[rows, :] = (modr[base + 1 : base + 2, :] * v + modr[base : base + 1, :]).astype(BF)

        each(0, count // 16, step)

    def modulate_block(cc):
        modulate(cc * TB, TB, True)
        modulate(TXT + cc * IB, IB, False)

    modulate_block(c)
    x_recv(1)
    x_send(5, 9)
    x_recv(2)
    x_send(6, 10)
    w_recv(1)
    w_send(5, 11)
    w_recv(2)
    w_send(6, 12)
    g_send(1, 2)
    modulate_block(c_zm)
    modulate_block(c_zp)
    x_recv(0)
    x_send(3, 4)
    w_recv(0)
    w_send(3, 4, 10)
    g_send(0)
    modulate_block(yc)
    x_recv(5, 6)
    x_send(11)
    w_recv(5, 6)
    w_send(15)
    modulate_block(c_z2)
    g_recv(1)
    g_send(5, 9)
    g_recv(2)
    g_send(6, 10)
    x_recv(3)
    x_send(7)
    x_recv(4)
    x_send(8)
    w_recv(3)
    w_send(7, 13)
    w_recv(4)
    w_send(8, 14)
    x_recv(9, 10)
    modulate_block(y_zm)
    modulate_block(y_zp)
    g_recv(0)
    g_send(3, 4)
    x_recv(7, 8, 11)
    w_recv(7, 8)
    w_send(16)
    modulate_block(y_z2)
    g_recv(5, 6)
    g_send(11)
    w_recv(9, 10, 11, 12, 13, 14, 15, 16)

    def project(rows, col):
        left = st[rows, :]
        for j, out in enumerate((qb, kb, vb)):
            acc = dot(left, w[:, col + j * 256 : col + (j + 1) * 256])
            if j == 2:
                out[rows, :] = acc.astype(BF)
                continue
            pq[rows, j * 256 : (j + 1) * 256] = acc
            for h in range(2):
                a = acc[:, h * 128 : (h + 1) * 128]
                f = lax.rsqrt(jnp.mean(a * a, axis=-1, keepdims=True) + EPS)
                out[rows, h * 128 : (h + 1) * 128] = (a * f).astype(BF)

    def project_image(i):
        project(pl.ds(m16(TXT + i * 448), 448), QI)

    each(0, 2, project_image)
    project(pl.ds(0, TXT), QT)

    for h in range(2):
        cols = slice(h * 128, (h + 1) * 128)

        def forward(i, cols=cols):
            rows = pl.ds(m16(i * 256), 256)
            e = jnp.exp(dot_last(qb[rows, cols], kb[:, cols]) * SCALE)
            p = e / jnp.sum(e, axis=-1, keepdims=True)
            att[rows, cols] = dot(p.astype(BF), vb[:, cols]).astype(BF)

        each(0, 4, forward)

    def mix(i):
        n = pl.ds(pl.multiple_of(i * 512, 512), 512)
        st[0:TXT, n] = dot_last(att[0:TXT, :], w[n, OT : OT + 256]).astype(BF)
        st[TXT:576, n] = dot_last(att[TXT:576, :], w[n, OI : OI + 256]).astype(BF)
        st[576:SEQ, n] = dot_last(att[576:SEQ, :], w[n, OI : OI + 256]).astype(BF)

    each(0, 6, mix)

    zs = (c_z2, c_zp, c_zm, c)
    for n, cc in enumerate(zs):
        dst = cc + ylflip
        go(rcopy(st.at[trow(dst)], mland.at[n, pl.ds(0, TB)], mys.at[2 * n], myr.at[2 * n], yl))
        go(
            rcopy(
                st.at[irow(dst)],
                mland.at[n, pl.ds(TB, IB)],
                mys.at[2 * n + 1],
                myr.at[2 * n + 1],
                yl,
            )
        )

    def mixed_stage(n):
        cc = zs[n]
        for i, (rw, off, size) in enumerate(((trow(cc), 0, TB), (irow(cc), TB, IB))):
            rcopy(
                st.at[rw],
                mland.at[n, pl.ds(off, size)],
                mys.at[2 * n + i],
                myr.at[2 * n + i],
                yl,
            ).wait_recv()

        def step(i):
            rows = pl.ds(m16(jnp.where(i == 0, cc * TB, TXT + cc * IB + (i - 1) * 16)), 16)
            land = mland[n, pl.ds(m16(i * 16), 16), :].astype(F32)
            st[rows, :] = (st[rows, :].astype(F32) + land).astype(BF)

        each(0, 8, step)
        dev = (z2, zp, zm)[n]
        go(rcopy(st.at[trow(cc)], mzl.at[n, pl.ds(0, TB)], mzs.at[2 * n], mzr.at[2 * n], dev))
        go(
            rcopy(
                st.at[irow(cc)],
                mzl.at[n, pl.ds(TB, IB)],
                mzs.at[2 * n + 1],
                mzr.at[2 * n + 1],
                dev,
            )
        )

    def chip(k):
        j = k // 2
        dx = jnp.where(j == 0, 2, jnp.where(j == 1, 1, jnp.where(j == 2, 3, 0)))
        yy = jnp.where(lax.rem(k, 2) == 0, 1 - yh, yh)
        return lax.rem(xpos + dx, 4) * 2 + yy

    def out_tile(k):
        cols = pl.ds(pl.multiple_of(chip(k) * 384, 128), 384)
        so[k, :, 0:256] = dot_rows(g[TXT:SEQ, cols], att[TXT:SEQ, :]).astype(BF)
        so[k, :, 256:512] = dot_rows(g[0:TXT, cols], att[0:TXT, :]).astype(BF)

    def stage_cols(k):
        return pl.ds(pl.multiple_of(lax.rem(k, 4) * 768, 256), 768)

    def qkv_tile(k, text):
        p = chip(k)
        cols = pl.ds(pl.multiple_of(p * 384, 128), 384)
        rows = slice(0, TXT) if text else slice(TXT, SEQ)
        base = 3 if text else 0
        wcol = QT if text else QI
        back = bq[rows, :]
        grad = dot_rows(xn[rows, cols], back)
        total = jnp.sum(back.astype(F32), axis=0, keepdims=True)
        own = w[pl.ds(m16(p * 384), 384), wcol : wcol + 768].astype(F32)
        shift_part = jnp.sum(own * total, axis=-1, keepdims=True)
        scale_part = jnp.sum(own * grad, axis=-1, keepdims=True)
        lane = lax.broadcasted_iota(jnp.int32, (384, 128), 1)
        vals = jnp.where(lane == base, shift_part, jnp.where(lane == base + 1, scale_part, 0.0))
        mrow = pl.ds(m16(lax.rem(p, 2) * 384), 384)
        mcol = pl.ds(pl.multiple_of(p // 2 * 128, 128), 128)
        if text:
            vals = vals + pq[mrow, mcol]
        pq[mrow, mcol] = vals
        mod = jnp.transpose(modr[:, cols])
        full_grad = mod[:, base + 1 : base + 2] * grad + mod[:, base : base + 1] * total
        g[pl.ds(m16(k // 4 * 384), 384), stage_cols(k)] = full_grad.astype(BF)

    def stage(gi, k, half):
        rows = half * WR
        if gi == 0:
            return so.at[k, pl.ds(m16(rows), WR)]
        return g.at[pl.ds(m16(k // 4 * 384 + rows), WR), stage_cols(k)]

    def to_sib(gi, k):
        c0, n = GROUPS[gi]
        return rcopy(
            stage(gi, k, 1 - core),
            sland.at[k, :, c0 : c0 + n],
            ss.at[gi * 8 + k],
            sr.at[gi * 8 + k],
            sib,
        )

    def grad_range(gi, k0, k1):
        c0, n = GROUPS[gi]

        def compute(k):
            if gi == 0:
                out_tile(k)
            else:
                qkv_tile(k, gi == 2)
            to_sib(gi, k).start()

        each_io(k0, k1, compute)

        def combine(k):
            to_sib(gi, k).wait()

            def step(i):
                r = pl.ds(m16(i * 32), 32)
                if gi == 0:
                    mine = so[k, pl.ds(m16(core * WR + i * 32), 32), :]
                else:
                    mine = g[pl.ds(m16(k // 4 * 384 + core * WR + i * 32), 32), stage_cols(k)]
                land = sland[k, r, c0 : c0 + n].astype(F32)
                sland[k, r, c0 : c0 + n] = (mine.astype(F32) + land).astype(BF)

            each(0, 6, step)

        each_io(k0, k1, combine)

    def gcopy(gi, n, src, dst, dev):
        return rcopy(src, dst, rs.at[gi * 9 + n], rr.at[gi * 9 + n], dev)

    def far_copy(gi, v, side):
        c0, n = GROUPS[gi]
        cs = slice(c0, c0 + n)
        src = sland.at[v, pl.ds(side * HALF, HALF), cs]
        dst = (ha, hb)[side].at[v, :, cs]
        return gcopy(gi, 2 * v + side, src, dst, (xp, xm)[side])

    def near_copy(gi, v, side):
        c0, n = GROUPS[gi]
        cs = slice(c0, c0 + n)
        src = sland.at[2 + 2 * side + v, :, cs]
        return gcopy(gi, 4 + 2 * v + side, src, xl.at[side, v, :, cs], (xp, xm)[side])

    def yh_copy(gi):
        c0, n = GROUPS[gi]
        cs = slice(c0, c0 + n)
        return gcopy(gi, 8, sland.at[6, :, cs], yhl.at[:, cs], yhp)

    def grad_far(gi):
        for v in range(2):
            for side in range(2):
                go(far_copy(gi, v, side))

    def grad_near(gi):
        c0, n = GROUPS[gi]
        cs = slice(c0, c0 + n)
        for v in range(2):
            for side, land in ((0, ha), (1, hb)):
                far_copy(gi, v, side).wait_recv()
                k = 2 + 2 * side + v

                def step(i, land=land, k=k, side=side, v=v):
                    r = pl.ds(m16(side * HALF + i * 32), 32)
                    q = pl.ds(m16(i * 32), 32)
                    sland[k, r, cs] = (
                        sland[k, r, cs].astype(F32) + land[v, q, cs].astype(F32)
                    ).astype(BF)

                each(0, 3, step)
                go(near_copy(gi, v, side))

    def grad_yh(gi):
        c0, n = GROUPS[gi]
        cs = slice(c0, c0 + n)
        near_copy(gi, 0, 0).wait_recv()
        near_copy(gi, 0, 1).wait_recv()

        def step(i):
            r = pl.ds(m16(i * 32), 32)
            total = sland[6, r, cs].astype(F32) + xl[0, 0, r, cs].astype(F32)
            sland[6, r, cs] = (total + xl[1, 0, r, cs].astype(F32)).astype(BF)

        each(0, 6, step)
        go(yh_copy(gi))

    def grad_last(gi):
        c0, n = GROUPS[gi]
        near_copy(gi, 1, 0).wait_recv()
        near_copy(gi, 1, 1).wait_recv()
        yh_copy(gi).wait_recv()
        for b in range(c0 // 256, (c0 + n) // 256):
            cs = slice(b * 256, (b + 1) * 256)

            def step(i, cs=cs, b=b):
                r = pl.ds(m16(i * 32), 32)
                total = sland[7, r, cs].astype(F32) + xl[0, 1, r, cs].astype(F32)
                total = total + xl[1, 1, r, cs].astype(F32) + yhl[r, cs].astype(F32)
                orow = pl.ds(m16(b // 2 * WR + i * 32), 32)
                pq[orow, b % 2 * 256 : b % 2 * 256 + 256] = total

            each(0, 6, step)

    def rms_back(a, slope):
        f = lax.rsqrt(jnp.mean(a * a, axis=-1, keepdims=True) + EPS)
        normal = a * f
        return f * (slope - normal * jnp.mean(slope * normal, axis=-1, keepdims=True))

    def backward(ca, cb, fresh):
        parts = ((trow(ca), 0, TB), (trow(cb), 16, TB), (irow(ca), 32, IB), (irow(cb), 144, IB))

        def pick(ref, cols):
            return jnp.concatenate([ref[rw, cols] for rw, _, _ in parts], axis=0)

        every = slice(0, D)
        texts = jnp.concatenate([g[trow(ca), every], g[trow(cb), every]], axis=0)
        batt[0:32, :] = dot(texts, w[:, OT : OT + 256]).astype(BF)
        images = jnp.concatenate([g[irow(ca), every], g[irow(cb), every]], axis=0)
        batt[32:256, :] = dot(images, w[:, OI : OI + 256]).astype(BF)
        for h in range(2):
            cols = slice(h * 128, (h + 1) * 128)
            qt = pick(qb, cols)
            bt = batt[:, cols]
            e = jnp.exp(dot_last(kb[:, cols], qt) * SCALE)
            p = e / jnp.sum(e, axis=0, keepdims=True)
            dp = dot_last(vb[:, cols], bt)
            ds = p * (dp - jnp.sum(p * dp, axis=0, keepdims=True)) * SCALE
            ds = ds.astype(BF)
            if fresh:
                dv[:, cols] = dot(p.astype(BF), bt)
                dk[:, cols] = dot(ds, qt)
            else:
                dv[:, cols] += dot(p.astype(BF), bt)
                dk[:, cols] += dot(ds, qt)
            dq = rms_back(pick(pq, cols), dot_rows(ds, kb[:, cols])).astype(BF)
            for rw, off, size in parts:
                bq[rw, cols] = dq[off : off + size, :]

    def finish(i):
        rows = pl.ds(m16(i * 256), 256)
        for h in range(2):
            cols = slice(h * 128, (h + 1) * 128)
            kcols = slice(256 + h * 128, 384 + h * 128)
            bq[rows, kcols] = rms_back(pq[rows, kcols], dk[rows, cols]).astype(BF)
            bq[rows, 512 + h * 128 : 640 + h * 128] = dv[rows, cols].astype(BF)

    def run(step, *args):
        step(*args)

    run(backward, c, yc, True)
    g_recv(3)
    g_send(7)
    g_recv(4)
    g_send(8)
    run(backward, c_zm, c_zp, False)
    g_recv(9, 10)
    run(backward, y_zm, y_zp, False)
    g_recv(7, 8, 11)
    grad_range(0, 0, 2)
    grad_far(0)
    run(backward, c_z2, y_z2, False)
    each(0, 4, finish)
    grad_range(0, 2, 8)
    grad_near(0)

    for cp in sent_g:
        cp.wait_send()
    slopes = [
        pltpu.make_async_copy(slo_t.at[0], g.at[pl.ds(768, TB)], loc.at[8]),
        pltpu.make_async_copy(slo_i.at[0], g.at[pl.ds(784, IB)], loc.at[9]),
    ]
    for cp in slopes:
        cp.start()

    for gi in (1, 2):
        grad_range(gi, 0, 2)
        grad_far(gi)
        grad_range(gi, 2, 8)
        if gi == 1:
            mixed_stage(0)
    grad_near(1)
    mixed_stage(1)
    mixed_stage(2)
    grad_near(2)
    grad_yh(0)

    def turn(p):
        mrow = pl.ds(m16(lax.rem(p, 2) * 384), 384)
        mcol = pl.ds(pl.multiple_of(p // 2 * 128, 128), 128)
        flat = jnp.transpose(pq[mrow, mcol])
        ms[0, :, pl.ds(pl.multiple_of(p * 384, 128), 384)] = flat[0:8, :]

    each(0, 8, turn)
    grad_yh(1)

    for i, (off, size) in enumerate(((0, TB), (TB, IB))):
        rcopy(
            st.at[pl.ds(0, size)], mland.at[3, pl.ds(off, size)], mys.at[6 + i], myr.at[6 + i], yl
        ).wait_recv()
        for n in range(3):
            rcopy(
                st.at[pl.ds(0, size)],
                mzl.at[n, pl.ds(off, size)],
                mzs.at[2 * n + i],
                mzr.at[2 * n + i],
                zp,
            ).wait_recv()
    for cp in slopes:
        cp.wait()

    def own_mixed(i, gate, acc):
        rows = own_row(i)
        q = pl.ds(m16(i * 16), 16)
        total = st[rows, :].astype(F32) + mland[3, q, :].astype(F32)
        for n in range(3):
            total = total + mzl[n, q, :].astype(F32)
        st[rows, :] = (gate * total).astype(BF)
        slope = g[pl.ds(m16(768 + i * 16), 16), :].astype(F32)
        return acc + jnp.sum(slope * total, axis=0, keepdims=True)

    zero = jnp.zeros((1, D), F32)
    ms[0, 5:6, :] = own_mixed(0, modr[5:6, :], zero)
    ms[0, 2:3, :] = zero

    def image_mixed(i):
        ms[0, 2:3, :] = own_mixed(i, modr[2:3, :], ms[0, 2:3, :])

    each(1, 8, image_mixed)
    outs = [
        pltpu.make_async_copy(st.at[trow(c)], upd_t.at[0], loc.at[10]),
        pltpu.make_async_copy(st.at[irow(c)], upd_i.at[0], loc.at[11]),
    ]
    for cp in outs:
        cp.start()

    first = rcopy(ms.at[0], ml.at[0], mss.at[0], msr.at[0], yl)
    go(first)
    first.wait_recv()
    ms[1] = ms[0] + ml[0]
    more = [
        rcopy(ms.at[1], ml.at[1 + n], mss.at[1 + n], msr.at[1 + n], dev)
        for n, dev in enumerate((zp, zm, z2))
    ]
    for cp in more:
        go(cp)
    grad_yh(2)
    for cp in more:
        cp.wait_recv()
    modsum = ms[1] + ml[1] + ml[2] + ml[3]
    ms_i[0] = modsum[0:3, :]
    ms_t[0] = modsum[3:6, :]

    for gi in range(3):
        grad_last(gi)
    for n, (c0, wide, dst) in enumerate(
        ((QI, 512, gq_i.at[:, 0:512]), (QI + 512, 256, gq_i.at[:, 512:768]),
         (QT, 256, gq_t.at[:, 0:256]), (QT + 256, 512, gq_t.at[:, 256:768]),
         (OI, 256, go_i), (OT, 256, go_t))
    ):
        src = pq.at[pl.ds(c0 // 512 * WR, WR), pl.ds(c0 % 512, wide)]
        cp = pltpu.make_async_copy(src, dst, loc.at[12 + n])
        cp.start()
        outs.append(cp)
    for cp in outs:
        cp.wait()
    for cp in sent:
        cp.wait_send()


def body(
    image_tokens,
    text_tokens,
    image_mod,
    text_mod,
    image_qkv_weight,
    text_qkv_weight,
    image_out_weight,
    text_out_weight,
    image_slope,
    text_slope,
):
    hbm = pl.BlockSpec(memory_space=pl.ANY)
    vmem = pl.BlockSpec(memory_space=pltpu.VMEM)
    dma = pltpu.SemaphoreType.DMA
    shape = jax.ShapeDtypeStruct
    upd_i, upd_t, gq_i, gq_t, go_i, go_t, ms_i, ms_t = pl.pallas_call(
        kernel,
        out_shape=(
            shape((1, IB, D), BF),
            shape((1, TB, D), BF),
            shape((WR, 768), F32),
            shape((WR, 768), F32),
            shape((WR, 256), F32),
            shape((WR, 256), F32),
            shape((1, 3, D), F32),
            shape((1, 3, D), F32),
        ),
        in_specs=[hbm] * 8 + [vmem] * 2,
        out_specs=(hbm,) * 6 + (vmem,) * 2,
        scratch_shapes=[
            pltpu.VMEM((SEQ, D), BF),
            pltpu.VMEM((SEQ, D), BF),
            pltpu.VMEM((D, WC), BF),
            pltpu.VMEM((SEQ, D), BF),
            pltpu.VMEM((SEQ, 512), F32),
            pltpu.VMEM((SEQ, 256), BF),
            pltpu.VMEM((SEQ, 256), BF),
            pltpu.VMEM((SEQ, 256), BF),
            pltpu.VMEM((SEQ, 256), BF),
            pltpu.VMEM((256, 256), BF),
            pltpu.VMEM((SEQ, 768), BF),
            pltpu.VMEM((SEQ, 256), F32),
            pltpu.VMEM((SEQ, 256), F32),
            pltpu.VMEM((8, D), F32),
            pltpu.VMEM((4, 128, D), BF),
            pltpu.VMEM((3, 128, D), BF),
            pltpu.VMEM((8, WR, WC), BF),
            pltpu.VMEM((8, 384, 512), BF),
            pltpu.VMEM((2, HALF, WC), BF),
            pltpu.VMEM((2, HALF, WC), BF),
            pltpu.VMEM((2, 2, WR, WC), BF),
            pltpu.VMEM((WR, WC), BF),
            pltpu.VMEM((2, 8, D), F32),
            pltpu.VMEM((4, 8, D), F32),
            dma((19,)),
            dma((19,)),
            dma((19,)),
            dma((19,)),
            dma((17,)),
            dma((17,)),
            dma((8,)),
            dma((8,)),
            dma((6,)),
            dma((6,)),
            dma((24,)),
            dma((24,)),
            dma((27,)),
            dma((27,)),
            dma((4,)),
            dma((4,)),
            dma((18,)),
        ],
        compiler_params=pltpu.CompilerParams(
            collective_id=0, has_side_effects=True, vmem_limit_bytes=63 * 2**20
        ),
    )(
        image_tokens,
        text_tokens,
        image_slope,
        text_slope,
        image_qkv_weight.reshape(WR, 768),
        text_qkv_weight.reshape(WR, 768),
        image_out_weight.reshape(WR, 256),
        text_out_weight.reshape(WR, 256),
        image_mod,
        text_mod,
    )
    return (
        upd_i,
        upd_t,
        gq_i.reshape(WR, 3, 2, 128),
        gq_t.reshape(WR, 3, 2, 128),
        go_i.reshape(WR, 2, 128),
        go_t.reshape(WR, 2, 128),
        ms_i,
        ms_t,
    )


def solution(mesh):
    tokens = P("dp", "context", None)
    mods = P("dp", None, None)
    qkv = P("dp", None, "context", None)
    return jax.shard_map(
        body,
        mesh=mesh,
        in_specs=(tokens, tokens, mods, mods, qkv, qkv, tokens, tokens, tokens, tokens),
        out_specs=(tokens, tokens, qkv, qkv, tokens, tokens, mods, mods),
        check_vma=False,
    )
```

```python
import jax
import jax.numpy as jnp
from jax import lax
from jax.experimental import pallas as pl
from jax.experimental.pallas import tpu as pltpu
from jax.sharding import PartitionSpec as P

EPS = 1e-06
BF = jnp.bfloat16
F32 = jnp.float32
D = 3072
TXT = 128
SEQ = 1024
TB = 16
IB = 112
WR = 192
HALF = 96
MC = 1536
SCALE = 128 ** (-0.5)
QI, QT, OI, OT, WC = 0, 768, 1536, 1792, 2048
GROUPS = ((OI, 512), (QI, 768), (QT, 768))


def dot(a, b):
    return jnp.dot(a, b, preferred_element_type=F32)


def dot_last(a, b):
    return lax.dot_general(a, b, (((1,), (1,)), ((), ())), preferred_element_type=F32)


def dot_rows(a, b):
    return lax.dot_general(a, b, (((0,), (0,)), ((), ())), preferred_element_type=F32)


def each(low, high, step):
    lax.fori_loop(low, high, lambda i, _: (step(i), 0)[1], 0)


each_io = each


def m16(v):
    return pl.multiple_of(v, 16)


def kernel(
    tok_i,
    tok_t,
    slo_i,
    slo_t,
    wq_i,
    wq_t,
    wo_i,
    wo_t,
    mod_i,
    mod_t,
    upd_i,
    upd_t,
    gq_i,
    gq_t,
    go_i,
    go_t,
    ms_i,
    ms_t,
    xn,
    g,
    w,
    st,
    pq,
    qb,
    kb,
    vb,
    att,
    batt,
    bq,
    dk,
    dv,
    modr,
    mland,
    mzl,
    zland,
    yland,
    sland,
    so,
    ha,
    hb,
    xl,
    yhl,
    ms,
    ml,
    xs,
    xr,
    gs,
    gr,
    ws,
    wr,
    mys,
    myr,
    mzs,
    mzr,
    ss,
    sr,
    rs,
    rr,
    mss,
    msr,
    loc,
):
    d = lax.axis_index("dp")
    c = lax.axis_index("context")
    core = lax.rem(d, 2)
    yh = lax.rem(d // 2, 2)
    xpos = d // 4
    c_zp, c_zm, c_z2 = lax.rem(c + 2, 8), lax.rem(c + 6, 8), lax.rem(c + 4, 8)
    ylflip = 1 - 2 * lax.rem(c, 2)
    d_xp, d_xm, d_x2 = lax.rem(d + 4, 16), lax.rem(d + 12, 16), lax.rem(d + 8, 16)
    yhflip = 2 - 4 * yh
    zp, zm, z2, yl = (d, c_zp), (d, c_zm), (d, c_z2), (d, c + ylflip)
    xp, xm, yhp, sib = (d_xp, c), (d_xm, c), (d + yhflip, c), (d + 1 - 2 * core, c)

    def rcopy(src, dst, ssem, rsem, dev):
        return pltpu.make_async_remote_copy(
            src_ref=src,
            dst_ref=dst,
            send_sem=ssem,
            recv_sem=rsem,
            device_id=dev,
            device_id_type=pl.DeviceIdType.MESH,
        )

    def trow(cc):
        return pl.ds(m16(cc * TB), TB)

    def irow(cc, off=0, n=IB):
        return pl.ds(m16(TXT + cc * IB + off), n)

    sent = []
    sent_g = []
    outs = []

    def go(cp, kept=sent):
        cp.start()
        kept.append(cp)

    pieces = tuple((r, p, q, 6) for r, q in ((wq_i, QI), (wq_t, QT)) for p in range(3))
    pieces += ((wo_i, 0, OI, 2), (wo_t, 0, OT, 2))
    locs = [
        pltpu.make_async_copy(src, dst, loc.at[n])
        for n, (src, dst) in enumerate(
            (
                (tok_t.at[0], xn.at[trow(c)]),
                (tok_i.at[0], xn.at[irow(c)]),
                (slo_t.at[0], g.at[trow(c)]),
                (slo_i.at[0], g.at[irow(c)]),
            )
            + tuple(
                (ref.at[pl.ds(384 * p, 384)], so.at[k, :, 0:128])
                for k, (ref, p, _, _) in enumerate(pieces)
            )
        )
    ]
    for cp in locs:
        cp.start()
    bar = pltpu.get_barrier_semaphore()
    peers = (zp, zm, z2, yl, xp, xm, yhp, sib)
    for dev in peers:
        pl.semaphore_signal(bar, inc=1, device_id=dev, device_id_type=pl.DeviceIdType.MESH)
    modr[...] = jnp.zeros_like(modr)
    modr[0:3, :] = mod_i[0].astype(F32)
    modr[3:6, :] = mod_t[0].astype(F32)
    modr[1:2, :] = modr[1:2, :] + 1.0
    modr[4:5, :] = modr[4:5, :] + 1.0
    for cp in locs:
        cp.wait()

    for k, (_, p, col, heads) in enumerate(pieces):
        r0, n = k // 4 * 384, 384 // heads
        pq[k % 4, r0 : r0 + 384, :] = so[k, :, 0:128].astype(F32)
        rows = pl.ds(m16(d * WR + p * n), n)
        for j in range(heads):
            part = pq[k % 4, pl.ds(r0 + j, n, stride=heads), :]
            w[rows, col + j * 128 : col + (j + 1) * 128] = part.astype(BF)

    def own_row(i):
        return pl.ds(m16(jnp.where(i == 0, c * TB, TXT + c * IB + (i - 1) * 16)), 16)

    def norm_rows(i):
        rows = own_row(i)
        v = xn[rows, :].astype(F32)
        v = v - jnp.mean(v, axis=-1, keepdims=True)
        v = v * lax.rsqrt(jnp.mean(v * v, axis=-1, keepdims=True) + EPS)
        xn[rows, :] = v.astype(BF)

    each(0, 8, norm_rows)
    pl.semaphore_wait(bar, len(peers))

    def full(cc):
        return (trow(cc), irow(cc))

    def half_a(cc):
        return (irow(cc, 0, 64),)

    def half_b(cc):
        return (irow(cc, 64, 48), trow(cc))

    def main(cc):
        return (trow(cc), irow(cc, 0, 80))

    def main_a(cc):
        return (irow(cc, 0, 48),)

    def main_b(cc):
        return (irow(cc, 48, 32), trow(cc))

    def edge(cc):
        return (irow(cc, 80, 32),)

    yc = c + ylflip
    y_zp, y_zm, y_z2 = c_zp + ylflip, c_zm + ylflip, c_z2 + ylflip
    plan = (
        (0, yl, full(c), full(yc)),
        (2, zp, full(c), full(c_zm)),
        (4, zm, full(c), full(c_zp)),
        (6, zp, main(yc), main(y_zm)),
        (8, zm, main(yc), main(y_zp)),
        (10, zp, half_a(c_zm), half_a(c_z2)),
        (11, zm, half_b(c_zp), half_b(c_z2)),
        (13, zp, main_a(y_zm), main_a(y_z2)),
        (14, zm, main_b(y_zp), main_b(y_z2)),
        (16, yl, edge(c_zm), edge(y_zm)),
        (17, yl, edge(c_zp), edge(y_zp)),
        (18, yl, edge(c_z2), edge(y_z2)),
    )

    def ctx_send(buf, s, r, n):
        first, dev, rows, _ = plan[n]
        for i, rw in enumerate(rows):
            cp = rcopy(buf.at[rw], buf.at[rw], s.at[first + i], r.at[first + i], dev)
            go(cp, sent_g if buf is g else sent)

    def ctx_recv(buf, s, r, n):
        first, dev, _, rows = plan[n]
        for i, rw in enumerate(rows):
            rcopy(buf.at[rw], buf.at[rw], s.at[first + i], r.at[first + i], dev).wait_recv()

    def wrow(dd, off=0, n=WR):
        return pl.ds(m16(dd * WR + off), n)

    wplan = (
        (yhp, wrow(d), wrow(d + yhflip)),
        (xp, wrow(d), wrow(d_xm)),
        (xm, wrow(d), wrow(d_xp)),
        (xp, wrow(d + yhflip), wrow(d_xm + yhflip)),
        (xm, wrow(d + yhflip), wrow(d_xp + yhflip)),
        (xp, wrow(d_xm, 0, HALF), wrow(d_x2, 0, HALF)),
        (xm, wrow(d_xp, HALF, HALF), wrow(d_x2, HALF, HALF)),
        (xp, wrow(d_xm + yhflip, 0, HALF), wrow(d_x2 + yhflip, 0, HALF)),
        (xm, wrow(d_xp + yhflip, HALF, HALF), wrow(d_x2 + yhflip, HALF, HALF)),
    ) + tuple(
        (sib, wrow(b), wrow(b + 1 - 2 * core))
        for b in (
            d,
            d + yhflip,
            d_xm,
            d_xp,
            d_xm + yhflip,
            d_xp + yhflip,
            d_x2,
            d_x2 + yhflip,
        )
    )

    def w_send(*ns):
        for n in ns:
            dev, rows, _ = wplan[n]
            go(rcopy(w.at[rows], w.at[rows], ws.at[n], wr.at[n], dev))

    def w_recv(*ns):
        for n in ns:
            dev, _, rows = wplan[n]
            rcopy(w.at[rows], w.at[rows], ws.at[n], wr.at[n], dev).wait_recv()

    def x_send(*ns):
        for n in ns:
            ctx_send(xn, xs, xr, n)

    def x_recv(*ns):
        for n in ns:
            ctx_recv(xn, xs, xr, n)

    def g_send(*ns):
        for n in ns:
            ctx_send(g, gs, gr, n)

    def g_recv(*ns):
        for n in ns:
            ctx_recv(g, gs, gr, n)

    x_send(1, 2)
    w_send(0, 1, 2, 9)

    def gate_rows(i):
        rows = own_row(i)
        gate = jnp.where(i == 0, modr[5:6, :], modr[2:3, :])
        g[rows, :] = (gate * g[rows, :].astype(F32)).astype(BF)

    each(0, 8, gate_rows)

    def modulate(start, count, text):
        def step(i):
            rows = pl.ds(m16(start + i * 16), 16)
            base = 3 if text else 0
            v = xn[rows, :].astype(F32)
            st[rows, :] = (modr[base + 1 : base + 2, :] * v + modr[base : base + 1, :]).astype(BF)

        each(0, count // 16, step)

    def modulate_block(cc):
        modulate(cc * TB, TB, True)
        modulate(TXT + cc * IB, IB, False)

    modulate_block(c)
    x_recv(1)
    x_send(5)
    x_recv(2)
    x_send(6)
    w_recv(1)
    w_send(5, 11)
    w_recv(2)
    w_send(6, 12)
    w_recv(0)
    w_send(3, 4, 10)
    x_send(0, 9, 10)
    g_send(1, 2)
    modulate_block(c_zm)
    modulate_block(c_zp)
    x_recv(5, 6)
    x_send(11)
    w_recv(5, 6)
    w_send(15)
    x_recv(0)
    x_send(3, 4)
    g_send(0)
    modulate_block(c_z2)
    modulate_block(yc)
    w_recv(3)
    w_send(7, 13)
    w_recv(4)
    w_send(8, 14)
    g_recv(1)
    g_send(5, 9)
    g_recv(2)
    g_send(6, 10)
    x_recv(3)
    x_send(7)
    x_recv(4)
    x_send(8)
    x_recv(9, 10)
    modulate_block(y_zm)
    modulate_block(y_zp)
    w_recv(7, 8)
    w_send(16)
    g_recv(0)
    g_send(3, 4)
    x_recv(7, 8, 11)
    modulate_block(y_z2)
    g_recv(5, 6)
    g_send(11)
    w_recv(9, 10, 11, 12, 13, 14, 15, 16)

    def project(rows, col):
        left = st[rows, :]
        for j, out in enumerate((qb, kb, vb)):
            acc = dot(left, w[:, col + j * 256 : col + (j + 1) * 256])
            if j == 2:
                out[rows, :] = acc.astype(BF)
                continue
            for h in range(2):
                a = acc[:, h * 128 : (h + 1) * 128]
                pq[2 * j + h, rows, :] = a
                f = lax.rsqrt(jnp.mean(a * a, axis=-1, keepdims=True) + EPS)
                out[rows, h * 128 : (h + 1) * 128] = (a * f).astype(BF)

    def project_image(i):
        project(pl.ds(m16(TXT + i * 448), 448), QI)

    each(0, 2, project_image)
    project(pl.ds(0, TXT), QT)

    for h in range(2):
        cols = slice(h * 128, (h + 1) * 128)

        def forward(i, cols=cols):
            rows = pl.ds(m16(i * 256), 256)
            e = jnp.exp(dot_last(qb[rows, cols], kb[:, cols]) * SCALE)
            p = e / jnp.sum(e, axis=-1, keepdims=True)
            att[rows, cols] = dot(p.astype(BF), vb[:, cols]).astype(BF)

        each(0, 4, forward)

    def mix(i):
        n = pl.ds(pl.multiple_of(i * 512, 512), 512)
        st[0:TXT, n] = dot_last(att[0:TXT, :], w[n, OT : OT + 256]).astype(BF)
        st[TXT:576, n] = dot_last(att[TXT:576, :], w[n, OI : OI + 256]).astype(BF)
        st[576:SEQ, n] = dot_last(att[576:SEQ, :], w[n, OI : OI + 256]).astype(BF)

    each(0, 6, mix)

    zs = (c_z2, c_zp, c_zm, c)
    zdevs = (z2, zp, zm)
    left, right = slice(0, MC), slice(MC, D)

    def mix_copies(block, cols, land, ssem, rsem, first, dev):
        return [
            rcopy(st.at[rw, cols], land.at[pl.ds(off, size)], ssem.at[first + i], rsem.at[first + i], dev)
            for i, (rw, off, size) in enumerate(((trow(block), 0, TB), (irow(block), TB, IB)))
        ]

    def left_y(n):
        return mix_copies(zs[n] + ylflip, left, mland.at[n], mys, myr, 2 * n, yl)

    def left_z(n):
        return mix_copies(zs[n], left, mzl.at[n], mzs, mzr, 2 * n, zdevs[n])

    def right_z(n, v):
        block = zs[n] if v else zs[n] + ylflip
        return mix_copies(block, right, zland.at[n, v], mzs, mzr, 6 + 4 * n + 2 * v, zdevs[n])

    def right_y():
        return mix_copies(yc, right, yland, mys, myr, 8, yl)

    def start_all(cps):
        for cp in cps:
            go(cp)

    def recv_all(cps):
        for cp in cps:
            cp.wait_recv()

    def block_row(cc, i):
        return pl.ds(m16(jnp.where(i == 0, cc * TB, TXT + cc * IB + (i - 1) * 16)), 16)

    for n in range(4):
        start_all(left_y(n))

    def mixed_left(n):
        recv_all(left_y(n))

        def step(i):
            rows = block_row(zs[n], i)
            land = mland[n, pl.ds(m16(i * 16), 16), :].astype(F32)
            st[rows, left] = (st[rows, left].astype(F32) + land).astype(BF)

        each(0, 8, step)
        start_all(left_z(n))

    def mixed_right():
        for n in range(3):
            recv_all(right_z(n, 0))

        def step(i):
            rows = block_row(yc, i)
            total = st[rows, right].astype(F32)
            for n in range(3):
                total = total + zland[n, 0, pl.ds(m16(i * 16), 16), :].astype(F32)
            st[rows, right] = total.astype(BF)

        each(0, 8, step)
        start_all(right_y())

    def chip(k):
        j = k // 2
        dx = jnp.where(j == 0, 2, jnp.where(j == 1, 1, jnp.where(j == 2, 3, 0)))
        yy = jnp.where(lax.rem(k, 2) == 0, 1 - yh, yh)
        return lax.rem(xpos + dx, 4) * 2 + yy

    def out_tile(k):
        cols = pl.ds(pl.multiple_of(chip(k) * 384, 128), 384)
        so[k, :, 0:256] = dot_rows(g[TXT:SEQ, cols], att[TXT:SEQ, :]).astype(BF)
        so[k, :, 256:512] = dot_rows(g[0:TXT, cols], att[0:TXT, :]).astype(BF)

    def stage_cols(k):
        return pl.ds(pl.multiple_of(lax.rem(k, 4) * 768, 256), 768)

    def qkv_tile(k, text):
        p = chip(k)
        cols = pl.ds(pl.multiple_of(p * 384, 128), 384)
        rows = slice(0, TXT) if text else slice(TXT, SEQ)
        base = 3 if text else 0
        wcol = QT if text else QI
        back = bq[rows, :]
        grad = dot_rows(xn[rows, cols], back)
        total = jnp.sum(back.astype(F32), axis=0, keepdims=True)
        own = w[pl.ds(m16(p * 384), 384), wcol : wcol + 768].astype(F32)
        shift_part = jnp.sum(own * total, axis=-1, keepdims=True)
        scale_part = jnp.sum(own * grad, axis=-1, keepdims=True)
        lane = lax.broadcasted_iota(jnp.int32, (384, 128), 1)
        vals = jnp.where(lane == base, shift_part, jnp.where(lane == base + 1, scale_part, 0.0))
        mrow = pl.ds(m16(lax.rem(p, 2) * 384), 384)
        mcol = p // 2
        if text:
            vals = vals + pq[mcol, mrow, :]
        pq[mcol, mrow, :] = vals
        mod = jnp.transpose(modr[:, cols])
        full_grad = mod[:, base + 1 : base + 2] * grad + mod[:, base : base + 1] * total
        g[pl.ds(m16(k // 4 * 384), 384), stage_cols(k)] = full_grad.astype(BF)

    def stage(gi, k, half):
        rows = half * WR
        if gi == 0:
            return so.at[k, pl.ds(m16(rows), WR)]
        return g.at[pl.ds(m16(k // 4 * 384 + rows), WR), stage_cols(k)]

    def to_sib(gi, k):
        c0, n = GROUPS[gi]
        return rcopy(
            stage(gi, k, 1 - core),
            sland.at[k, :, c0 : c0 + n],
            ss.at[gi * 8 + k],
            sr.at[gi * 8 + k],
            sib,
        )

    def grad_range(gi, k0, k1):
        c0, n = GROUPS[gi]

        def compute(k):
            if gi == 0:
                out_tile(k)
            else:
                qkv_tile(k, gi == 2)
            to_sib(gi, k).start()

        each_io(k0, k1, compute)

        def combine(k):
            to_sib(gi, k).wait()

            def step(i):
                r = pl.ds(m16(i * 32), 32)
                if gi == 0:
                    mine = so[k, pl.ds(m16(core * WR + i * 32), 32), :]
                else:
                    mine = g[pl.ds(m16(k // 4 * 384 + core * WR + i * 32), 32), stage_cols(k)]
                land = sland[k, r, c0 : c0 + n].astype(F32)
                sland[k, r, c0 : c0 + n] = (mine.astype(F32) + land).astype(BF)

            each(0, 6, step)

        each_io(k0, k1, combine)

    def gcopy(gi, n, src, dst, dev):
        return rcopy(src, dst, rs.at[gi * 9 + n], rr.at[gi * 9 + n], dev)

    def far_copy(gi, v, side):
        c0, n = GROUPS[gi]
        cs = slice(c0, c0 + n)
        src = sland.at[v, pl.ds(side * HALF, HALF), cs]
        dst = (ha, hb)[side].at[v, :, cs]
        return gcopy(gi, 2 * v + side, src, dst, (xp, xm)[side])

    def near_copy(gi, v, side):
        c0, n = GROUPS[gi]
        cs = slice(c0, c0 + n)
        src = sland.at[2 + 2 * side + v, :, cs]
        return gcopy(gi, 4 + 2 * v + side, src, xl.at[side, v, :, cs], (xp, xm)[side])

    def yh_copy(gi):
        c0, n = GROUPS[gi]
        cs = slice(c0, c0 + n)
        return gcopy(gi, 8, sland.at[6, :, cs], yhl.at[:, cs], yhp)

    def grad_far(gi):
        for v in range(2):
            for side in range(2):
                go(far_copy(gi, v, side))

    def grad_near(gi):
        c0, n = GROUPS[gi]
        cs = slice(c0, c0 + n)
        for v in range(2):
            for side, land in ((0, ha), (1, hb)):
                far_copy(gi, v, side).wait_recv()
                k = 2 + 2 * side + v

                def step(i, land=land, k=k, side=side, v=v):
                    r = pl.ds(m16(side * HALF + i * 32), 32)
                    q = pl.ds(m16(i * 32), 32)
                    sland[k, r, cs] = (
                        sland[k, r, cs].astype(F32) + land[v, q, cs].astype(F32)
                    ).astype(BF)

                each(0, 3, step)
                go(near_copy(gi, v, side))

    def grad_yh(gi):
        c0, n = GROUPS[gi]
        cs = slice(c0, c0 + n)
        near_copy(gi, 0, 0).wait_recv()
        near_copy(gi, 0, 1).wait_recv()

        def step(i):
            r = pl.ds(m16(i * 32), 32)
            total = sland[6, r, cs].astype(F32) + xl[0, 0, r, cs].astype(F32)
            sland[6, r, cs] = (total + xl[1, 0, r, cs].astype(F32)).astype(BF)

        each(0, 6, step)
        go(yh_copy(gi))

    def grad_last(gi):
        c0, n = GROUPS[gi]
        near_copy(gi, 1, 0).wait_recv()
        near_copy(gi, 1, 1).wait_recv()
        yh_copy(gi).wait_recv()
        heads = 6 if gi else 2
        for b in range(n // 128):
            cs = slice(c0 + b * 128, c0 + (b + 1) * 128)
            for i in range(6):
                r = slice(i * 32, (i + 1) * 32)
                total = sland[7, r, cs].astype(F32) + xl[0, 1, r, cs].astype(F32)
                total = total + xl[1, 1, r, cs].astype(F32) + yhl[r, cs].astype(F32)
                if gi == 0:
                    dk[b // 2, pl.ds(i * 64 + b % 2, 32, stride=heads), :] = total
                else:
                    part = (gi - 1) * 2 + i // 3
                    pq[part, pl.ds(i % 3 * 192 + b, 32, stride=heads), :] = total
        if gi == 0:
            moves = [(dk.at[0, 0:384], go_i), (dk.at[1, 0:384], go_t)]
        else:
            ref = (gq_i, gq_t)[gi - 1]
            part = (gi - 1) * 2
            moves = [
                (pq.at[part, 0:576], ref.at[0:576]),
                (pq.at[part + 1, 0:576], ref.at[576:1152]),
            ]
        for i, (src, dst) in enumerate(moves):
            cp = pltpu.make_async_copy(src, dst, loc.at[16 + 2 * gi + i])
            cp.start()
            outs.append(cp)

    def rms_back(a, slope):
        f = lax.rsqrt(jnp.mean(a * a, axis=-1, keepdims=True) + EPS)
        normal = a * f
        return f * (slope - normal * jnp.mean(slope * normal, axis=-1, keepdims=True))

    def backward(ca, cb, fresh):
        parts = ((trow(ca), 0, TB), (trow(cb), 16, TB), (irow(ca), 32, IB), (irow(cb), 144, IB))

        def pick(ref, cols):
            return jnp.concatenate([ref[rw, cols] for rw, _, _ in parts], axis=0)

        every = slice(0, D)
        texts = jnp.concatenate([g[trow(ca), every], g[trow(cb), every]], axis=0)
        batt[0:32, :] = dot(texts, w[:, OT : OT + 256]).astype(BF)
        images = jnp.concatenate([g[irow(ca), every], g[irow(cb), every]], axis=0)
        batt[32:256, :] = dot(images, w[:, OI : OI + 256]).astype(BF)
        for h in range(2):
            cols = slice(h * 128, (h + 1) * 128)
            qt = pick(qb, cols)
            bt = batt[:, cols]
            e = jnp.exp(dot_last(kb[:, cols], qt) * SCALE)
            p = e / jnp.sum(e, axis=0, keepdims=True)
            dp = dot_last(vb[:, cols], bt)
            ds = p * (dp - jnp.sum(p * dp, axis=0, keepdims=True)) * SCALE
            ds = ds.astype(BF)
            if fresh:
                dv[h] = dot(p.astype(BF), bt)
                dk[h] = dot(ds, qt)
            else:
                dv[h] += dot(p.astype(BF), bt)
                dk[h] += dot(ds, qt)
            dq = rms_back(pick(pq.at[h], slice(0, 128)), dot_rows(ds, kb[:, cols])).astype(BF)
            for rw, off, size in parts:
                bq[rw, cols] = dq[off : off + size, :]

    def finish(i):
        rows = pl.ds(m16(i * 256), 256)
        for h in range(2):
            kcols = slice(256 + h * 128, 384 + h * 128)
            bq[rows, kcols] = rms_back(pq[2 + h, rows, :], dk[h, rows, :]).astype(BF)
            bq[rows, 512 + h * 128 : 640 + h * 128] = dv[h, rows, :].astype(BF)

    def run(step, *args):
        step(*args)

    run(backward, c, yc, True)
    g_recv(3)
    g_send(7)
    g_recv(4)
    g_send(8)
    run(backward, c_zm, c_zp, False)
    g_recv(9, 10)
    run(backward, y_zm, y_zp, False)
    g_recv(7, 8, 11)
    for n in range(3):
        start_all(right_z(n, 0))
    for n in range(3):
        start_all(right_z(n, 1))
    grad_range(0, 0, 2)
    grad_far(0)
    run(backward, c_z2, y_z2, False)
    each(0, 4, finish)
    grad_range(0, 2, 8)
    mixed_left(0)
    grad_near(0)

    for cp in sent_g:
        cp.wait_send()
    slopes = [
        pltpu.make_async_copy(slo_t.at[0], g.at[pl.ds(768, TB)], loc.at[12]),
        pltpu.make_async_copy(slo_i.at[0], g.at[pl.ds(784, IB)], loc.at[13]),
    ]
    for cp in slopes:
        cp.start()

    for gi in (1, 2):
        grad_range(gi, 0, 2)
        grad_far(gi)
        grad_range(gi, 2, 8)
        mixed_left(gi)
    grad_near(1)
    grad_near(2)
    grad_yh(0)

    def turn(p):
        mrow = pl.ds(m16(lax.rem(p, 2) * 384), 384)
        mcol = p // 2
        flat = jnp.transpose(pq[mcol, mrow, :])
        ms[0, :, pl.ds(pl.multiple_of(p * 384, 128), 384)] = flat[0:8, :]

    each(0, 8, turn)
    mixed_right()
    grad_last(0)
    grad_yh(1)
    grad_yh(2)

    recv_all(left_y(3))
    for n in range(3):
        recv_all(left_z(n))
        recv_all(right_z(n, 1))
    recv_all(right_y())
    for cp in slopes:
        cp.wait()

    def own_mixed(i, gate):
        rows = own_row(i)
        q = pl.ds(m16(i * 16), 16)
        for cols, others in ((left, (mland.at[3], mzl.at[0], mzl.at[1], mzl.at[2])),
                             (right, (yland, zland.at[0, 1], zland.at[1, 1], zland.at[2, 1]))):
            total = st[rows, cols].astype(F32)
            for other in others:
                total = total + other[q, :].astype(F32)
            st[rows, cols] = (modr[gate : gate + 1, cols] * total).astype(BF)
            slope = g[pl.ds(m16(768 + i * 16), 16), cols].astype(F32)
            ms[0, gate : gate + 1, cols] += jnp.sum(slope * total, axis=0, keepdims=True)

    own_mixed(0, 5)
    each(1, 8, lambda i: own_mixed(i, 2))
    for cp in (
        pltpu.make_async_copy(st.at[trow(c)], upd_t.at[0], loc.at[14]),
        pltpu.make_async_copy(st.at[irow(c)], upd_i.at[0], loc.at[15]),
    ):
        cp.start()
        outs.append(cp)

    first = rcopy(ms.at[0], ml.at[0], mss.at[0], msr.at[0], yl)
    go(first)
    first.wait_recv()
    ms[1] = ms[0] + ml[0]
    more = [
        rcopy(ms.at[1], ml.at[1 + n], mss.at[1 + n], msr.at[1 + n], dev)
        for n, dev in enumerate((zp, zm, z2))
    ]
    for cp in more:
        go(cp)
    grad_last(1)
    for cp in more:
        cp.wait_recv()
    modsum = ms[1] + ml[1] + ml[2] + ml[3]
    ms_i[0] = modsum[0:3, :]
    ms_t[0] = modsum[3:6, :]

    grad_last(2)
    for cp in outs:
        cp.wait()
    for cp in sent:
        cp.wait_send()


def deliver(*refs):
    for n in range(6):
        refs[8 + n][...] = refs[n][...]
    for n in (6, 7):
        for row in range(3):
            for j in range(24):
                line = refs[n][0, row : row + 1, j * 128 : (j + 1) * 128]
                refs[8 + n][row * 24 + j : row * 24 + j + 1, :] = line


def body(
    image_tokens,
    text_tokens,
    image_mod,
    text_mod,
    image_qkv_weight,
    text_qkv_weight,
    image_out_weight,
    text_out_weight,
    image_slope,
    text_slope,
):
    hbm = pl.BlockSpec(memory_space=pl.ANY)
    vmem = pl.BlockSpec(memory_space=pltpu.VMEM)
    dma = pltpu.SemaphoreType.DMA
    shape = jax.ShapeDtypeStruct
    results = pl.pallas_call(
        kernel,
        out_shape=(
            shape((1, IB, D), BF),
            shape((1, TB, D), BF),
            shape((WR * 6, 128), F32),
            shape((WR * 6, 128), F32),
            shape((WR * 2, 128), F32),
            shape((WR * 2, 128), F32),
            shape((1, 3, D), F32),
            shape((1, 3, D), F32),
        ),
        in_specs=[hbm] * 8 + [vmem] * 2,
        out_specs=(hbm,) * 6 + (vmem,) * 2,
        scratch_shapes=[
            pltpu.VMEM((SEQ, D), BF),
            pltpu.VMEM((SEQ, D), BF),
            pltpu.VMEM((D, WC), BF),
            pltpu.VMEM((SEQ, D), BF),
            pltpu.VMEM((4, SEQ, 128), F32),
            pltpu.VMEM((SEQ, 256), BF),
            pltpu.VMEM((SEQ, 256), BF),
            pltpu.VMEM((SEQ, 256), BF),
            pltpu.VMEM((SEQ, 256), BF),
            pltpu.VMEM((256, 256), BF),
            pltpu.VMEM((SEQ, 768), BF),
            pltpu.VMEM((2, SEQ, 128), F32),
            pltpu.VMEM((2, SEQ, 128), F32),
            pltpu.VMEM((8, D), F32),
            pltpu.VMEM((4, 128, MC), BF),
            pltpu.VMEM((3, 128, MC), BF),
            pltpu.VMEM((3, 2, 128, D - MC), BF),
            pltpu.VMEM((128, D - MC), BF),
            pltpu.VMEM((8, WR, WC), BF),
            pltpu.VMEM((8, 384, 512), BF),
            pltpu.VMEM((2, HALF, WC), BF),
            pltpu.VMEM((2, HALF, WC), BF),
            pltpu.VMEM((2, 2, WR, WC), BF),
            pltpu.VMEM((WR, WC), BF),
            pltpu.VMEM((2, 8, D), F32),
            pltpu.VMEM((4, 8, D), F32),
            dma((19,)),
            dma((19,)),
            dma((19,)),
            dma((19,)),
            dma((17,)),
            dma((17,)),
            dma((10,)),
            dma((10,)),
            dma((18,)),
            dma((18,)),
            dma((24,)),
            dma((24,)),
            dma((27,)),
            dma((27,)),
            dma((4,)),
            dma((4,)),
            dma((22,)),
        ],
        compiler_params=pltpu.CompilerParams(
            collective_id=0, has_side_effects=True, vmem_limit_bytes=63 * 2**20
        ),
    )(
        image_tokens,
        text_tokens,
        image_slope,
        text_slope,
        image_qkv_weight.reshape(WR * 6, 128),
        text_qkv_weight.reshape(WR * 6, 128),
        image_out_weight.reshape(WR * 2, 128),
        text_out_weight.reshape(WR * 2, 128),
        image_mod,
        text_mod,
    )
    upd_i, upd_t, gq_i, gq_t, go_i, go_t, ms_i, ms_t = pl.pallas_call(
        deliver,
        out_shape=tuple(shape(v.shape, v.dtype) for v in results[:6]) + (shape((72, 128), F32),) * 2,
        in_specs=[vmem] * 8,
        out_specs=(vmem,) * 8,
        compiler_params=pltpu.CompilerParams(vmem_limit_bytes=16 * 2**20),
    )(*results)
    return (
        upd_i,
        upd_t,
        gq_i.reshape(WR, 3, 2, 128),
        gq_t.reshape(WR, 3, 2, 128),
        go_i.reshape(WR, 2, 128),
        go_t.reshape(WR, 2, 128),
        ms_i.reshape(1, 3, D),
        ms_t.reshape(1, 3, D),
    )


def solution(mesh):
    tokens = P("dp", "context", None)
    mods = P("dp", None, None)
    qkv = P("dp", None, "context", None)
    return jax.shard_map(
        body,
        mesh=mesh,
        in_specs=(tokens, tokens, mods, mods, qkv, qkv, tokens, tokens, tokens, tokens),
        out_specs=(tokens, tokens, qkv, qkv, tokens, tokens, mods, mods),
        check_vma=False,
    )
```

```python
import jax
import jax.numpy as jnp
from jax import lax
from jax.experimental import pallas as pl
from jax.experimental.pallas import tpu as pltpu
from jax.sharding import PartitionSpec as P

EPS = 1e-06
BF = jnp.bfloat16
F32 = jnp.float32
D = 3072
TXT = 128
SEQ = 1024
TB = 16
IB = 112
WR = 192
HALF = 96
MC = 1536
SCALE = 128 ** (-0.5)
QI, QT, OI, OT, WC = 0, 768, 1536, 1792, 2048
GROUPS = ((OI, 512), (QI, 768), (QT, 768))


def dot(a, b):
    return jnp.dot(a, b, preferred_element_type=F32)


def dot_last(a, b):
    return lax.dot_general(a, b, (((1,), (1,)), ((), ())), preferred_element_type=F32)


def dot_rows(a, b):
    return lax.dot_general(a, b, (((0,), (0,)), ((), ())), preferred_element_type=F32)


def each(low, high, step):
    lax.fori_loop(low, high, lambda i, _: (step(i), 0)[1], 0)


each_io = each


def m16(v):
    return pl.multiple_of(v, 16)


def kernel(
    tok_i,
    tok_t,
    slo_i,
    slo_t,
    wq_i,
    wq_t,
    wo_i,
    wo_t,
    mod_i,
    mod_t,
    upd_i,
    upd_t,
    gq_i,
    gq_t,
    go_i,
    go_t,
    ms_i,
    ms_t,
    xn,
    g,
    w,
    st,
    pq,
    qb,
    kb,
    vb,
    att,
    batt,
    bq,
    dk,
    dv,
    modr,
    mland,
    mzl,
    zland,
    yland,
    sland,
    so,
    ha,
    hb,
    xl,
    yhl,
    ms,
    ml,
    xs,
    xr,
    gs,
    gr,
    ws,
    wr,
    mys,
    myr,
    mzs,
    mzr,
    ss,
    sr,
    rs,
    rr,
    mss,
    msr,
    loc,
):
    d = lax.axis_index("dp")
    c = lax.axis_index("context")
    core = lax.rem(d, 2)
    yh = lax.rem(d // 2, 2)
    xpos = d // 4
    c_zp, c_zm, c_z2 = lax.rem(c + 2, 8), lax.rem(c + 6, 8), lax.rem(c + 4, 8)
    ylflip = 1 - 2 * lax.rem(c, 2)
    d_xp, d_xm, d_x2 = lax.rem(d + 4, 16), lax.rem(d + 12, 16), lax.rem(d + 8, 16)
    yhflip = 2 - 4 * yh
    zp, zm, z2, yl = (d, c_zp), (d, c_zm), (d, c_z2), (d, c + ylflip)
    xp, xm, yhp, sib = (d_xp, c), (d_xm, c), (d + yhflip, c), (d + 1 - 2 * core, c)

    def rcopy(src, dst, ssem, rsem, dev):
        return pltpu.make_async_remote_copy(
            src_ref=src,
            dst_ref=dst,
            send_sem=ssem,
            recv_sem=rsem,
            device_id=dev,
            device_id_type=pl.DeviceIdType.MESH,
        )

    def trow(cc):
        return pl.ds(m16(cc * TB), TB)

    def irow(cc, off=0, n=IB):
        return pl.ds(m16(TXT + cc * IB + off), n)

    sent = []
    sent_g = []
    outs = []

    def go(cp, kept=sent):
        cp.start()
        kept.append(cp)

    pieces = tuple((r, p, q, 6) for r, q in ((wq_i, QI), (wq_t, QT)) for p in range(3))
    pieces += ((wo_i, 0, OI, 2), (wo_t, 0, OT, 2))
    locs = [
        pltpu.make_async_copy(src, dst, loc.at[n])
        for n, (src, dst) in enumerate(
            (
                (tok_t.at[0], xn.at[trow(c)]),
                (tok_i.at[0], xn.at[irow(c)]),
                (slo_t.at[0], g.at[trow(c)]),
                (slo_i.at[0], g.at[irow(c)]),
            )
            + tuple(
                (ref.at[pl.ds(384 * p, 384)], so.at[k, :, 0:128])
                for k, (ref, p, _, _) in enumerate(pieces)
            )
        )
    ]
    for cp in locs:
        cp.start()
    bar = pltpu.get_barrier_semaphore()
    peers = (zp, zm, z2, yl, xp, xm, yhp, sib)
    for dev in peers:
        pl.semaphore_signal(bar, inc=1, device_id=dev, device_id_type=pl.DeviceIdType.MESH)
    modr[...] = jnp.zeros_like(modr)
    modr[0:3, :] = mod_i[0].astype(F32)
    modr[3:6, :] = mod_t[0].astype(F32)
    modr[1:2, :] = modr[1:2, :] + 1.0
    modr[4:5, :] = modr[4:5, :] + 1.0
    for cp in locs:
        cp.wait()

    for k, (_, p, col, heads) in enumerate(pieces):
        r0, n = k // 4 * 384, 384 // heads
        pq[k % 4, r0 : r0 + 384, :] = so[k, :, 0:128].astype(F32)
        rows = pl.ds(m16(d * WR + p * n), n)
        for j in range(heads):
            part = pq[k % 4, pl.ds(r0 + j, n, stride=heads), :]
            w[rows, col + j * 128 : col + (j + 1) * 128] = part.astype(BF)

    def own_row(i):
        return pl.ds(m16(jnp.where(i == 0, c * TB, TXT + c * IB + (i - 1) * 16)), 16)

    def norm_rows(i):
        rows = own_row(i)
        v = xn[rows, :].astype(F32)
        v = v - jnp.mean(v, axis=-1, keepdims=True)
        v = v * lax.rsqrt(jnp.mean(v * v, axis=-1, keepdims=True) + EPS)
        xn[rows, :] = v.astype(BF)

    each(0, 8, norm_rows)
    pl.semaphore_wait(bar, len(peers))

    def full(cc):
        return (trow(cc), irow(cc))

    def half_a(cc):
        return (irow(cc, 0, 64),)

    def half_b(cc):
        return (irow(cc, 64, 48), trow(cc))

    def main(cc):
        return (trow(cc), irow(cc, 0, 80))

    def main_a(cc):
        return (irow(cc, 0, 48),)

    def main_b(cc):
        return (irow(cc, 48, 32), trow(cc))

    def edge(cc):
        return (irow(cc, 80, 32),)

    yc = c + ylflip
    y_zp, y_zm, y_z2 = c_zp + ylflip, c_zm + ylflip, c_z2 + ylflip
    plan = (
        (0, yl, full(c), full(yc)),
        (2, zp, full(c), full(c_zm)),
        (4, zm, full(c), full(c_zp)),
        (6, zp, main(yc), main(y_zm)),
        (8, zm, main(yc), main(y_zp)),
        (10, zp, half_a(c_zm), half_a(c_z2)),
        (11, zm, half_b(c_zp), half_b(c_z2)),
        (13, zp, main_a(y_zm), main_a(y_z2)),
        (14, zm, main_b(y_zp), main_b(y_z2)),
        (16, yl, edge(c_zm), edge(y_zm)),
        (17, yl, edge(c_zp), edge(y_zp)),
        (18, yl, edge(c_z2), edge(y_z2)),
    )

    def ctx_send(buf, s, r, n):
        first, dev, rows, _ = plan[n]
        for i, rw in enumerate(rows):
            cp = rcopy(buf.at[rw], buf.at[rw], s.at[first + i], r.at[first + i], dev)
            go(cp, sent_g if buf is g else sent)

    def ctx_recv(buf, s, r, n):
        first, dev, _, rows = plan[n]
        for i, rw in enumerate(rows):
            rcopy(buf.at[rw], buf.at[rw], s.at[first + i], r.at[first + i], dev).wait_recv()

    def wrow(dd, off=0, n=WR):
        return pl.ds(m16(dd * WR + off), n)

    wplan = (
        (yhp, wrow(d), wrow(d + yhflip)),
        (xp, wrow(d), wrow(d_xm)),
        (xm, wrow(d), wrow(d_xp)),
        (xp, wrow(d + yhflip), wrow(d_xm + yhflip)),
        (xm, wrow(d + yhflip), wrow(d_xp + yhflip)),
        (xp, wrow(d_xm, 0, HALF), wrow(d_x2, 0, HALF)),
        (xm, wrow(d_xp, HALF, HALF), wrow(d_x2, HALF, HALF)),
        (xp, wrow(d_xm + yhflip, 0, HALF), wrow(d_x2 + yhflip, 0, HALF)),
        (xm, wrow(d_xp + yhflip, HALF, HALF), wrow(d_x2 + yhflip, HALF, HALF)),
    ) + tuple(
        (sib, wrow(b), wrow(b + 1 - 2 * core))
        for b in (
            d,
            d + yhflip,
            d_xm,
            d_xp,
            d_xm + yhflip,
            d_xp + yhflip,
            d_x2,
            d_x2 + yhflip,
        )
    )

    def w_send(*ns):
        for n in ns:
            dev, rows, _ = wplan[n]
            go(rcopy(w.at[rows], w.at[rows], ws.at[n], wr.at[n], dev))

    def w_recv(*ns):
        for n in ns:
            dev, _, rows = wplan[n]
            rcopy(w.at[rows], w.at[rows], ws.at[n], wr.at[n], dev).wait_recv()

    def x_send(*ns):
        for n in ns:
            ctx_send(xn, xs, xr, n)

    def x_recv(*ns):
        for n in ns:
            ctx_recv(xn, xs, xr, n)

    def g_send(*ns):
        for n in ns:
            ctx_send(g, gs, gr, n)

    def g_recv(*ns):
        for n in ns:
            ctx_recv(g, gs, gr, n)

    x_send(1, 2)
    w_send(0, 1, 2, 9)

    def gate_rows(i):
        rows = own_row(i)
        gate = jnp.where(i == 0, modr[5:6, :], modr[2:3, :])
        g[rows, :] = (gate * g[rows, :].astype(F32)).astype(BF)

    each(0, 8, gate_rows)

    def modulate(start, count, text):
        def step(i):
            rows = pl.ds(m16(start + i * 16), 16)
            base = 3 if text else 0
            v = xn[rows, :].astype(F32)
            st[rows, :] = (modr[base + 1 : base + 2, :] * v + modr[base : base + 1, :]).astype(BF)

        each(0, count // 16, step)

    def modulate_block(cc):
        modulate(cc * TB, TB, True)
        modulate(TXT + cc * IB, IB, False)

    modulate_block(c)
    x_recv(1)
    x_send(5)
    x_recv(2)
    x_send(6)
    w_recv(1)
    w_send(5, 11)
    w_recv(2)
    w_send(6, 12)
    w_recv(0)
    w_send(3, 4, 10)
    x_send(0, 9, 10)
    g_send(1, 2)
    modulate_block(c_zm)
    modulate_block(c_zp)
    x_recv(5, 6)
    x_send(11)
    w_recv(5, 6)
    w_send(15)
    x_recv(0)
    x_send(3, 4)
    g_send(0)
    modulate_block(c_z2)
    modulate_block(yc)
    w_recv(3)
    w_send(7, 13)
    w_recv(4)
    w_send(8, 14)
    g_recv(1)
    g_send(5, 9)
    g_recv(2)
    g_send(6, 10)
    x_recv(3)
    x_send(7)
    x_recv(4)
    x_send(8)
    x_recv(9, 10)
    modulate_block(y_zm)
    modulate_block(y_zp)
    w_recv(7, 8)
    w_send(16)
    g_recv(0)
    g_send(3, 4)
    x_recv(7, 8, 11)
    modulate_block(y_z2)
    g_recv(5, 6)
    g_send(11)
    w_recv(9, 10, 11, 12, 13, 14, 15, 16)

    def project(rows, col):
        left = st[rows, :]
        for j, out in enumerate((qb, kb, vb)):
            acc = dot(left, w[:, col + j * 256 : col + (j + 1) * 256])
            if j == 2:
                out[rows, :] = acc.astype(BF)
                continue
            for h in range(2):
                a = acc[:, h * 128 : (h + 1) * 128]
                pq[2 * j + h, rows, :] = a
                f = lax.rsqrt(jnp.mean(a * a, axis=-1, keepdims=True) + EPS)
                out[rows, h * 128 : (h + 1) * 128] = (a * f).astype(BF)

    def project_image(i):
        project(pl.ds(m16(TXT + i * 448), 448), QI)

    each(0, 2, project_image)
    project(pl.ds(0, TXT), QT)

    for h in range(2):
        cols = slice(h * 128, (h + 1) * 128)

        def forward(i, cols=cols):
            rows = pl.ds(m16(i * 256), 256)
            e = jnp.exp(dot_last(qb[rows, cols], kb[:, cols]) * SCALE)
            p = e / jnp.sum(e, axis=-1, keepdims=True)
            att[rows, cols] = dot(p.astype(BF), vb[:, cols]).astype(BF)

        each(0, 4, forward)

    def mix(i):
        n = pl.ds(pl.multiple_of(i * 512, 512), 512)
        st[0:TXT, n] = dot_last(att[0:TXT, :], w[n, OT : OT + 256]).astype(BF)
        st[TXT:576, n] = dot_last(att[TXT:576, :], w[n, OI : OI + 256]).astype(BF)
        st[576:SEQ, n] = dot_last(att[576:SEQ, :], w[n, OI : OI + 256]).astype(BF)

    each(0, 6, mix)

    zs = (c_z2, c_zp, c_zm, c)
    zdevs = (z2, zp, zm)
    left, right = slice(0, MC), slice(MC, D)

    def mix_copies(block, cols, land, ssem, rsem, first, dev):
        return [
            rcopy(st.at[rw, cols], land.at[pl.ds(off, size)], ssem.at[first + i], rsem.at[first + i], dev)
            for i, (rw, off, size) in enumerate(((trow(block), 0, TB), (irow(block), TB, IB)))
        ]

    def left_y(n):
        return mix_copies(zs[n] + ylflip, left, mland.at[n], mys, myr, 2 * n, yl)

    def left_z(n):
        return mix_copies(zs[n], left, mzl.at[n], mzs, mzr, 2 * n, zdevs[n])

    def right_z(n, v):
        block = zs[n] if v else zs[n] + ylflip
        return mix_copies(block, right, zland.at[n, v], mzs, mzr, 6 + 4 * n + 2 * v, zdevs[n])

    def right_y():
        return mix_copies(yc, right, yland, mys, myr, 8, yl)

    def start_all(cps):
        for cp in cps:
            go(cp)

    def recv_all(cps):
        for cp in cps:
            cp.wait_recv()

    def block_row(cc, i):
        return pl.ds(m16(jnp.where(i == 0, cc * TB, TXT + cc * IB + (i - 1) * 16)), 16)

    for n in range(4):
        start_all(left_y(n))

    def mixed_left(n):
        recv_all(left_y(n))

        def step(i):
            rows = block_row(zs[n], i)
            land = mland[n, pl.ds(m16(i * 16), 16), :].astype(F32)
            st[rows, left] = (st[rows, left].astype(F32) + land).astype(BF)

        each(0, 8, step)
        start_all(left_z(n))

    def mixed_right():
        for n in range(3):
            recv_all(right_z(n, 0))

        def step(i):
            rows = block_row(yc, i)
            total = st[rows, right].astype(F32)
            for n in range(3):
                total = total + zland[n, 0, pl.ds(m16(i * 16), 16), :].astype(F32)
            st[rows, right] = total.astype(BF)

        each(0, 8, step)
        start_all(right_y())

    def chip(k):
        j = k // 2
        dx = jnp.where(j == 0, 2, jnp.where(j == 1, 1, jnp.where(j == 2, 3, 0)))
        yy = jnp.where(lax.rem(k, 2) == 0, 1 - yh, yh)
        return lax.rem(xpos + dx, 4) * 2 + yy

    def out_tile(k):
        cols = pl.ds(pl.multiple_of(chip(k) * 384, 128), 384)
        so[k, :, 0:256] = dot_rows(g[TXT:SEQ, cols], att[TXT:SEQ, :]).astype(BF)
        so[k, :, 256:512] = dot_rows(g[0:TXT, cols], att[0:TXT, :]).astype(BF)

    def stage_cols(k):
        return pl.ds(pl.multiple_of(lax.rem(k, 4) * 768, 256), 768)

    def qkv_tile(k, text):
        p = chip(k)
        cols = pl.ds(pl.multiple_of(p * 384, 128), 384)
        rows = slice(0, TXT) if text else slice(TXT, SEQ)
        base = 3 if text else 0
        wcol = QT if text else QI
        back = bq[rows, :]
        grad = dot_rows(xn[rows, cols], back)
        total = jnp.sum(back.astype(F32), axis=0, keepdims=True)
        own = w[pl.ds(m16(p * 384), 384), wcol : wcol + 768].astype(F32)
        shift_part = jnp.sum(own * total, axis=-1, keepdims=True)
        scale_part = jnp.sum(own * grad, axis=-1, keepdims=True)
        lane = lax.broadcasted_iota(jnp.int32, (384, 128), 1)
        vals = jnp.where(lane == base, shift_part, jnp.where(lane == base + 1, scale_part, 0.0))
        mrow = pl.ds(m16(lax.rem(p, 2) * 384), 384)
        mcol = p // 2
        if text:
            vals = vals + pq[mcol, mrow, :]
        pq[mcol, mrow, :] = vals
        mod = jnp.transpose(modr[:, cols])
        full_grad = mod[:, base + 1 : base + 2] * grad + mod[:, base : base + 1] * total
        g[pl.ds(m16(k // 4 * 384), 384), stage_cols(k)] = full_grad.astype(BF)

    def stage(gi, k, half):
        rows = half * WR
        if gi == 0:
            return so.at[k, pl.ds(m16(rows), WR)]
        return g.at[pl.ds(m16(k // 4 * 384 + rows), WR), stage_cols(k)]

    def to_sib(gi, k):
        c0, n = GROUPS[gi]
        return rcopy(
            stage(gi, k, 1 - core),
            sland.at[k, :, c0 : c0 + n],
            ss.at[gi * 8 + k],
            sr.at[gi * 8 + k],
            sib,
        )

    def grad_range(gi, k0, k1):
        c0, n = GROUPS[gi]

        def compute(k):
            if gi == 0:
                out_tile(k)
            else:
                qkv_tile(k, gi == 2)
            to_sib(gi, k).start()

        each_io(k0, k1, compute)

        def combine(k):
            to_sib(gi, k).wait()

            def step(i):
                r = pl.ds(m16(i * 32), 32)
                if gi == 0:
                    mine = so[k, pl.ds(m16(core * WR + i * 32), 32), :]
                else:
                    mine = g[pl.ds(m16(k // 4 * 384 + core * WR + i * 32), 32), stage_cols(k)]
                land = sland[k, r, c0 : c0 + n].astype(F32)
                sland[k, r, c0 : c0 + n] = (mine.astype(F32) + land).astype(BF)

            each(0, 6, step)

        each_io(k0, k1, combine)

    def gcopy(gi, n, src, dst, dev):
        return rcopy(src, dst, rs.at[gi * 9 + n], rr.at[gi * 9 + n], dev)

    def far_copy(gi, v, side):
        c0, n = GROUPS[gi]
        cs = slice(c0, c0 + n)
        src = sland.at[v, pl.ds(side * HALF, HALF), cs]
        dst = (ha, hb)[side].at[v, :, cs]
        return gcopy(gi, 2 * v + side, src, dst, (xp, xm)[side])

    def near_copy(gi, v, side):
        c0, n = GROUPS[gi]
        cs = slice(c0, c0 + n)
        src = sland.at[2 + 2 * side + v, :, cs]
        return gcopy(gi, 4 + 2 * v + side, src, xl.at[side, v, :, cs], (xp, xm)[side])

    def yh_copy(gi):
        c0, n = GROUPS[gi]
        cs = slice(c0, c0 + n)
        return gcopy(gi, 8, sland.at[6, :, cs], yhl.at[:, cs], yhp)

    def grad_far(gi):
        for v in range(2):
            for side in range(2):
                go(far_copy(gi, v, side))

    def grad_near(gi):
        c0, n = GROUPS[gi]
        cs = slice(c0, c0 + n)
        for v in range(2):
            for side, land in ((0, ha), (1, hb)):
                far_copy(gi, v, side).wait_recv()
                k = 2 + 2 * side + v

                def step(i, land=land, k=k, side=side, v=v):
                    r = pl.ds(m16(side * HALF + i * 32), 32)
                    q = pl.ds(m16(i * 32), 32)
                    sland[k, r, cs] = (
                        sland[k, r, cs].astype(F32) + land[v, q, cs].astype(F32)
                    ).astype(BF)

                each(0, 3, step)
                go(near_copy(gi, v, side))

    def grad_yh(gi):
        c0, n = GROUPS[gi]
        cs = slice(c0, c0 + n)
        near_copy(gi, 0, 0).wait_recv()
        near_copy(gi, 0, 1).wait_recv()

        def step(i):
            r = pl.ds(m16(i * 32), 32)
            total = sland[6, r, cs].astype(F32) + xl[0, 0, r, cs].astype(F32)
            sland[6, r, cs] = (total + xl[1, 0, r, cs].astype(F32)).astype(BF)

        each(0, 6, step)
        go(yh_copy(gi))

    def grad_last(gi):
        c0, n = GROUPS[gi]
        near_copy(gi, 1, 0).wait_recv()
        near_copy(gi, 1, 1).wait_recv()
        yh_copy(gi).wait_recv()
        heads = 6 if gi else 2
        for b in range(n // 128):
            cs = slice(c0 + b * 128, c0 + (b + 1) * 128)
            for i in range(6):
                r = slice(i * 32, (i + 1) * 32)
                total = sland[7, r, cs].astype(F32) + xl[0, 1, r, cs].astype(F32)
                total = total + xl[1, 1, r, cs].astype(F32) + yhl[r, cs].astype(F32)
                if gi == 0:
                    dk[b // 2, pl.ds(i * 64 + b % 2, 32, stride=heads), :] = total
                else:
                    part = (gi - 1) * 2 + i // 3
                    pq[part, pl.ds(i % 3 * 192 + b, 32, stride=heads), :] = total
        if gi == 0:
            moves = [(dk.at[0, 0:384], go_i), (dk.at[1, 0:384], go_t)]
        else:
            ref = (gq_i, gq_t)[gi - 1]
            part = (gi - 1) * 2
            moves = [
                (pq.at[part, 0:576], ref.at[0:576]),
                (pq.at[part + 1, 0:576], ref.at[576:1152]),
            ]
        for i, (src, dst) in enumerate(moves):
            cp = pltpu.make_async_copy(src, dst, loc.at[16 + 2 * gi + i])
            cp.start()
            outs.append(cp)

    def rms_back(a, slope):
        f = lax.rsqrt(jnp.mean(a * a, axis=-1, keepdims=True) + EPS)
        normal = a * f
        return f * (slope - normal * jnp.mean(slope * normal, axis=-1, keepdims=True))

    def backward(ca, cb, fresh):
        parts = ((trow(ca), 0, TB), (trow(cb), 16, TB), (irow(ca), 32, IB), (irow(cb), 144, IB))

        def pick(ref, cols):
            return jnp.concatenate([ref[rw, cols] for rw, _, _ in parts], axis=0)

        every = slice(0, D)
        texts = jnp.concatenate([g[trow(ca), every], g[trow(cb), every]], axis=0)
        batt[0:32, :] = dot(texts, w[:, OT : OT + 256]).astype(BF)
        images = jnp.concatenate([g[irow(ca), every], g[irow(cb), every]], axis=0)
        batt[32:256, :] = dot(images, w[:, OI : OI + 256]).astype(BF)
        for h in range(2):
            cols = slice(h * 128, (h + 1) * 128)
            qt = pick(qb, cols)
            bt = batt[:, cols]
            e = jnp.exp(dot_last(kb[:, cols], qt) * SCALE)
            p = e / jnp.sum(e, axis=0, keepdims=True)
            dp = dot_last(vb[:, cols], bt)
            ds = p * (dp - jnp.sum(p * dp, axis=0, keepdims=True)) * SCALE
            ds = ds.astype(BF)
            if fresh:
                dv[h] = dot(p.astype(BF), bt)
                dk[h] = dot(ds, qt)
            else:
                dv[h] += dot(p.astype(BF), bt)
                dk[h] += dot(ds, qt)
            dq = rms_back(pick(pq.at[h], slice(0, 128)), dot_rows(ds, kb[:, cols])).astype(BF)
            for rw, off, size in parts:
                bq[rw, cols] = dq[off : off + size, :]

    def finish(i):
        rows = pl.ds(m16(i * 256), 256)
        for h in range(2):
            kcols = slice(256 + h * 128, 384 + h * 128)
            bq[rows, kcols] = rms_back(pq[2 + h, rows, :], dk[h, rows, :]).astype(BF)
            bq[rows, 512 + h * 128 : 640 + h * 128] = dv[h, rows, :].astype(BF)

    def run(step, *args):
        step(*args)

    run(backward, c, yc, True)
    g_recv(3)
    g_send(7)
    g_recv(4)
    g_send(8)
    run(backward, c_zm, c_zp, False)
    g_recv(9, 10)
    run(backward, y_zm, y_zp, False)
    g_recv(7, 8, 11)
    for n in range(3):
        start_all(right_z(n, 0))
    for n in range(3):
        start_all(right_z(n, 1))
    grad_range(0, 0, 2)
    grad_far(0)
    run(backward, c_z2, y_z2, False)
    each(0, 4, finish)
    grad_range(0, 2, 8)
    mixed_left(0)
    grad_near(0)

    for cp in sent_g:
        cp.wait_send()
    slopes = [
        pltpu.make_async_copy(slo_t.at[0], g.at[pl.ds(768, TB)], loc.at[12]),
        pltpu.make_async_copy(slo_i.at[0], g.at[pl.ds(784, IB)], loc.at[13]),
    ]
    for cp in slopes:
        cp.start()

    for gi in (1, 2):
        grad_range(gi, 0, 2)
        grad_far(gi)
        grad_range(gi, 2, 8)
        mixed_left(gi)
    grad_near(1)
    grad_near(2)
    grad_yh(0)

    def turn(p):
        mrow = pl.ds(m16(lax.rem(p, 2) * 384), 384)
        mcol = p // 2
        flat = jnp.transpose(pq[mcol, mrow, :])
        ms[0, :, pl.ds(pl.multiple_of(p * 384, 128), 384)] = flat[0:8, :]

    each(0, 8, turn)
    mixed_right()
    grad_last(0)
    grad_yh(1)
    grad_yh(2)

    recv_all(left_y(3))
    for n in range(3):
        recv_all(left_z(n))
        recv_all(right_z(n, 1))
    recv_all(right_y())
    for cp in slopes:
        cp.wait()

    def own_mixed(i, gate):
        rows = own_row(i)
        q = pl.ds(m16(i * 16), 16)
        for cols, others in ((left, (mland.at[3], mzl.at[0], mzl.at[1], mzl.at[2])),
                             (right, (yland, zland.at[0, 1], zland.at[1, 1], zland.at[2, 1]))):
            total = st[rows, cols].astype(F32)
            for other in others:
                total = total + other[q, :].astype(F32)
            st[rows, cols] = (modr[gate : gate + 1, cols] * total).astype(BF)
            slope = g[pl.ds(m16(768 + i * 16), 16), cols].astype(F32)
            ms[0, gate : gate + 1, cols] += jnp.sum(slope * total, axis=0, keepdims=True)

    own_mixed(0, 5)
    each(1, 8, lambda i: own_mixed(i, 2))
    for cp in (
        pltpu.make_async_copy(st.at[trow(c)], upd_t.at[0], loc.at[14]),
        pltpu.make_async_copy(st.at[irow(c)], upd_i.at[0], loc.at[15]),
    ):
        cp.start()
        outs.append(cp)

    first = rcopy(ms.at[0], ml.at[0], mss.at[0], msr.at[0], yl)
    go(first)
    first.wait_recv()
    ms[1] = ms[0] + ml[0]
    more = [
        rcopy(ms.at[1], ml.at[1 + n], mss.at[1 + n], msr.at[1 + n], dev)
        for n, dev in enumerate((zp, zm, z2))
    ]
    for cp in more:
        go(cp)
    grad_last(1)
    for cp in more:
        cp.wait_recv()
    modsum = ms[1] + ml[1] + ml[2] + ml[3]
    ms_i[0] = modsum[0:3, :]
    ms_t[0] = modsum[3:6, :]

    grad_last(2)
    for cp in outs:
        cp.wait()
    for cp in sent:
        cp.wait_send()


def deliver(*refs):
    for n in range(6):
        refs[8 + n][...] = refs[n][...]
    for n in (6, 7):
        for row in range(3):
            for j in range(24):
                line = refs[n][0, row : row + 1, j * 128 : (j + 1) * 128]
                refs[8 + n][row * 24 + j : row * 24 + j + 1, :] = line


def body(
    image_tokens,
    text_tokens,
    image_mod,
    text_mod,
    image_qkv_weight,
    text_qkv_weight,
    image_out_weight,
    text_out_weight,
    image_slope,
    text_slope,
):
    hbm = pl.BlockSpec(memory_space=pl.ANY)
    vmem = pl.BlockSpec(memory_space=pltpu.VMEM)
    dma = pltpu.SemaphoreType.DMA
    shape = jax.ShapeDtypeStruct
    results = pl.pallas_call(
        kernel,
        out_shape=(
            shape((1, IB, D), BF),
            shape((1, TB, D), BF),
            shape((WR * 6, 128), F32),
            shape((WR * 6, 128), F32),
            shape((WR * 2, 128), F32),
            shape((WR * 2, 128), F32),
            shape((1, 3, D), F32),
            shape((1, 3, D), F32),
        ),
        in_specs=[hbm] * 8 + [vmem] * 2,
        out_specs=(hbm,) * 6 + (vmem,) * 2,
        scratch_shapes=[
            pltpu.VMEM((SEQ, D), BF),
            pltpu.VMEM((SEQ, D), BF),
            pltpu.VMEM((D, WC), BF),
            pltpu.VMEM((SEQ, D), BF),
            pltpu.VMEM((4, SEQ, 128), F32),
            pltpu.VMEM((SEQ, 256), BF),
            pltpu.VMEM((SEQ, 256), BF),
            pltpu.VMEM((SEQ, 256), BF),
            pltpu.VMEM((SEQ, 256), BF),
            pltpu.VMEM((256, 256), BF),
            pltpu.VMEM((SEQ, 768), BF),
            pltpu.VMEM((2, SEQ, 128), F32),
            pltpu.VMEM((2, SEQ, 128), F32),
            pltpu.VMEM((8, D), F32),
            pltpu.VMEM((4, 128, MC), BF),
            pltpu.VMEM((3, 128, MC), BF),
            pltpu.VMEM((3, 2, 128, D - MC), BF),
            pltpu.VMEM((128, D - MC), BF),
            pltpu.VMEM((8, WR, WC), BF),
            pltpu.VMEM((8, 384, 512), BF),
            pltpu.VMEM((2, HALF, WC), BF),
            pltpu.VMEM((2, HALF, WC), BF),
            pltpu.VMEM((2, 2, WR, WC), BF),
            pltpu.VMEM((WR, WC), BF),
            pltpu.VMEM((2, 8, D), F32),
            pltpu.VMEM((4, 8, D), F32),
            dma((19,)),
            dma((19,)),
            dma((19,)),
            dma((19,)),
            dma((17,)),
            dma((17,)),
            dma((10,)),
            dma((10,)),
            dma((18,)),
            dma((18,)),
            dma((24,)),
            dma((24,)),
            dma((27,)),
            dma((27,)),
            dma((4,)),
            dma((4,)),
            dma((22,)),
        ],
        compiler_params=pltpu.CompilerParams(
            collective_id=0, has_side_effects=True, vmem_limit_bytes=63 * 2**20
        ),
    )(
        image_tokens,
        text_tokens,
        image_slope,
        text_slope,
        image_qkv_weight.reshape(WR * 6, 128),
        text_qkv_weight.reshape(WR * 6, 128),
        image_out_weight.reshape(WR * 2, 128),
        text_out_weight.reshape(WR * 2, 128),
        image_mod,
        text_mod,
    )
    upd_i, upd_t, gq_i, gq_t, go_i, go_t, ms_i, ms_t = pl.pallas_call(
        deliver,
        out_shape=tuple(shape(v.shape, v.dtype) for v in results[:6]) + (shape((72, 128), F32),) * 2,
        in_specs=[vmem] * 8,
        out_specs=(vmem,) * 8,
        compiler_params=pltpu.CompilerParams(vmem_limit_bytes=60 * 2**20),
    )(*results)
    return (
        upd_i,
        upd_t,
        gq_i.reshape(WR, 3, 2, 128),
        gq_t.reshape(WR, 3, 2, 128),
        go_i.reshape(WR, 2, 128),
        go_t.reshape(WR, 2, 128),
        ms_i.reshape(1, 3, D),
        ms_t.reshape(1, 3, D),
    )


def solution(mesh):
    tokens = P("dp", "context", None)
    mods = P("dp", None, None)
    qkv = P("dp", None, "context", None)
    return jax.shard_map(
        body,
        mesh=mesh,
        in_specs=(tokens, tokens, mods, mods, qkv, qkv, tokens, tokens, tokens, tokens),
        out_specs=(tokens, tokens, qkv, qkv, tokens, tokens, mods, mods),
        check_vma=False,
    )
```

```python
import jax
import jax.numpy as jnp
from jax import lax
from jax.experimental import pallas as pl
from jax.experimental.pallas import tpu as pltpu
from jax.sharding import PartitionSpec as P

EPS = 1e-06
BF = jnp.bfloat16
F32 = jnp.float32
D = 3072
TXT = 128
SEQ = 1024
TB = 16
IB = 112
WR = 192
HALF = 96
MC = 1536
SCALE = 128 ** (-0.5)
QI, QT, OI, OT, WC = 0, 768, 1536, 1792, 2048
GROUPS = ((OI, 512), (QI, 768), (QT, 768))


def dot(a, b):
    return jnp.dot(a, b, preferred_element_type=F32)


def dot_last(a, b):
    return lax.dot_general(a, b, (((1,), (1,)), ((), ())), preferred_element_type=F32)


def dot_rows(a, b):
    return lax.dot_general(a, b, (((0,), (0,)), ((), ())), preferred_element_type=F32)


def each(low, high, step):
    lax.fori_loop(low, high, lambda i, _: (step(i), 0)[1], 0)


each_io = each


def m16(v):
    return pl.multiple_of(v, 16)


def kernel(
    tok_i,
    tok_t,
    slo_i,
    slo_t,
    wq_i,
    wq_t,
    wo_i,
    wo_t,
    mod_i,
    mod_t,
    upd_i,
    upd_t,
    gq_i,
    gq_t,
    go_i,
    go_t,
    ms_i,
    ms_t,
    xn,
    g,
    w,
    st,
    pq,
    qb,
    kb,
    vb,
    att,
    batt,
    bq,
    dk,
    dv,
    modr,
    mland,
    mzl,
    zland,
    yland,
    sland,
    so,
    ha,
    hb,
    xl,
    yhl,
    ms,
    ml,
    xs,
    xr,
    gs,
    gr,
    ws,
    wr,
    mys,
    myr,
    mzs,
    mzr,
    ss,
    sr,
    rs,
    rr,
    mss,
    msr,
    loc,
):
    d = lax.axis_index("dp")
    c = lax.axis_index("context")
    core = lax.rem(d, 2)
    yh = lax.rem(d // 2, 2)
    xpos = d // 4
    c_zp, c_zm, c_z2 = lax.rem(c + 2, 8), lax.rem(c + 6, 8), lax.rem(c + 4, 8)
    ylflip = 1 - 2 * lax.rem(c, 2)
    d_xp, d_xm, d_x2 = lax.rem(d + 4, 16), lax.rem(d + 12, 16), lax.rem(d + 8, 16)
    yhflip = 2 - 4 * yh
    zp, zm, z2, yl = (d, c_zp), (d, c_zm), (d, c_z2), (d, c + ylflip)
    xp, xm, yhp, sib = (d_xp, c), (d_xm, c), (d + yhflip, c), (d + 1 - 2 * core, c)

    def rcopy(src, dst, ssem, rsem, dev):
        return pltpu.make_async_remote_copy(
            src_ref=src,
            dst_ref=dst,
            send_sem=ssem,
            recv_sem=rsem,
            device_id=dev,
            device_id_type=pl.DeviceIdType.MESH,
        )

    def trow(cc):
        return pl.ds(m16(cc * TB), TB)

    def irow(cc, off=0, n=IB):
        return pl.ds(m16(TXT + cc * IB + off), n)

    sent = []
    sent_g = []
    outs = []

    def go(cp, kept=sent):
        cp.start()
        kept.append(cp)

    pieces = tuple((r, p, q, 6) for r, q in ((wq_i, QI), (wq_t, QT)) for p in range(3))
    pieces += ((wo_i, 0, OI, 2), (wo_t, 0, OT, 2))
    locs = [
        pltpu.make_async_copy(src, dst, loc.at[n])
        for n, (src, dst) in enumerate(
            (
                (tok_t.at[0], xn.at[trow(c)]),
                (tok_i.at[0], xn.at[irow(c)]),
                (slo_t.at[0], g.at[trow(c)]),
                (slo_i.at[0], g.at[irow(c)]),
            )
            + tuple(
                (ref.at[pl.ds(384 * p, 384)], so.at[k, :, 0:128])
                for k, (ref, p, _, _) in enumerate(pieces)
            )
        )
    ]
    for cp in locs:
        cp.start()
    bar = pltpu.get_barrier_semaphore()
    peers = (zp, zm, z2, yl, xp, xm, yhp, sib)
    for dev in peers:
        pl.semaphore_signal(bar, inc=1, device_id=dev, device_id_type=pl.DeviceIdType.MESH)
    modr[...] = jnp.zeros_like(modr)
    modr[0:3, :] = mod_i[0].astype(F32)
    modr[3:6, :] = mod_t[0].astype(F32)
    modr[1:2, :] = modr[1:2, :] + 1.0
    modr[4:5, :] = modr[4:5, :] + 1.0
    for cp in locs:
        cp.wait()

    for k, (_, p, col, heads) in enumerate(pieces):
        r0, n = k // 4 * 384, 384 // heads
        pq[k % 4, r0 : r0 + 384, :] = so[k, :, 0:128].astype(F32)
        rows = pl.ds(m16(d * WR + p * n), n)
        for j in range(heads):
            part = pq[k % 4, pl.ds(r0 + j, n, stride=heads), :]
            w[rows, col + j * 128 : col + (j + 1) * 128] = part.astype(BF)

    def own_row(i):
        return pl.ds(m16(jnp.where(i == 0, c * TB, TXT + c * IB + (i - 1) * 16)), 16)

    def norm_rows(i):
        rows = own_row(i)
        v = xn[rows, :].astype(F32)
        v = v - jnp.mean(v, axis=-1, keepdims=True)
        v = v * lax.rsqrt(jnp.mean(v * v, axis=-1, keepdims=True) + EPS)
        xn[rows, :] = v.astype(BF)

    each(0, 8, norm_rows)
    pl.semaphore_wait(bar, len(peers))

    def full(cc):
        return (trow(cc), irow(cc))

    def half_a(cc):
        return (irow(cc, 0, 64),)

    def half_b(cc):
        return (irow(cc, 64, 48), trow(cc))

    def main(cc):
        return (trow(cc), irow(cc, 0, 80))

    def main_a(cc):
        return (irow(cc, 0, 48),)

    def main_b(cc):
        return (irow(cc, 48, 32), trow(cc))

    def edge(cc):
        return (irow(cc, 80, 32),)

    yc = c + ylflip
    y_zp, y_zm, y_z2 = c_zp + ylflip, c_zm + ylflip, c_z2 + ylflip
    plan = (
        (0, yl, full(c), full(yc)),
        (2, zp, full(c), full(c_zm)),
        (4, zm, full(c), full(c_zp)),
        (6, zp, main(yc), main(y_zm)),
        (8, zm, main(yc), main(y_zp)),
        (10, zp, half_a(c_zm), half_a(c_z2)),
        (11, zm, half_b(c_zp), half_b(c_z2)),
        (13, zp, main_a(y_zm), main_a(y_z2)),
        (14, zm, main_b(y_zp), main_b(y_z2)),
        (16, yl, edge(c_zm), edge(y_zm)),
        (17, yl, edge(c_zp), edge(y_zp)),
        (18, yl, edge(c_z2), edge(y_z2)),
    )

    def ctx_send(buf, s, r, n):
        first, dev, rows, _ = plan[n]
        for i, rw in enumerate(rows):
            cp = rcopy(buf.at[rw], buf.at[rw], s.at[first + i], r.at[first + i], dev)
            go(cp, sent_g if buf is g else sent)

    def ctx_recv(buf, s, r, n):
        first, dev, _, rows = plan[n]
        for i, rw in enumerate(rows):
            rcopy(buf.at[rw], buf.at[rw], s.at[first + i], r.at[first + i], dev).wait_recv()

    def wrow(dd, off=0, n=WR):
        return pl.ds(m16(dd * WR + off), n)

    wplan = (
        (yhp, wrow(d), wrow(d + yhflip)),
        (xp, wrow(d), wrow(d_xm)),
        (xm, wrow(d), wrow(d_xp)),
        (xp, wrow(d + yhflip), wrow(d_xm + yhflip)),
        (xm, wrow(d + yhflip), wrow(d_xp + yhflip)),
        (xp, wrow(d_xm, 0, HALF), wrow(d_x2, 0, HALF)),
        (xm, wrow(d_xp, HALF, HALF), wrow(d_x2, HALF, HALF)),
        (xp, wrow(d_xm + yhflip, 0, HALF), wrow(d_x2 + yhflip, 0, HALF)),
        (xm, wrow(d_xp + yhflip, HALF, HALF), wrow(d_x2 + yhflip, HALF, HALF)),
    ) + tuple(
        (sib, wrow(b), wrow(b + 1 - 2 * core))
        for b in (
            d,
            d + yhflip,
            d_xm,
            d_xp,
            d_xm + yhflip,
            d_xp + yhflip,
            d_x2,
            d_x2 + yhflip,
        )
    )

    def w_send(*ns):
        for n in ns:
            dev, rows, _ = wplan[n]
            go(rcopy(w.at[rows], w.at[rows], ws.at[n], wr.at[n], dev))

    def w_recv(*ns):
        for n in ns:
            dev, _, rows = wplan[n]
            rcopy(w.at[rows], w.at[rows], ws.at[n], wr.at[n], dev).wait_recv()

    def x_send(*ns):
        for n in ns:
            ctx_send(xn, xs, xr, n)

    def x_recv(*ns):
        for n in ns:
            ctx_recv(xn, xs, xr, n)

    def g_send(*ns):
        for n in ns:
            ctx_send(g, gs, gr, n)

    def g_recv(*ns):
        for n in ns:
            ctx_recv(g, gs, gr, n)

    x_send(1, 2)
    w_send(0, 1, 2, 9)

    def gate_rows(i):
        rows = own_row(i)
        gate = jnp.where(i == 0, modr[5:6, :], modr[2:3, :])
        g[rows, :] = (gate * g[rows, :].astype(F32)).astype(BF)

    each(0, 8, gate_rows)

    def modulate(start, count, text):
        def step(i):
            rows = pl.ds(m16(start + i * 16), 16)
            base = 3 if text else 0
            v = xn[rows, :].astype(F32)
            st[rows, :] = (modr[base + 1 : base + 2, :] * v + modr[base : base + 1, :]).astype(BF)

        each(0, count // 16, step)

    def modulate_block(cc):
        modulate(cc * TB, TB, True)
        modulate(TXT + cc * IB, IB, False)

    modulate_block(c)
    x_recv(1)
    x_send(5)
    x_recv(2)
    x_send(6)
    w_recv(1)
    w_send(5, 11)
    w_recv(2)
    w_send(6, 12)
    w_recv(0)
    w_send(3, 4, 10)
    x_send(0, 9, 10)
    g_send(1, 2)
    modulate_block(c_zm)
    modulate_block(c_zp)
    x_recv(5, 6)
    x_send(11)
    w_recv(5, 6)
    w_send(15)
    x_recv(0)
    x_send(3, 4)
    g_send(0)
    modulate_block(c_z2)
    modulate_block(yc)
    w_recv(3)
    w_send(7, 13)
    w_recv(4)
    w_send(8, 14)
    g_recv(1)
    g_send(5, 9)
    g_recv(2)
    g_send(6, 10)
    x_recv(3)
    x_send(7)
    x_recv(4)
    x_send(8)
    x_recv(9, 10)
    modulate_block(y_zm)
    modulate_block(y_zp)
    w_recv(7, 8)
    w_send(16)
    g_recv(0)
    g_send(3, 4)
    x_recv(7, 8, 11)
    modulate_block(y_z2)
    g_recv(5, 6)
    g_send(11)
    w_recv(9, 10, 11, 12, 13, 14, 15, 16)

    def project(rows, col):
        left = st[rows, :]
        for j, out in enumerate((qb, kb, vb)):
            acc = dot(left, w[:, col + j * 256 : col + (j + 1) * 256])
            if j == 2:
                out[rows, :] = acc.astype(BF)
                continue
            for h in range(2):
                a = acc[:, h * 128 : (h + 1) * 128]
                pq[2 * j + h, rows, :] = a
                f = lax.rsqrt(jnp.mean(a * a, axis=-1, keepdims=True) + EPS)
                out[rows, h * 128 : (h + 1) * 128] = (a * f).astype(BF)

    def project_image(i):
        project(pl.ds(m16(TXT + i * 448), 448), QI)

    each(0, 2, project_image)
    project(pl.ds(0, TXT), QT)

    for h in range(2):
        cols = slice(h * 128, (h + 1) * 128)

        def forward(i, cols=cols):
            rows = pl.ds(m16(i * 256), 256)
            e = jnp.exp(dot_last(qb[rows, cols], kb[:, cols]) * SCALE)
            p = e / jnp.sum(e, axis=-1, keepdims=True)
            att[rows, cols] = dot(p.astype(BF), vb[:, cols]).astype(BF)

        each(0, 4, forward)

    def mix(i):
        n = pl.ds(pl.multiple_of(i * 512, 512), 512)
        st[0:TXT, n] = dot_last(att[0:TXT, :], w[n, OT : OT + 256]).astype(BF)
        st[TXT:576, n] = dot_last(att[TXT:576, :], w[n, OI : OI + 256]).astype(BF)
        st[576:SEQ, n] = dot_last(att[576:SEQ, :], w[n, OI : OI + 256]).astype(BF)

    each(0, 6, mix)

    zs = (c_z2, c_zp, c_zm, c)
    zdevs = (z2, zp, zm)
    left, right = slice(0, MC), slice(MC, D)

    def mix_copies(block, cols, land, ssem, rsem, first, dev):
        return [
            rcopy(st.at[rw, cols], land.at[pl.ds(off, size)], ssem.at[first + i], rsem.at[first + i], dev)
            for i, (rw, off, size) in enumerate(((trow(block), 0, TB), (irow(block), TB, IB)))
        ]

    def left_y(n):
        return mix_copies(zs[n] + ylflip, left, mland.at[n], mys, myr, 2 * n, yl)

    def left_z(n):
        return mix_copies(zs[n], left, mzl.at[n], mzs, mzr, 2 * n, zdevs[n])

    def right_z(n, v):
        block = zs[n] if v else zs[n] + ylflip
        return mix_copies(block, right, zland.at[n, v], mzs, mzr, 6 + 4 * n + 2 * v, zdevs[n])

    def right_y():
        return mix_copies(yc, right, yland, mys, myr, 8, yl)

    def start_all(cps):
        for cp in cps:
            go(cp)

    def recv_all(cps):
        for cp in cps:
            cp.wait_recv()

    def block_row(cc, i):
        return pl.ds(m16(jnp.where(i == 0, cc * TB, TXT + cc * IB + (i - 1) * 16)), 16)

    for n in range(4):
        start_all(left_y(n))

    def mixed_left(n):
        recv_all(left_y(n))

        def step(i):
            rows = block_row(zs[n], i)
            land = mland[n, pl.ds(m16(i * 16), 16), :].astype(F32)
            st[rows, left] = (st[rows, left].astype(F32) + land).astype(BF)

        each(0, 8, step)
        start_all(left_z(n))

    def mixed_right():
        for n in range(3):
            recv_all(right_z(n, 0))

        def step(i):
            rows = block_row(yc, i)
            total = st[rows, right].astype(F32)
            for n in range(3):
                total = total + zland[n, 0, pl.ds(m16(i * 16), 16), :].astype(F32)
            st[rows, right] = total.astype(BF)

        each(0, 8, step)
        start_all(right_y())

    def chip(k):
        j = k // 2
        dx = jnp.where(j == 0, 2, jnp.where(j == 1, 1, jnp.where(j == 2, 3, 0)))
        yy = jnp.where(lax.rem(k, 2) == 0, 1 - yh, yh)
        return lax.rem(xpos + dx, 4) * 2 + yy

    def out_tile(k):
        cols = pl.ds(pl.multiple_of(chip(k) * 384, 128), 384)
        so[k, :, 0:256] = dot_rows(g[TXT:SEQ, cols], att[TXT:SEQ, :]).astype(BF)
        so[k, :, 256:512] = dot_rows(g[0:TXT, cols], att[0:TXT, :]).astype(BF)

    def stage_cols(k):
        return pl.ds(pl.multiple_of(lax.rem(k, 4) * 768, 256), 768)

    def qkv_tile(k, text):
        p = chip(k)
        cols = pl.ds(pl.multiple_of(p * 384, 128), 384)
        rows = slice(0, TXT) if text else slice(TXT, SEQ)
        base = 3 if text else 0
        wcol = QT if text else QI
        back = bq[rows, :]
        grad = dot_rows(xn[rows, cols], back)
        total = jnp.sum(back.astype(F32), axis=0, keepdims=True)
        own = w[pl.ds(m16(p * 384), 384), wcol : wcol + 768].astype(F32)
        shift_part = jnp.sum(own * total, axis=-1, keepdims=True)
        scale_part = jnp.sum(own * grad, axis=-1, keepdims=True)
        lane = lax.broadcasted_iota(jnp.int32, (384, 128), 1)
        vals = jnp.where(lane == base, shift_part, jnp.where(lane == base + 1, scale_part, 0.0))
        mrow = pl.ds(m16(lax.rem(p, 2) * 384), 384)
        mcol = p // 2
        if text:
            vals = vals + pq[mcol, mrow, :]
        pq[mcol, mrow, :] = vals
        mod = jnp.transpose(modr[:, cols])
        full_grad = mod[:, base + 1 : base + 2] * grad + mod[:, base : base + 1] * total
        g[pl.ds(m16(k // 4 * 384), 384), stage_cols(k)] = full_grad.astype(BF)

    def stage(gi, k, half):
        rows = half * WR
        if gi == 0:
            return so.at[k, pl.ds(m16(rows), WR)]
        return g.at[pl.ds(m16(k // 4 * 384 + rows), WR), stage_cols(k)]

    def to_sib(gi, k):
        c0, n = GROUPS[gi]
        return rcopy(
            stage(gi, k, 1 - core),
            sland.at[k, :, c0 : c0 + n],
            ss.at[gi * 8 + k],
            sr.at[gi * 8 + k],
            sib,
        )

    def grad_range(gi, k0, k1):
        c0, n = GROUPS[gi]

        def compute(k):
            if gi == 0:
                out_tile(k)
            else:
                qkv_tile(k, gi == 2)
            to_sib(gi, k).start()

        each_io(k0, k1, compute)

        def combine(k):
            to_sib(gi, k).wait()

            def step(i):
                r = pl.ds(m16(i * 32), 32)
                if gi == 0:
                    mine = so[k, pl.ds(m16(core * WR + i * 32), 32), :]
                else:
                    mine = g[pl.ds(m16(k // 4 * 384 + core * WR + i * 32), 32), stage_cols(k)]
                land = sland[k, r, c0 : c0 + n].astype(F32)
                sland[k, r, c0 : c0 + n] = (mine.astype(F32) + land).astype(BF)

            each(0, 6, step)

        each_io(k0, k1, combine)

    def gcopy(gi, n, src, dst, dev):
        return rcopy(src, dst, rs.at[gi * 9 + n], rr.at[gi * 9 + n], dev)

    def far_copy(gi, v, side):
        c0, n = GROUPS[gi]
        cs = slice(c0, c0 + n)
        src = sland.at[v, pl.ds(side * HALF, HALF), cs]
        dst = (ha, hb)[side].at[v, :, cs]
        return gcopy(gi, 2 * v + side, src, dst, (xp, xm)[side])

    def near_copy(gi, v, side):
        c0, n = GROUPS[gi]
        cs = slice(c0, c0 + n)
        src = sland.at[2 + 2 * side + v, :, cs]
        return gcopy(gi, 4 + 2 * v + side, src, xl.at[side, v, :, cs], (xp, xm)[side])

    def yh_copy(gi):
        c0, n = GROUPS[gi]
        cs = slice(c0, c0 + n)
        return gcopy(gi, 8, sland.at[6, :, cs], yhl.at[:, cs], yhp)

    def grad_far(gi):
        for v in range(2):
            for side in range(2):
                go(far_copy(gi, v, side))

    def grad_near(gi):
        c0, n = GROUPS[gi]
        cs = slice(c0, c0 + n)
        for v in range(2):
            for side, land in ((0, ha), (1, hb)):
                far_copy(gi, v, side).wait_recv()
                k = 2 + 2 * side + v

                def step(i, land=land, k=k, side=side, v=v):
                    r = pl.ds(m16(side * HALF + i * 32), 32)
                    q = pl.ds(m16(i * 32), 32)
                    sland[k, r, cs] = (
                        sland[k, r, cs].astype(F32) + land[v, q, cs].astype(F32)
                    ).astype(BF)

                each(0, 3, step)
                go(near_copy(gi, v, side))

    def grad_yh(gi):
        c0, n = GROUPS[gi]
        cs = slice(c0, c0 + n)
        near_copy(gi, 0, 0).wait_recv()
        near_copy(gi, 0, 1).wait_recv()

        def step(i):
            r = pl.ds(m16(i * 32), 32)
            total = sland[6, r, cs].astype(F32) + xl[0, 0, r, cs].astype(F32)
            sland[6, r, cs] = (total + xl[1, 0, r, cs].astype(F32)).astype(BF)

        each(0, 6, step)
        go(yh_copy(gi))

    def grad_last(gi):
        c0, n = GROUPS[gi]
        near_copy(gi, 1, 0).wait_recv()
        near_copy(gi, 1, 1).wait_recv()
        yh_copy(gi).wait_recv()
        heads = 6 if gi else 2
        for b in range(n // 128):
            cs = slice(c0 + b * 128, c0 + (b + 1) * 128)
            for i in range(6):
                r = slice(i * 32, (i + 1) * 32)
                total = sland[7, r, cs].astype(F32) + xl[0, 1, r, cs].astype(F32)
                total = total + xl[1, 1, r, cs].astype(F32) + yhl[r, cs].astype(F32)
                if gi == 0:
                    dk[b // 2, pl.ds(i * 64 + b % 2, 32, stride=heads), :] = total
                else:
                    part = (gi - 1) * 2 + i // 3
                    pq[part, pl.ds(i % 3 * 192 + b, 32, stride=heads), :] = total
        if gi == 0:
            moves = [(dk.at[0, 0:384], go_i), (dk.at[1, 0:384], go_t)]
        else:
            ref = (gq_i, gq_t)[gi - 1]
            part = (gi - 1) * 2
            moves = [
                (pq.at[part, 0:576], ref.at[0:576]),
                (pq.at[part + 1, 0:576], ref.at[576:1152]),
            ]
        for i, (src, dst) in enumerate(moves):
            cp = pltpu.make_async_copy(src, dst, loc.at[16 + 2 * gi + i])
            cp.start()
            outs.append(cp)

    def rms_back(a, slope):
        f = lax.rsqrt(jnp.mean(a * a, axis=-1, keepdims=True) + EPS)
        normal = a * f
        return f * (slope - normal * jnp.mean(slope * normal, axis=-1, keepdims=True))

    def backward(ca, cb, fresh):
        parts = ((trow(ca), 0, TB), (trow(cb), 16, TB), (irow(ca), 32, IB), (irow(cb), 144, IB))

        def pick(ref, cols):
            return jnp.concatenate([ref[rw, cols] for rw, _, _ in parts], axis=0)

        every = slice(0, D)
        texts = jnp.concatenate([g[trow(ca), every], g[trow(cb), every]], axis=0)
        batt[0:32, :] = dot(texts, w[:, OT : OT + 256]).astype(BF)
        images = jnp.concatenate([g[irow(ca), every], g[irow(cb), every]], axis=0)
        batt[32:256, :] = dot(images, w[:, OI : OI + 256]).astype(BF)
        for h in range(2):
            cols = slice(h * 128, (h + 1) * 128)
            qt = pick(qb, cols)
            bt = batt[:, cols]
            e = jnp.exp(dot_last(kb[:, cols], qt) * SCALE)
            p = e / jnp.sum(e, axis=0, keepdims=True)
            dp = dot_last(vb[:, cols], bt)
            ds = p * (dp - jnp.sum(p * dp, axis=0, keepdims=True)) * SCALE
            ds = ds.astype(BF)
            if fresh:
                dv[h] = dot(p.astype(BF), bt)
                dk[h] = dot(ds, qt)
            else:
                dv[h] += dot(p.astype(BF), bt)
                dk[h] += dot(ds, qt)
            dq = rms_back(pick(pq.at[h], slice(0, 128)), dot_rows(ds, kb[:, cols])).astype(BF)
            for rw, off, size in parts:
                bq[rw, cols] = dq[off : off + size, :]

    def finish(i):
        rows = pl.ds(m16(i * 256), 256)
        for h in range(2):
            kcols = slice(256 + h * 128, 384 + h * 128)
            bq[rows, kcols] = rms_back(pq[2 + h, rows, :], dk[h, rows, :]).astype(BF)
            bq[rows, 512 + h * 128 : 640 + h * 128] = dv[h, rows, :].astype(BF)

    def run(step, *args):
        step(*args)

    g_recv(3)
    g_send(7)
    g_recv(4)
    g_send(8)
    run(backward, c, yc, True)
    run(backward, c_zm, c_zp, False)
    g_recv(9, 10)
    run(backward, y_zm, y_zp, False)
    g_recv(7, 8, 11)
    for n in range(3):
        start_all(right_z(n, 0))
    for n in range(3):
        start_all(right_z(n, 1))
    grad_range(0, 0, 2)
    grad_far(0)
    run(backward, c_z2, y_z2, False)
    each(0, 4, finish)
    grad_range(0, 2, 8)
    mixed_left(0)
    grad_near(0)

    for cp in sent_g:
        cp.wait_send()
    slopes = [
        pltpu.make_async_copy(slo_t.at[0], g.at[pl.ds(768, TB)], loc.at[12]),
        pltpu.make_async_copy(slo_i.at[0], g.at[pl.ds(784, IB)], loc.at[13]),
    ]
    for cp in slopes:
        cp.start()

    for gi in (1, 2):
        grad_range(gi, 0, 2)
        grad_far(gi)
        grad_range(gi, 2, 8)
        mixed_left(gi)
    grad_near(1)
    grad_near(2)
    grad_yh(0)

    def turn(p):
        mrow = pl.ds(m16(lax.rem(p, 2) * 384), 384)
        mcol = p // 2
        flat = jnp.transpose(pq[mcol, mrow, :])
        ms[0, :, pl.ds(pl.multiple_of(p * 384, 128), 384)] = flat[0:8, :]

    each(0, 8, turn)
    mixed_right()
    grad_last(0)
    grad_yh(1)
    grad_yh(2)

    recv_all(left_y(3))
    for n in range(3):
        recv_all(left_z(n))
        recv_all(right_z(n, 1))
    recv_all(right_y())
    for cp in slopes:
        cp.wait()

    def own_mixed(i, gate):
        rows = own_row(i)
        q = pl.ds(m16(i * 16), 16)
        for cols, others in ((left, (mland.at[3], mzl.at[0], mzl.at[1], mzl.at[2])),
                             (right, (yland, zland.at[0, 1], zland.at[1, 1], zland.at[2, 1]))):
            total = st[rows, cols].astype(F32)
            for other in others:
                total = total + other[q, :].astype(F32)
            st[rows, cols] = (modr[gate : gate + 1, cols] * total).astype(BF)
            slope = g[pl.ds(m16(768 + i * 16), 16), cols].astype(F32)
            ms[0, gate : gate + 1, cols] += jnp.sum(slope * total, axis=0, keepdims=True)

    own_mixed(0, 5)
    each(1, 8, lambda i: own_mixed(i, 2))
    for cp in (
        pltpu.make_async_copy(st.at[trow(c)], upd_t.at[0], loc.at[14]),
        pltpu.make_async_copy(st.at[irow(c)], upd_i.at[0], loc.at[15]),
    ):
        cp.start()
        outs.append(cp)

    first = rcopy(ms.at[0], ml.at[0], mss.at[0], msr.at[0], yl)
    go(first)
    first.wait_recv()
    ms[1] = ms[0] + ml[0]
    more = [
        rcopy(ms.at[1], ml.at[1 + n], mss.at[1 + n], msr.at[1 + n], dev)
        for n, dev in enumerate((zp, zm, z2))
    ]
    for cp in more:
        go(cp)
    grad_last(1)
    for cp in more:
        cp.wait_recv()
    modsum = ms[1] + ml[1] + ml[2] + ml[3]
    ms_i[0] = modsum[0:3, :]
    ms_t[0] = modsum[3:6, :]

    grad_last(2)
    for cp in outs:
        cp.wait()
    for cp in sent:
        cp.wait_send()


def deliver(*refs):
    for n in range(6):
        refs[8 + n][...] = refs[n][...]
    for n in (6, 7):
        for row in range(3):
            for j in range(24):
                line = refs[n][0, row : row + 1, j * 128 : (j + 1) * 128]
                refs[8 + n][row * 24 + j : row * 24 + j + 1, :] = line


def body(
    image_tokens,
    text_tokens,
    image_mod,
    text_mod,
    image_qkv_weight,
    text_qkv_weight,
    image_out_weight,
    text_out_weight,
    image_slope,
    text_slope,
):
    hbm = pl.BlockSpec(memory_space=pl.ANY)
    vmem = pl.BlockSpec(memory_space=pltpu.VMEM)
    dma = pltpu.SemaphoreType.DMA
    shape = jax.ShapeDtypeStruct
    results = pl.pallas_call(
        kernel,
        out_shape=(
            shape((1, IB, D), BF),
            shape((1, TB, D), BF),
            shape((WR * 6, 128), F32),
            shape((WR * 6, 128), F32),
            shape((WR * 2, 128), F32),
            shape((WR * 2, 128), F32),
            shape((1, 3, D), F32),
            shape((1, 3, D), F32),
        ),
        in_specs=[hbm] * 8 + [vmem] * 2,
        out_specs=(hbm,) * 6 + (vmem,) * 2,
        scratch_shapes=[
            pltpu.VMEM((SEQ, D), BF),
            pltpu.VMEM((SEQ, D), BF),
            pltpu.VMEM((D, WC), BF),
            pltpu.VMEM((SEQ, D), BF),
            pltpu.VMEM((4, SEQ, 128), F32),
            pltpu.VMEM((SEQ, 256), BF),
            pltpu.VMEM((SEQ, 256), BF),
            pltpu.VMEM((SEQ, 256), BF),
            pltpu.VMEM((SEQ, 256), BF),
            pltpu.VMEM((256, 256), BF),
            pltpu.VMEM((SEQ, 768), BF),
            pltpu.VMEM((2, SEQ, 128), F32),
            pltpu.VMEM((2, SEQ, 128), F32),
            pltpu.VMEM((8, D), F32),
            pltpu.VMEM((4, 128, MC), BF),
            pltpu.VMEM((3, 128, MC), BF),
            pltpu.VMEM((3, 2, 128, D - MC), BF),
            pltpu.VMEM((128, D - MC), BF),
            pltpu.VMEM((8, WR, WC), BF),
            pltpu.VMEM((8, 384, 512), BF),
            pltpu.VMEM((2, HALF, WC), BF),
            pltpu.VMEM((2, HALF, WC), BF),
            pltpu.VMEM((2, 2, WR, WC), BF),
            pltpu.VMEM((WR, WC), BF),
            pltpu.VMEM((2, 8, D), F32),
            pltpu.VMEM((4, 8, D), F32),
            dma((19,)),
            dma((19,)),
            dma((19,)),
            dma((19,)),
            dma((17,)),
            dma((17,)),
            dma((10,)),
            dma((10,)),
            dma((18,)),
            dma((18,)),
            dma((24,)),
            dma((24,)),
            dma((27,)),
            dma((27,)),
            dma((4,)),
            dma((4,)),
            dma((22,)),
        ],
        compiler_params=pltpu.CompilerParams(
            collective_id=0, has_side_effects=True, vmem_limit_bytes=63 * 2**20
        ),
    )(
        image_tokens,
        text_tokens,
        image_slope,
        text_slope,
        image_qkv_weight.reshape(WR * 6, 128),
        text_qkv_weight.reshape(WR * 6, 128),
        image_out_weight.reshape(WR * 2, 128),
        text_out_weight.reshape(WR * 2, 128),
        image_mod,
        text_mod,
    )
    upd_i, upd_t, gq_i, gq_t, go_i, go_t, ms_i, ms_t = pl.pallas_call(
        deliver,
        out_shape=tuple(shape(v.shape, v.dtype) for v in results[:6]) + (shape((72, 128), F32),) * 2,
        in_specs=[vmem] * 8,
        out_specs=(vmem,) * 8,
        compiler_params=pltpu.CompilerParams(vmem_limit_bytes=60 * 2**20),
    )(*results)
    return (
        upd_i,
        upd_t,
        gq_i.reshape(WR, 3, 2, 128),
        gq_t.reshape(WR, 3, 2, 128),
        go_i.reshape(WR, 2, 128),
        go_t.reshape(WR, 2, 128),
        ms_i.reshape(1, 3, D),
        ms_t.reshape(1, 3, D),
    )


def solution(mesh):
    tokens = P("dp", "context", None)
    mods = P("dp", None, None)
    qkv = P("dp", None, "context", None)
    return jax.shard_map(
        body,
        mesh=mesh,
        in_specs=(tokens, tokens, mods, mods, qkv, qkv, tokens, tokens, tokens, tokens),
        out_specs=(tokens, tokens, qkv, qkv, tokens, tokens, mods, mods),
        check_vma=False,
    )
```

```python
import jax
import jax.numpy as jnp
from jax import lax
from jax.experimental import pallas as pl
from jax.experimental.pallas import tpu as pltpu
from jax.sharding import PartitionSpec as P

EPS = 1e-06
BF = jnp.bfloat16
F32 = jnp.float32
D = 3072
TXT = 128
SEQ = 1024
TB = 16
IB = 112
WR = 192
HALF = 96
MC = 1792
SCALE = 128 ** (-0.5)
QI, QT, OI, OT, WC = 0, 768, 1536, 1792, 2048
GROUPS = ((OI, 512), (QI, 768), (QT, 768))


def dot(a, b):
    return jnp.dot(a, b, preferred_element_type=F32)


def dot_last(a, b):
    return lax.dot_general(a, b, (((1,), (1,)), ((), ())), preferred_element_type=F32)


def dot_rows(a, b):
    return lax.dot_general(a, b, (((0,), (0,)), ((), ())), preferred_element_type=F32)


def each(low, high, step):
    lax.fori_loop(low, high, lambda i, _: (step(i), 0)[1], 0)


each_io = each


def m16(v):
    return pl.multiple_of(v, 16)


def kernel(
    tok_i,
    tok_t,
    slo_i,
    slo_t,
    wq_i,
    wq_t,
    wo_i,
    wo_t,
    mod_i,
    mod_t,
    upd_i,
    upd_t,
    gq_i,
    gq_t,
    go_i,
    go_t,
    ms_i,
    ms_t,
    xn,
    g,
    w,
    st,
    pq,
    qb,
    kb,
    vb,
    att,
    batt,
    bq,
    dk,
    dv,
    modr,
    mland,
    mzl,
    zland,
    yland,
    sland,
    so,
    ha,
    hb,
    xl,
    yhl,
    ms,
    ml,
    xs,
    xr,
    gs,
    gr,
    ws,
    wr,
    mys,
    myr,
    mzs,
    mzr,
    ss,
    sr,
    rs,
    rr,
    mss,
    msr,
    loc,
):
    d = lax.axis_index("dp")
    c = lax.axis_index("context")
    core = lax.rem(d, 2)
    yh = lax.rem(d // 2, 2)
    xpos = d // 4
    c_zp, c_zm, c_z2 = lax.rem(c + 2, 8), lax.rem(c + 6, 8), lax.rem(c + 4, 8)
    ylflip = 1 - 2 * lax.rem(c, 2)
    d_xp, d_xm, d_x2 = lax.rem(d + 4, 16), lax.rem(d + 12, 16), lax.rem(d + 8, 16)
    yhflip = 2 - 4 * yh
    zp, zm, z2, yl = (d, c_zp), (d, c_zm), (d, c_z2), (d, c + ylflip)
    xp, xm, yhp, sib = (d_xp, c), (d_xm, c), (d + yhflip, c), (d + 1 - 2 * core, c)

    def rcopy(src, dst, ssem, rsem, dev):
        return pltpu.make_async_remote_copy(
            src_ref=src,
            dst_ref=dst,
            send_sem=ssem,
            recv_sem=rsem,
            device_id=dev,
            device_id_type=pl.DeviceIdType.MESH,
        )

    def trow(cc):
        return pl.ds(m16(cc * TB), TB)

    def irow(cc, off=0, n=IB):
        return pl.ds(m16(TXT + cc * IB + off), n)

    sent = []
    sent_g = []
    outs = []

    def go(cp, kept=sent):
        cp.start()
        kept.append(cp)

    pieces = tuple((r, p, q, 6) for r, q in ((wq_i, QI), (wq_t, QT)) for p in range(3))
    pieces += ((wo_i, 0, OI, 2), (wo_t, 0, OT, 2))
    locs = [
        pltpu.make_async_copy(src, dst, loc.at[n])
        for n, (src, dst) in enumerate(
            (
                (tok_t.at[0], xn.at[trow(c)]),
                (tok_i.at[0], xn.at[irow(c)]),
                (slo_t.at[0], g.at[trow(c)]),
                (slo_i.at[0], g.at[irow(c)]),
            )
            + tuple(
                (ref.at[pl.ds(384 * p, 384)], so.at[k, :, 0:128])
                for k, (ref, p, _, _) in enumerate(pieces)
            )
        )
    ]
    for cp in locs:
        cp.start()
    bar = pltpu.get_barrier_semaphore()
    peers = (zp, zm, z2, yl, xp, xm, yhp, sib)
    for dev in peers:
        pl.semaphore_signal(bar, inc=1, device_id=dev, device_id_type=pl.DeviceIdType.MESH)
    modr[...] = jnp.zeros_like(modr)
    modr[0:3, :] = mod_i[0].astype(F32)
    modr[3:6, :] = mod_t[0].astype(F32)
    modr[1:2, :] = modr[1:2, :] + 1.0
    modr[4:5, :] = modr[4:5, :] + 1.0
    for cp in locs:
        cp.wait()

    for k, (_, p, col, heads) in enumerate(pieces):
        r0, n = k // 4 * 384, 384 // heads
        pq[k % 4, r0 : r0 + 384, :] = so[k, :, 0:128].astype(F32)
        rows = pl.ds(m16(d * WR + p * n), n)
        for j in range(heads):
            part = pq[k % 4, pl.ds(r0 + j, n, stride=heads), :]
            w[rows, col + j * 128 : col + (j + 1) * 128] = part.astype(BF)

    def own_row(i):
        return pl.ds(m16(jnp.where(i == 0, c * TB, TXT + c * IB + (i - 1) * 16)), 16)

    def norm_rows(i):
        rows = own_row(i)
        v = xn[rows, :].astype(F32)
        v = v - jnp.mean(v, axis=-1, keepdims=True)
        v = v * lax.rsqrt(jnp.mean(v * v, axis=-1, keepdims=True) + EPS)
        xn[rows, :] = v.astype(BF)

    each(0, 8, norm_rows)
    pl.semaphore_wait(bar, len(peers))

    def full(cc):
        return (trow(cc), irow(cc))

    def half_a(cc):
        return (irow(cc, 0, 64),)

    def half_b(cc):
        return (irow(cc, 64, 48), trow(cc))

    def main(cc):
        return (trow(cc), irow(cc, 0, 80))

    def main_a(cc):
        return (irow(cc, 0, 48),)

    def main_b(cc):
        return (irow(cc, 48, 32), trow(cc))

    def edge(cc):
        return (irow(cc, 80, 32),)

    yc = c + ylflip
    y_zp, y_zm, y_z2 = c_zp + ylflip, c_zm + ylflip, c_z2 + ylflip
    plan = (
        (0, yl, full(c), full(yc)),
        (2, zp, full(c), full(c_zm)),
        (4, zm, full(c), full(c_zp)),
        (6, zp, main(yc), main(y_zm)),
        (8, zm, main(yc), main(y_zp)),
        (10, zp, half_a(c_zm), half_a(c_z2)),
        (11, zm, half_b(c_zp), half_b(c_z2)),
        (13, zp, main_a(y_zm), main_a(y_z2)),
        (14, zm, main_b(y_zp), main_b(y_z2)),
        (16, yl, edge(c_zm), edge(y_zm)),
        (17, yl, edge(c_zp), edge(y_zp)),
        (18, yl, edge(c_z2), edge(y_z2)),
    )

    def ctx_send(buf, s, r, n):
        first, dev, rows, _ = plan[n]
        for i, rw in enumerate(rows):
            cp = rcopy(buf.at[rw], buf.at[rw], s.at[first + i], r.at[first + i], dev)
            go(cp, sent_g if buf is g else sent)

    def ctx_recv(buf, s, r, n):
        first, dev, _, rows = plan[n]
        for i, rw in enumerate(rows):
            rcopy(buf.at[rw], buf.at[rw], s.at[first + i], r.at[first + i], dev).wait_recv()

    def wrow(dd, off=0, n=WR):
        return pl.ds(m16(dd * WR + off), n)

    wplan = (
        (yhp, wrow(d), wrow(d + yhflip)),
        (xp, wrow(d), wrow(d_xm)),
        (xm, wrow(d), wrow(d_xp)),
        (xp, wrow(d + yhflip), wrow(d_xm + yhflip)),
        (xm, wrow(d + yhflip), wrow(d_xp + yhflip)),
        (xp, wrow(d_xm, 0, HALF), wrow(d_x2, 0, HALF)),
        (xm, wrow(d_xp, HALF, HALF), wrow(d_x2, HALF, HALF)),
        (xp, wrow(d_xm + yhflip, 0, HALF), wrow(d_x2 + yhflip, 0, HALF)),
        (xm, wrow(d_xp + yhflip, HALF, HALF), wrow(d_x2 + yhflip, HALF, HALF)),
    ) + tuple(
        (sib, wrow(b), wrow(b + 1 - 2 * core))
        for b in (
            d,
            d + yhflip,
            d_xm,
            d_xp,
            d_xm + yhflip,
            d_xp + yhflip,
            d_x2,
            d_x2 + yhflip,
        )
    )

    def w_send(*ns):
        for n in ns:
            dev, rows, _ = wplan[n]
            go(rcopy(w.at[rows], w.at[rows], ws.at[n], wr.at[n], dev))

    def w_recv(*ns):
        for n in ns:
            dev, _, rows = wplan[n]
            rcopy(w.at[rows], w.at[rows], ws.at[n], wr.at[n], dev).wait_recv()

    def x_send(*ns):
        for n in ns:
            ctx_send(xn, xs, xr, n)

    def x_recv(*ns):
        for n in ns:
            ctx_recv(xn, xs, xr, n)

    def g_send(*ns):
        for n in ns:
            ctx_send(g, gs, gr, n)

    def g_recv(*ns):
        for n in ns:
            ctx_recv(g, gs, gr, n)

    x_send(1, 2)
    w_send(0, 1, 2, 9)

    def gate_rows(i):
        rows = own_row(i)
        gate = jnp.where(i == 0, modr[5:6, :], modr[2:3, :])
        g[rows, :] = (gate * g[rows, :].astype(F32)).astype(BF)

    each(0, 8, gate_rows)

    def modulate(start, count, text):
        def step(i):
            rows = pl.ds(m16(start + i * 16), 16)
            base = 3 if text else 0
            v = xn[rows, :].astype(F32)
            st[rows, :] = (modr[base + 1 : base + 2, :] * v + modr[base : base + 1, :]).astype(BF)

        each(0, count // 16, step)

    def modulate_block(cc):
        modulate(cc * TB, TB, True)
        modulate(TXT + cc * IB, IB, False)

    modulate_block(c)
    x_recv(1)
    x_send(5)
    x_recv(2)
    x_send(6)
    w_recv(1)
    w_send(5, 11)
    w_recv(2)
    w_send(6, 12)
    w_recv(0)
    w_send(3, 4, 10)
    x_send(0, 9, 10)
    g_send(1, 2)
    modulate_block(c_zm)
    modulate_block(c_zp)
    x_recv(5, 6)
    x_send(11)
    w_recv(5, 6)
    w_send(15)
    x_recv(0)
    x_send(3, 4)
    g_send(0)
    modulate_block(c_z2)
    modulate_block(yc)
    w_recv(3)
    w_send(7, 13)
    w_recv(4)
    w_send(8, 14)
    g_recv(1)
    g_send(5, 9)
    g_recv(2)
    g_send(6, 10)
    x_recv(3)
    x_send(7)
    x_recv(4)
    x_send(8)
    x_recv(9, 10)
    modulate_block(y_zm)
    modulate_block(y_zp)
    w_recv(7, 8)
    w_send(16)
    g_recv(0)
    g_send(3, 4)
    x_recv(7, 8, 11)
    modulate_block(y_z2)
    g_recv(5, 6)
    g_send(11)
    w_recv(9, 10, 11, 12, 13, 14, 15, 16)

    def project(rows, col):
        left = st[rows, :]
        for j, out in enumerate((qb, kb, vb)):
            acc = dot(left, w[:, col + j * 256 : col + (j + 1) * 256])
            if j == 2:
                out[rows, :] = acc.astype(BF)
                continue
            for h in range(2):
                a = acc[:, h * 128 : (h + 1) * 128]
                pq[2 * j + h, rows, :] = a
                f = lax.rsqrt(jnp.mean(a * a, axis=-1, keepdims=True) + EPS)
                out[rows, h * 128 : (h + 1) * 128] = (a * f).astype(BF)

    def project_image(i):
        project(pl.ds(m16(TXT + i * 448), 448), QI)

    each(0, 2, project_image)
    project(pl.ds(0, TXT), QT)

    for h in range(2):
        cols = slice(h * 128, (h + 1) * 128)

        def forward(i, cols=cols):
            rows = pl.ds(m16(i * 256), 256)
            e = jnp.exp(dot_last(qb[rows, cols], kb[:, cols]) * SCALE)
            p = e / jnp.sum(e, axis=-1, keepdims=True)
            att[rows, cols] = dot(p.astype(BF), vb[:, cols]).astype(BF)

        each(0, 4, forward)

    def mix(i):
        n = pl.ds(pl.multiple_of(i * 512, 512), 512)
        st[0:TXT, n] = dot_last(att[0:TXT, :], w[n, OT : OT + 256]).astype(BF)
        st[TXT:576, n] = dot_last(att[TXT:576, :], w[n, OI : OI + 256]).astype(BF)
        st[576:SEQ, n] = dot_last(att[576:SEQ, :], w[n, OI : OI + 256]).astype(BF)

    each(0, 6, mix)

    zs = (c_z2, c_zp, c_zm, c)
    zdevs = (z2, zp, zm)
    left, right = slice(0, MC), slice(MC, D)

    def mix_copies(block, cols, land, ssem, rsem, first, dev):
        return [
            rcopy(st.at[rw, cols], land.at[pl.ds(off, size)], ssem.at[first + i], rsem.at[first + i], dev)
            for i, (rw, off, size) in enumerate(((trow(block), 0, TB), (irow(block), TB, IB)))
        ]

    def left_y(n):
        return mix_copies(zs[n] + ylflip, left, mland.at[n], mys, myr, 2 * n, yl)

    def left_z(n):
        return mix_copies(zs[n], left, mzl.at[n], mzs, mzr, 2 * n, zdevs[n])

    def right_z(n, v):
        block = zs[n] if v else zs[n] + ylflip
        return mix_copies(block, right, zland.at[n, v], mzs, mzr, 6 + 4 * n + 2 * v, zdevs[n])

    def right_y():
        return mix_copies(yc, right, yland, mys, myr, 8, yl)

    def start_all(cps):
        for cp in cps:
            go(cp)

    def recv_all(cps):
        for cp in cps:
            cp.wait_recv()

    def block_row(cc, i):
        return pl.ds(m16(jnp.where(i == 0, cc * TB, TXT + cc * IB + (i - 1) * 16)), 16)

    for n in range(4):
        start_all(left_y(n))

    def mixed_left(n):
        recv_all(left_y(n))

        def step(i):
            rows = block_row(zs[n], i)
            land = mland[n, pl.ds(m16(i * 16), 16), :].astype(F32)
            st[rows, left] = (st[rows, left].astype(F32) + land).astype(BF)

        each(0, 8, step)
        start_all(left_z(n))

    def mixed_right():
        for n in range(3):
            recv_all(right_z(n, 0))

        def step(i):
            rows = block_row(yc, i)
            total = st[rows, right].astype(F32)
            for n in range(3):
                total = total + zland[n, 0, pl.ds(m16(i * 16), 16), :].astype(F32)
            st[rows, right] = total.astype(BF)

        each(0, 8, step)
        start_all(right_y())

    def chip(k):
        j = k // 2
        dx = jnp.where(j == 0, 2, jnp.where(j == 1, 1, jnp.where(j == 2, 3, 0)))
        yy = jnp.where(lax.rem(k, 2) == 0, 1 - yh, yh)
        return lax.rem(xpos + dx, 4) * 2 + yy

    def out_tile(k):
        cols = pl.ds(pl.multiple_of(chip(k) * 384, 128), 384)
        so[k, :, 0:256] = dot_rows(g[TXT:SEQ, cols], att[TXT:SEQ, :]).astype(BF)
        so[k, :, 256:512] = dot_rows(g[0:TXT, cols], att[0:TXT, :]).astype(BF)

    def stage_cols(k):
        return pl.ds(pl.multiple_of(lax.rem(k, 4) * 768, 256), 768)

    def qkv_tile(k, text):
        p = chip(k)
        cols = pl.ds(pl.multiple_of(p * 384, 128), 384)
        rows = slice(0, TXT) if text else slice(TXT, SEQ)
        base = 3 if text else 0
        wcol = QT if text else QI
        back = bq[rows, :]
        grad = dot_rows(xn[rows, cols], back)
        total = jnp.sum(back.astype(F32), axis=0, keepdims=True)
        own = w[pl.ds(m16(p * 384), 384), wcol : wcol + 768].astype(F32)
        shift_part = jnp.sum(own * total, axis=-1, keepdims=True)
        scale_part = jnp.sum(own * grad, axis=-1, keepdims=True)
        lane = lax.broadcasted_iota(jnp.int32, (384, 128), 1)
        vals = jnp.where(lane == base, shift_part, jnp.where(lane == base + 1, scale_part, 0.0))
        mrow = pl.ds(m16(lax.rem(p, 2) * 384), 384)
        mcol = p // 2
        if text:
            vals = vals + pq[mcol, mrow, :]
        pq[mcol, mrow, :] = vals
        mod = jnp.transpose(modr[:, cols])
        full_grad = mod[:, base + 1 : base + 2] * grad + mod[:, base : base + 1] * total
        g[pl.ds(m16(k // 4 * 384), 384), stage_cols(k)] = full_grad.astype(BF)

    def stage(gi, k, half):
        rows = half * WR
        if gi == 0:
            return so.at[k, pl.ds(m16(rows), WR)]
        return g.at[pl.ds(m16(k // 4 * 384 + rows), WR), stage_cols(k)]

    def to_sib(gi, k):
        c0, n = GROUPS[gi]
        return rcopy(
            stage(gi, k, 1 - core),
            sland.at[k, :, c0 : c0 + n],
            ss.at[gi * 8 + k],
            sr.at[gi * 8 + k],
            sib,
        )

    def grad_range(gi, k0, k1):
        c0, n = GROUPS[gi]

        def compute(k):
            if gi == 0:
                out_tile(k)
            else:
                qkv_tile(k, gi == 2)
            to_sib(gi, k).start()

        each_io(k0, k1, compute)

        def combine(k):
            to_sib(gi, k).wait()

            def step(i):
                r = pl.ds(m16(i * 32), 32)
                if gi == 0:
                    mine = so[k, pl.ds(m16(core * WR + i * 32), 32), :]
                else:
                    mine = g[pl.ds(m16(k // 4 * 384 + core * WR + i * 32), 32), stage_cols(k)]
                land = sland[k, r, c0 : c0 + n].astype(F32)
                sland[k, r, c0 : c0 + n] = (mine.astype(F32) + land).astype(BF)

            each(0, 6, step)

        each_io(k0, k1, combine)

    def gcopy(gi, n, src, dst, dev):
        return rcopy(src, dst, rs.at[gi * 9 + n], rr.at[gi * 9 + n], dev)

    def far_copy(gi, v, side):
        c0, n = GROUPS[gi]
        cs = slice(c0, c0 + n)
        src = sland.at[v, pl.ds(side * HALF, HALF), cs]
        dst = (ha, hb)[side].at[v, :, cs]
        return gcopy(gi, 2 * v + side, src, dst, (xp, xm)[side])

    def near_copy(gi, v, side):
        c0, n = GROUPS[gi]
        cs = slice(c0, c0 + n)
        src = sland.at[2 + 2 * side + v, :, cs]
        return gcopy(gi, 4 + 2 * v + side, src, xl.at[side, v, :, cs], (xp, xm)[side])

    def yh_copy(gi):
        c0, n = GROUPS[gi]
        cs = slice(c0, c0 + n)
        return gcopy(gi, 8, sland.at[6, :, cs], yhl.at[:, cs], yhp)

    def grad_far(gi):
        for v in range(2):
            for side in range(2):
                go(far_copy(gi, v, side))

    def grad_near(gi):
        c0, n = GROUPS[gi]
        cs = slice(c0, c0 + n)
        for v in range(2):
            for side, land in ((0, ha), (1, hb)):
                far_copy(gi, v, side).wait_recv()
                k = 2 + 2 * side + v

                def step(i, land=land, k=k, side=side, v=v):
                    r = pl.ds(m16(side * HALF + i * 32), 32)
                    q = pl.ds(m16(i * 32), 32)
                    sland[k, r, cs] = (
                        sland[k, r, cs].astype(F32) + land[v, q, cs].astype(F32)
                    ).astype(BF)

                each(0, 3, step)
                go(near_copy(gi, v, side))

    def grad_yh(gi):
        c0, n = GROUPS[gi]
        cs = slice(c0, c0 + n)
        near_copy(gi, 0, 0).wait_recv()
        near_copy(gi, 0, 1).wait_recv()

        def step(i):
            r = pl.ds(m16(i * 32), 32)
            total = sland[6, r, cs].astype(F32) + xl[0, 0, r, cs].astype(F32)
            sland[6, r, cs] = (total + xl[1, 0, r, cs].astype(F32)).astype(BF)

        each(0, 6, step)
        go(yh_copy(gi))

    def grad_last(gi):
        c0, n = GROUPS[gi]
        near_copy(gi, 1, 0).wait_recv()
        near_copy(gi, 1, 1).wait_recv()
        yh_copy(gi).wait_recv()
        heads = 6 if gi else 2
        for b in range(n // 128):
            cs = slice(c0 + b * 128, c0 + (b + 1) * 128)
            for i in range(6):
                r = slice(i * 32, (i + 1) * 32)
                total = sland[7, r, cs].astype(F32) + xl[0, 1, r, cs].astype(F32)
                total = total + xl[1, 1, r, cs].astype(F32) + yhl[r, cs].astype(F32)
                if gi == 0:
                    dk[b // 2, pl.ds(i * 64 + b % 2, 32, stride=heads), :] = total
                else:
                    part = (gi - 1) * 2 + i // 3
                    pq[part, pl.ds(i % 3 * 192 + b, 32, stride=heads), :] = total
        if gi == 0:
            moves = [(dk.at[0, 0:384], go_i), (dk.at[1, 0:384], go_t)]
        else:
            ref = (gq_i, gq_t)[gi - 1]
            part = (gi - 1) * 2
            moves = [
                (pq.at[part, 0:576], ref.at[0:576]),
                (pq.at[part + 1, 0:576], ref.at[576:1152]),
            ]
        for i, (src, dst) in enumerate(moves):
            cp = pltpu.make_async_copy(src, dst, loc.at[16 + 2 * gi + i])
            cp.start()
            outs.append(cp)

    def rms_back(a, slope):
        f = lax.rsqrt(jnp.mean(a * a, axis=-1, keepdims=True) + EPS)
        normal = a * f
        return f * (slope - normal * jnp.mean(slope * normal, axis=-1, keepdims=True))

    def backward(ca, cb, fresh):
        parts = ((trow(ca), 0, TB), (trow(cb), 16, TB), (irow(ca), 32, IB), (irow(cb), 144, IB))

        def pick(ref, cols):
            return jnp.concatenate([ref[rw, cols] for rw, _, _ in parts], axis=0)

        every = slice(0, D)
        texts = jnp.concatenate([g[trow(ca), every], g[trow(cb), every]], axis=0)
        batt[0:32, :] = dot(texts, w[:, OT : OT + 256]).astype(BF)
        images = jnp.concatenate([g[irow(ca), every], g[irow(cb), every]], axis=0)
        batt[32:256, :] = dot(images, w[:, OI : OI + 256]).astype(BF)
        for h in range(2):
            cols = slice(h * 128, (h + 1) * 128)
            qt = pick(qb, cols)
            bt = batt[:, cols]
            e = jnp.exp(dot_last(kb[:, cols], qt) * SCALE)
            p = e / jnp.sum(e, axis=0, keepdims=True)
            dp = dot_last(vb[:, cols], bt)
            ds = p * (dp - jnp.sum(p * dp, axis=0, keepdims=True)) * SCALE
            ds = ds.astype(BF)
            if fresh:
                dv[h] = dot(p.astype(BF), bt)
                dk[h] = dot(ds, qt)
            else:
                dv[h] += dot(p.astype(BF), bt)
                dk[h] += dot(ds, qt)
            dq = rms_back(pick(pq.at[h], slice(0, 128)), dot_rows(ds, kb[:, cols])).astype(BF)
            for rw, off, size in parts:
                bq[rw, cols] = dq[off : off + size, :]

    def finish(i):
        rows = pl.ds(m16(i * 256), 256)
        for h in range(2):
            kcols = slice(256 + h * 128, 384 + h * 128)
            bq[rows, kcols] = rms_back(pq[2 + h, rows, :], dk[h, rows, :]).astype(BF)
            bq[rows, 512 + h * 128 : 640 + h * 128] = dv[h, rows, :].astype(BF)

    def run(step, *args):
        step(*args)

    g_recv(3)
    g_send(7)
    g_recv(4)
    g_send(8)
    run(backward, c, yc, True)
    run(backward, c_zm, c_zp, False)
    g_recv(9, 10)
    run(backward, y_zm, y_zp, False)
    g_recv(7, 8, 11)
    for n in range(3):
        start_all(right_z(n, 0))
    for n in range(3):
        start_all(right_z(n, 1))
    grad_range(0, 0, 2)
    grad_far(0)
    run(backward, c_z2, y_z2, False)
    each(0, 4, finish)
    grad_range(0, 2, 8)
    grad_near(0)
    mixed_left(0)

    for cp in sent_g:
        cp.wait_send()
    slopes = [
        pltpu.make_async_copy(slo_t.at[0], g.at[pl.ds(768, TB)], loc.at[12]),
        pltpu.make_async_copy(slo_i.at[0], g.at[pl.ds(784, IB)], loc.at[13]),
    ]
    for cp in slopes:
        cp.start()

    for gi in (1, 2):
        grad_range(gi, 0, 2)
        grad_far(gi)
        grad_range(gi, 2, 8)
        mixed_left(gi)
    grad_near(1)
    grad_near(2)
    grad_yh(0)

    def turn(p):
        mrow = pl.ds(m16(lax.rem(p, 2) * 384), 384)
        mcol = p // 2
        flat = jnp.transpose(pq[mcol, mrow, :])
        ms[0, :, pl.ds(pl.multiple_of(p * 384, 128), 384)] = flat[0:8, :]

    each(0, 8, turn)
    mixed_right()
    grad_last(0)
    grad_yh(1)
    grad_yh(2)

    recv_all(left_y(3))
    for n in range(3):
        recv_all(left_z(n))
        recv_all(right_z(n, 1))
    recv_all(right_y())
    for cp in slopes:
        cp.wait()

    def own_mixed(i, gate):
        rows = own_row(i)
        q = pl.ds(m16(i * 16), 16)
        for cols, others in ((left, (mland.at[3], mzl.at[0], mzl.at[1], mzl.at[2])),
                             (right, (yland, zland.at[0, 1], zland.at[1, 1], zland.at[2, 1]))):
            total = st[rows, cols].astype(F32)
            for other in others:
                total = total + other[q, :].astype(F32)
            st[rows, cols] = (modr[gate : gate + 1, cols] * total).astype(BF)
            slope = g[pl.ds(m16(768 + i * 16), 16), cols].astype(F32)
            ms[0, gate : gate + 1, cols] += jnp.sum(slope * total, axis=0, keepdims=True)

    own_mixed(0, 5)
    each(1, 8, lambda i: own_mixed(i, 2))
    for cp in (
        pltpu.make_async_copy(st.at[trow(c)], upd_t.at[0], loc.at[14]),
        pltpu.make_async_copy(st.at[irow(c)], upd_i.at[0], loc.at[15]),
    ):
        cp.start()
        outs.append(cp)

    first = rcopy(ms.at[0], ml.at[0], mss.at[0], msr.at[0], yl)
    go(first)
    first.wait_recv()
    ms[1] = ms[0] + ml[0]
    more = [
        rcopy(ms.at[1], ml.at[1 + n], mss.at[1 + n], msr.at[1 + n], dev)
        for n, dev in enumerate((zp, zm, z2))
    ]
    for cp in more:
        go(cp)
    grad_last(1)
    for cp in more:
        cp.wait_recv()
    modsum = ms[1] + ml[1] + ml[2] + ml[3]
    ms_i[0] = modsum[0:3, :]
    ms_t[0] = modsum[3:6, :]

    grad_last(2)
    for cp in outs:
        cp.wait()
    for cp in sent:
        cp.wait_send()


def deliver(*refs):
    for n in range(6):
        refs[8 + n][...] = refs[n][...]
    for n in (6, 7):
        for row in range(3):
            for j in range(24):
                line = refs[n][0, row : row + 1, j * 128 : (j + 1) * 128]
                refs[8 + n][row * 24 + j : row * 24 + j + 1, :] = line


def body(
    image_tokens,
    text_tokens,
    image_mod,
    text_mod,
    image_qkv_weight,
    text_qkv_weight,
    image_out_weight,
    text_out_weight,
    image_slope,
    text_slope,
):
    hbm = pl.BlockSpec(memory_space=pl.ANY)
    vmem = pl.BlockSpec(memory_space=pltpu.VMEM)
    dma = pltpu.SemaphoreType.DMA
    shape = jax.ShapeDtypeStruct
    results = pl.pallas_call(
        kernel,
        out_shape=(
            shape((1, IB, D), BF),
            shape((1, TB, D), BF),
            shape((WR * 6, 128), F32),
            shape((WR * 6, 128), F32),
            shape((WR * 2, 128), F32),
            shape((WR * 2, 128), F32),
            shape((1, 3, D), F32),
            shape((1, 3, D), F32),
        ),
        in_specs=[hbm] * 8 + [vmem] * 2,
        out_specs=(hbm,) * 6 + (vmem,) * 2,
        scratch_shapes=[
            pltpu.VMEM((SEQ, D), BF),
            pltpu.VMEM((SEQ, D), BF),
            pltpu.VMEM((D, WC), BF),
            pltpu.VMEM((SEQ, D), BF),
            pltpu.VMEM((4, SEQ, 128), F32),
            pltpu.VMEM((SEQ, 256), BF),
            pltpu.VMEM((SEQ, 256), BF),
            pltpu.VMEM((SEQ, 256), BF),
            pltpu.VMEM((SEQ, 256), BF),
            pltpu.VMEM((256, 256), BF),
            pltpu.VMEM((SEQ, 768), BF),
            pltpu.VMEM((2, SEQ, 128), F32),
            pltpu.VMEM((2, SEQ, 128), F32),
            pltpu.VMEM((8, D), F32),
            pltpu.VMEM((4, 128, MC), BF),
            pltpu.VMEM((3, 128, MC), BF),
            pltpu.VMEM((3, 2, 128, D - MC), BF),
            pltpu.VMEM((128, D - MC), BF),
            pltpu.VMEM((8, WR, WC), BF),
            pltpu.VMEM((8, 384, 512), BF),
            pltpu.VMEM((2, HALF, WC), BF),
            pltpu.VMEM((2, HALF, WC), BF),
            pltpu.VMEM((2, 2, WR, WC), BF),
            pltpu.VMEM((WR, WC), BF),
            pltpu.VMEM((2, 8, D), F32),
            pltpu.VMEM((4, 8, D), F32),
            dma((19,)),
            dma((19,)),
            dma((19,)),
            dma((19,)),
            dma((17,)),
            dma((17,)),
            dma((10,)),
            dma((10,)),
            dma((18,)),
            dma((18,)),
            dma((24,)),
            dma((24,)),
            dma((27,)),
            dma((27,)),
            dma((4,)),
            dma((4,)),
            dma((22,)),
        ],
        compiler_params=pltpu.CompilerParams(
            collective_id=0, has_side_effects=True, vmem_limit_bytes=63 * 2**20
        ),
    )(
        image_tokens,
        text_tokens,
        image_slope,
        text_slope,
        image_qkv_weight.reshape(WR * 6, 128),
        text_qkv_weight.reshape(WR * 6, 128),
        image_out_weight.reshape(WR * 2, 128),
        text_out_weight.reshape(WR * 2, 128),
        image_mod,
        text_mod,
    )
    upd_i, upd_t, gq_i, gq_t, go_i, go_t, ms_i, ms_t = pl.pallas_call(
        deliver,
        out_shape=tuple(shape(v.shape, v.dtype) for v in results[:6]) + (shape((72, 128), F32),) * 2,
        in_specs=[vmem] * 8,
        out_specs=(vmem,) * 8,
        compiler_params=pltpu.CompilerParams(vmem_limit_bytes=60 * 2**20),
    )(*results)
    return (
        upd_i,
        upd_t,
        gq_i.reshape(WR, 3, 2, 128),
        gq_t.reshape(WR, 3, 2, 128),
        go_i.reshape(WR, 2, 128),
        go_t.reshape(WR, 2, 128),
        ms_i.reshape(1, 3, D),
        ms_t.reshape(1, 3, D),
    )


def solution(mesh):
    tokens = P("dp", "context", None)
    mods = P("dp", None, None)
    qkv = P("dp", None, "context", None)
    return jax.shard_map(
        body,
        mesh=mesh,
        in_specs=(tokens, tokens, mods, mods, qkv, qkv, tokens, tokens, tokens, tokens),
        out_specs=(tokens, tokens, qkv, qkv, tokens, tokens, mods, mods),
        check_vma=False,
    )
```
